256 devices in a mesh: dom: 32 (over y, x, z_lo), orient: 8 (over z_hi, core).
Axes of the slice: x: 4, y: 4, z: 8 (z_hi: 4, z_lo: 2; z = z_hi * 2 + z_lo), core: 2. Of those that a mesh axis runs over, the one named last changes fastest.
Arguments:
- particles: bfloat16 [8192, 16384], P('dom'), may hold values from -200 to 200
- refs: bfloat16 [64, 8, 16384], P('dom', 'orient'), may hold values from -6 to 6
- inv_sigma2: float32 [8192], replicated, may hold values from 0.0005 to 0.005
- offsets: int32 [9, 2], replicated, may hold values from -3 to 3, as said below
- owner_map: int32 [64], replicated, may hold values from 0 to 63, each once
- center: int32 [8192], P('dom'), may hold values from 0 to 7
Outputs:
- class_slices: float32 [64, 8, 16384], P('dom', 'orient')
- loglik: float32 [8192], P('dom')
The draws below stay inside these ranges and needn't reach their ends.
Inputs may be any that keep to these rules, and one draw needn't show every extreme that they name: `offsets`: each of the 9 translations has x and y within the range; every value of the range occurs in each column.
All inputs are finite; a program needn't handle non-finite values.
Results may differ from the reference program's by a relative error of at most 0.013.
Values may be sent and summed in bfloat16 or wider, within the bound.
A program may use at most 128 MiB of HBM per device.

```python
import math
import jax
import jax.numpy as jnp

BOX = 128
FREQS = 8192
FEAT = 16384
CLASSES = 64
ORIENTS = 8
PARTICLES = 8192
SHIFTS = 9


def phase_angles(offsets):
    freq_index = jnp.arange(FREQS, dtype=jnp.int32)
    half_box = BOX // 2
    freq_x = freq_index % half_box
    freq_y = freq_index // half_box
    freq_y = jnp.where(freq_y < half_box, freq_y, freq_y - BOX)
    angle_table = 2.0 * math.pi / BOX * (offsets[:, 0:1].astype(jnp.float32) * freq_x[None, :].astype(jnp.float32) + offsets[:, 1:2].astype(jnp.float32) * freq_y[None, :].astype(jnp.float32))
    return (jnp.cos(angle_table), jnp.sin(angle_table))


def slot_table(key):
    values = jax.random.normal(jax.random.fold_in(key, 101), (CLASSES, ORIENTS, FEAT), jnp.float32)
    return jnp.clip(values, -6.0, 6.0)


def offset_table(key):
    base = jax.random.fold_in(key, 202)
    key_a, key_b, key_c, key_d = jax.random.split(base, 4)
    across = jnp.concatenate([jax.random.permutation(key_a, 7).astype(jnp.int32) - 3, jax.random.randint(key_b, (SHIFTS - 7,), -3, 4).astype(jnp.int32)])
    along = jnp.concatenate([jax.random.permutation(key_c, 7).astype(jnp.int32) - 3, jax.random.randint(key_d, (SHIFTS - 7,), -3, 4).astype(jnp.int32)])
    return jnp.stack([across, along], axis=1).astype(jnp.int32)


def center_table(key):
    base = jax.random.fold_in(key, 303)
    key_a, key_b = jax.random.split(base, 2)
    leading = jax.random.permutation(key_a, ORIENTS).astype(jnp.int32)
    trailing = jax.random.randint(key_b, (PARTICLES - ORIENTS,), 0, ORIENTS).astype(jnp.int32)
    return jnp.concatenate([leading, trailing]).astype(jnp.int32)


def draw_refs(key, part):
    shared = slot_table(key)
    return shared.astype(jnp.bfloat16)


def draw_offsets(key, part):
    shared = offset_table(key)
    return shared


def draw_center(key, part):
    shared = center_table(key)
    return shared


def draw_particles(key, part):
    slots = slot_table(key)
    offsets = offset_table(key)
    center = center_table(key)
    key = jax.random.fold_in(key, 4)
    keys = jax.random.split(key, 6)
    true_slot = jax.random.randint(keys[0], (PARTICLES,), 0, CLASSES)
    true_shift = jax.random.randint(keys[3], (PARTICLES,), 0, SHIFTS)
    cosine_table, sine_table = phase_angles(offsets)
    cos_rows = cosine_table[true_shift]
    sin_rows = sine_table[true_shift]

    def placed(chosen):
        picked = slots[chosen, center]
        real_part = picked[:, :FREQS]
        imag_part = picked[:, FREQS:]
        return jnp.concatenate([real_part * cos_rows + imag_part * sin_rows, imag_part * cos_rows - real_part * sin_rows], axis=1)
    signal = placed(true_slot)
    strength = jax.random.uniform(keys[4], (PARTICLES,), jnp.float32, 0.02, 0.08)
    noise_field = jax.random.normal(keys[5], (PARTICLES, FEAT), jnp.float32)
    values = strength[:, None] * signal + noise_field
    return jnp.clip(values, -200.0, 200.0).astype(jnp.bfloat16)


def setup_inputs(seed: int = 0) -> dict:
    key_of = jax.random.split(jax.random.key(seed), 7)
    return {
        "particles": draw_particles(jax.random.fold_in(key_of[6], 71), 0),
        "refs": draw_refs(jax.random.fold_in(key_of[6], 71), 0),
        "inv_sigma2": jnp.clip(jnp.exp(jax.random.uniform(key_of[2], (FREQS,), jnp.float32, math.log(0.0005), math.log(0.005))), 0.0005, 0.005),
        "offsets": draw_offsets(jax.random.fold_in(key_of[6], 71), 0),
        "owner_map": jax.random.permutation(key_of[4], CLASSES).astype(jnp.int32),
        "center": draw_center(jax.random.fold_in(key_of[6], 71), 0),
    }


neg_fill = -1.0e30


def phase_tables(offsets):
    freq_index = jnp.arange(FREQS, dtype=jnp.int32)
    half_box = BOX // 2
    freq_x = freq_index % half_box
    freq_y = freq_index // half_box
    freq_y = jnp.where(freq_y < half_box, freq_y, freq_y - BOX)
    angle_table = (2.0 * math.pi / BOX) * (offsets[:, 0:1].astype(jnp.float32) * freq_x[None, :].astype(jnp.float32) + offsets[:, 1:2].astype(jnp.float32) * freq_y[None, :].astype(jnp.float32))
    return jnp.cos(angle_table), jnp.sin(angle_table)


def shift_slices(slices_f32, inv_sigma2, cosine_table, sine_table):
    real_part = slices_f32[:, :FREQS] * inv_sigma2[None, :]
    imag_part = slices_f32[:, FREQS:] * inv_sigma2[None, :]
    cos_rows = cosine_table[:, None, :]
    sin_rows = sine_table[:, None, :]
    shifted_real = real_part[None] * cos_rows + imag_part[None] * sin_rows
    shifted_imag = imag_part[None] * cos_rows - real_part[None] * sin_rows
    return jnp.concatenate([shifted_real, shifted_imag], axis=2).astype(jnp.bfloat16)


def slice_power(slices_f32, inv_sigma2):
    real_part = slices_f32[:, :FREQS]
    imag_part = slices_f32[:, FREQS:]
    return 0.5 * jnp.sum(inv_sigma2[None, :] * (real_part * real_part + imag_part * imag_part), axis=1)


def rotate_back(sums, cosine_table, sine_table):
    real_part = sums[:, :, :FREQS]
    imag_part = sums[:, :, FREQS:]
    cos_rows = cosine_table[:, None, :]
    sin_rows = sine_table[:, None, :]
    out_real = jnp.sum(real_part * cos_rows - imag_part * sin_rows, axis=0)
    out_imag = jnp.sum(imag_part * cos_rows + real_part * sin_rows, axis=0)
    return jnp.concatenate([out_real, out_imag], axis=1)


def allowed_mask(orient_ids, center, orients):
    distance = jnp.abs(orient_ids[:, None] - center[None, :])
    circular = jnp.minimum(distance, orients - distance)
    return circular <= orients // 4


def reference(particles, refs, inv_sigma2, offsets, owner_map, center):
    cosine_table, sine_table = phase_tables(offsets)
    slices_f32 = refs.reshape(CLASSES * ORIENTS, FEAT).astype(jnp.float32)
    shifted = shift_slices(slices_f32, inv_sigma2, cosine_table, sine_table)
    powers = slice_power(slices_f32, inv_sigma2)
    scores = jnp.dot(shifted.reshape(SHIFTS * CLASSES * ORIENTS, FEAT), particles.T, preferred_element_type=jnp.float32)
    log_like = scores.reshape(SHIFTS, CLASSES, ORIENTS, PARTICLES) - powers.reshape(1, CLASSES, ORIENTS, 1)
    allowed = allowed_mask(jnp.arange(ORIENTS, dtype=jnp.int32), center, ORIENTS)
    log_like = jnp.where(allowed[None, None], log_like, neg_fill)
    best_score = jnp.max(log_like, axis=(0, 1, 2))
    expo = jnp.exp(log_like - best_score)
    weight_total = jnp.sum(expo, axis=(0, 1, 2))
    weights = (expo / weight_total).astype(jnp.bfloat16)
    loglik = best_score + jnp.log(weight_total)
    sums = jnp.dot(weights.reshape(SHIFTS * CLASSES * ORIENTS, PARTICLES), particles, preferred_element_type=jnp.float32)
    sums = sums.reshape(SHIFTS, CLASSES * ORIENTS, FEAT)
    slot_sums = rotate_back(sums, cosine_table, sine_table).reshape(CLASSES, ORIENTS, FEAT)
    return slot_sums[owner_map], loglik
```

```python
import functools
import math

import jax
import jax.numpy as jnp
from jax import lax
from jax.experimental import pallas as pl
from jax.experimental.pallas import tpu as pltpu
from jax.sharding import PartitionSpec as P

BOX = 128
CHUNKS = 4
GROUPS = 4
RING = 4
NEG_FILL = -1e30
MESH = pl.DeviceIdType.MESH
BF16, F32 = jnp.bfloat16, jnp.float32


def unit_circle(phase):
    folded = ((phase + 64) & 127) - 64
    quarter = (folded + 16) >> 5
    x = (folded - quarter * 32).astype(F32) * (2.0 * math.pi / BOX)
    x2 = x * x
    sine = x * (1.0 + x2 * (-1 / 6 + x2 * (1 / 120 + x2 * (-1 / 5040 + x2 * (1 / 362880)))))
    cosine = 1.0 + x2 * (-0.5 + x2 * (1 / 24 + x2 * (-1 / 720 + x2 * (1 / 40320))))
    odd = (quarter & 1) == 1
    cos_sign = jnp.where(((quarter + 1) & 2) == 2, -1.0, 1.0)
    sin_sign = jnp.where((quarter & 2) == 2, -1.0, 1.0)
    return jnp.where(odd, sine, cosine) * cos_sign, jnp.where(odd, cosine, sine) * sin_sign


def em_kernel(
    n_dom, n_ori, shifts,
    refs_ref, part_hbm, inv_hbm, off_ref, omap_hbm, center_hbm,
    out_ref, loglik_ref,
    part, stage, mine, gath, rows, perm, perm_t, cos_tab, sin_tab, lhs, acc, prods, power, inv_ref, omap_ref, center_ref,
    stat_out, stat_in, by_class, sends, far_in, near_in, send2, recv2,
    part_sem, small_sem, ag_send, ag_recv, st_send, st_recv, rs_send, far_sem, early_sem, late_sem, rs_recv,
):
    freqs = inv_ref.shape[1]
    slots = 2 * n_dom
    lanes = mine.shape[2]
    width = freqs // CHUNKS
    half = RING
    me = lax.axis_index("dom")
    my_ori = lax.axis_index("orient")
    my_y, my_x, my_z = me // 8, (me // 2) % 4, me % 2

    def axes(c):
        odd = c % 2
        return odd, my_y * (1 - odd) + my_x * odd, my_x * (1 - odd) + my_y * odd

    def device(odd, v, u, z):
        return {"dom": ((v * (1 - odd) + u * odd) * 4 + u * (1 - odd) + v * odd) * 2 + z}

    def step(a, by):
        return (a + by) % RING

    def tile_row(odd, h, k):
        return pl.multiple_of((32 * h + 8 * k) * (1 - odd) + (16 * k + 8 * h) * odd, 8)

    def send(src, dst, send_sem, recv_sem, to):
        pltpu.make_async_remote_copy(
            src_ref=src, dst_ref=dst, send_sem=send_sem, recv_sem=recv_sem, device_id=to, device_id_type=MESH
        ).start()

    def wait(ref, sem):
        pltpu.make_async_copy(ref, ref, sem).wait()

    smalls = [
        pltpu.make_async_copy(src, dst, small_sem.at[k])
        for k, (src, dst) in enumerate(((inv_hbm, inv_ref), (omap_hbm, omap_ref), (center_hbm, center_ref)))
    ]

    def part_copies(k):
        return [
            pltpu.make_async_copy(
                part_hbm.at[:, pl.ds(pl.multiple_of(base + k * lanes, lanes), lanes)],
                part.at[:, pl.ds(pl.multiple_of((2 * k + r) * lanes, lanes), lanes)],
                part_sem.at[k // GROUPS],
            )
            for r, base in enumerate((0, freqs))
        ]

    for copy in smalls:
        copy.start()

    barrier = pltpu.get_barrier_semaphore()

    def greet(to):
        pl.semaphore_signal(barrier, inc=1, device_id=to, device_id_type=MESH)

    peers = [device(0, my_y, my_x, 1 - my_z)]
    for by in (1, 2, 3):
        for z in (my_z, 1 - my_z):
            peers.append(device(0, my_y, step(my_x, by), z))
            peers.append(device(0, step(my_y, by), my_x, z))
    for to in peers:
        greet(to)

    def greet_ori(i, carry):
        greet({"orient": lax.rem(my_ori + i, n_ori)})
        return carry

    lax.fori_loop(1, n_ori, greet_ori, 0)

    def exchange(first, second):
        for odd in range(2):
            there = lax.broadcasted_iota(jnp.int32, (256, 256), 0)
            here = lax.broadcasted_iota(jnp.int32, (256, 256), 1)
            for ref, out, src in ((first, there, here), (second, here, there)):
                at, s, q = src >> 4, (src >> 3) & 1, src & 7
                if odd:
                    row = ((at >> 1) & 3) * 8 + (at >> 3) * 4 + (at & 1) * 2 + s
                else:
                    row = at * 2 + s
                ref[odd] = (out == q * 32 + row).astype(F32).astype(BF16)

    for c in range(CHUNKS):
        for r in range(2):
            for g in range(GROUPS):
                for j in range(lanes // 128):
                    at = r * freqs + c * width + g * lanes + j * 128
                    stage[j, pl.ds(c * 16 + r * GROUPS + g, 2, stride=8), :] = refs_ref[:, pl.ds(at, 128)].astype(F32)
        for j in range(lanes // 128):
            mine[c, :, pl.ds(j * 128, 128)] = stage[j, pl.ds(c * 16, 16), :].astype(BF16)

    pl.semaphore_wait(barrier, len(peers) + n_ori - 1)

    def gather0(c, carry):
        odd, v, u = axes(c)
        at = v * 8 + u * 2 + my_z
        send(mine.at[c], gath.at[c, at], ag_send.at[c], ag_recv.at[c, 0], device(odd, v, u, 1 - my_z))
        gath[c, at] = mine[c]
        return carry

    def gather1(c):
        odd, v, u = axes(c)
        wait(mine.at[c], ag_recv.at[c, 0])
        pair = gath.at[c, pl.ds(v * 8 + u * 2, 2)]
        send(pair, pair, ag_send.at[c], ag_recv.at[c, 1], device(odd, v, step(u, 1), my_z))
        send(pair, pair, ag_send.at[c], ag_recv.at[c, 2], device(odd, v, step(u, 3), my_z))

    def gather2(c):
        odd, v, u = axes(c)
        for k, by in ((0, 1), (1, 3)):
            came = v * 8 + step(u, 4 - by) * 2
            wait(gath.at[c, pl.ds(came, 2)], ag_recv.at[c, 1 + k])
            one = gath.at[c, came + k]
            send(one, one, ag_send.at[c], ag_recv.at[c, 3 + k], device(odd, v, step(u, by), my_z))

    def gather3(c):
        odd, v, u = axes(c)
        for k in range(2):
            wait(gath.at[c, v * 8 + step(u, 2) * 2 + k], ag_recv.at[c, 3 + k])
        block = gath.at[c, pl.ds(v * 8, 8)]
        send(block, block, ag_send.at[c], ag_recv.at[c, 5], device(odd, step(v, 1), u, my_z))
        send(block, block, ag_send.at[c], ag_recv.at[c, 6], device(odd, step(v, 3), u, my_z))

    def gather4(c):
        odd, v, u = axes(c)
        for k, by in ((0, 1), (1, 3)):
            came = step(v, 4 - by) * 8
            wait(gath.at[c, pl.ds(came, 8)], ag_recv.at[c, 5 + k])
            part_of = gath.at[c, pl.ds(came + k * half, half)]
            send(part_of, part_of, ag_send.at[c], ag_recv.at[c, 7 + k], device(odd, step(v, by), u, my_z))

    def gather5(c):
        odd, v, u = axes(c)
        for k in range(2):
            wait(gath.at[c, pl.ds(step(v, 2) * 8 + k * half, half)], ag_recv.at[c, 7 + k])

    def pair(k, stage):
        def one(i, carry):
            stage(2 * k + i)
            return carry

        lax.fori_loop(0, 2, one, 0)

    lax.fori_loop(0, CHUNKS, gather0, 0)

    def fetch(k, carry):
        for copy in part_copies(k):
            copy.start()
        return carry

    lax.fori_loop(0, CHUNKS * GROUPS, fetch, 0)
    pair(0, gather1)
    exchange(perm, perm_t)

    shift_ids = lax.broadcasted_iota(jnp.int32, (shifts, 128), 0)
    off_x = jnp.zeros((shifts, 128), jnp.int32)
    off_y = jnp.zeros((shifts, 128), jnp.int32)
    for t in range(shifts):
        off_x = jnp.where(shift_ids == t, off_ref[0, t], off_x)
        off_y = jnp.where(shift_ids == t, off_ref[1, t], off_y)

    def tables(j, carry):
        for h in range(4):
            at = pl.multiple_of(j * 512 + h * 128, 128)
            freq = lax.broadcasted_iota(jnp.int32, (shifts, 128), 1) + at
            fx = freq & (BOX // 2 - 1)
            fy = freq >> 6
            fy = jnp.where(fy < BOX // 2, fy, fy - BOX)
            cosine, sine = unit_circle(off_x * fx + off_y * fy)
            cos_tab[:, pl.ds(at, 128)] = cosine
            sin_tab[:, pl.ds(at, 128)] = sine
        return carry

    lax.fori_loop(0, freqs // 1024, tables, 0)
    pair(0, gather2)
    pair(1, gather1)
    lax.fori_loop(freqs // 1024, freqs // 512, tables, 0)
    pair(0, gather3)
    pair(1, gather2)
    for copy in smalls:
        copy.wait()
    acc[...] = jnp.zeros_like(acc)
    power[...] = jnp.zeros_like(power)
    pair(0, gather4)
    pair(1, gather3)

    def score_chunk(c, carry):
        odd, v, u = axes(c)
        wait(part.at[:, pl.ds(0, 2 * width)], part_sem.at[c])
        gather5(c)

        for h in range(2):
            spread = jnp.dot(
                perm[odd], gath[c, pl.ds(16 * h, 16)].reshape(256, lanes), preferred_element_type=F32
            )
            for q in range(8):
                for k in range(4):
                    rows[q, pl.ds(tile_row(odd, h, k), 8), :] = spread[q * 32 + k * 8:q * 32 + k * 8 + 8, :]

        for g in range(GROUPS):
            base = pl.multiple_of(c * width + g * lanes, lanes)
            for j in range(lanes // 128):
                at = pl.ds(j * 128, 128)
                there = pl.ds(pl.multiple_of(base + j * 128, 128), 128)
                real = rows[g, :, at]
                imag = rows[GROUPS + g, :, at]
                inv = inv_ref[:, there]
                re = real * inv
                im = imag * inv
                power[...] += re * real + im * imag
                for t in range(shifts):
                    cosine = cos_tab[pl.ds(t, 1), there]
                    sine = sin_tab[pl.ds(t, 1), there]
                    into = lhs.at[g % 2, pl.ds(t * slots, slots)]
                    into[:, at] = (re * cosine + im * sine).astype(BF16)
                    into[:, pl.ds(lanes + j * 128, 128)] = (im * cosine - re * sine).astype(BF16)
            acc[...] += lax.dot_general(
                lhs[g % 2], part[:, pl.ds(pl.multiple_of(2 * base, 2 * lanes), 2 * lanes)],
                (((1,), (1,)), ((), ())), preferred_element_type=F32,
            )

        for k in range(CHUNKS // 2):
            @pl.when(c == k)
            def _():
                gather4(CHUNKS // 2 + k)

        return carry

    lax.fori_loop(0, CHUNKS, score_chunk, 0)

    power_col = 0.5 * jnp.sum(power[...], axis=1, keepdims=True)
    distance = jnp.abs(my_ori - center_ref[...])
    allowed = jnp.minimum(distance, n_ori - distance) <= n_ori // 4
    best = None
    for t in range(shifts):
        at = pl.ds(t * slots, slots)
        value = jnp.where(allowed, acc[at, :] - power_col, NEG_FILL)
        acc[at, :] = value
        top = jnp.max(value, axis=0, keepdims=True)
        best = top if best is None else jnp.maximum(best, top)
    total = jnp.zeros_like(best)
    for t in range(shifts):
        total += jnp.sum(jnp.exp(acc[pl.ds(t * slots, slots), :] - best), axis=0, keepdims=True)
    stat_out[0:1, :] = best
    stat_out[1:2, :] = total

    def stat_send(i, carry):
        send(stat_out, stat_in.at[my_ori], st_send, st_recv, {"orient": lax.rem(my_ori + i, n_ori)})
        return carry

    lax.fori_loop(1, n_ori, stat_send, 0)
    stat_in[my_ori] = stat_out[...]
    if n_ori > 1:
        others = stat_in.at[pl.ds(0, n_ori - 1)]
        wait(others, st_recv)
        wait(others, st_send)
    bests = [stat_in[o, 0:1, :] for o in range(n_ori)]
    best = functools.reduce(jnp.maximum, bests)
    total = sum(stat_in[o, 1:2, :] * jnp.exp(bests[o] - best) for o in range(n_ori))
    loglik_ref[...] = best + jnp.log(total)

    pick = (lax.broadcasted_iota(jnp.int32, (slots, slots), 0) == omap_ref[...]).astype(F32).astype(BF16)
    weights = jnp.concatenate(
        [(jnp.exp(acc[pl.ds(t * slots, slots), :] - best) / total).astype(BF16) for t in range(shifts)], axis=1
    )
    picked = lax.dot_general(pick, weights, (((0,), (0,)), ((), ())), preferred_element_type=F32).astype(BF16)
    pcount = acc.shape[1]
    for t in range(shifts):
        by_class[pl.ds(t * slots, slots), :] = picked[:, t * pcount:(t + 1) * pcount]

    def sum_chunk(c):
        odd, v, u = axes(c)

        def multiply(g):
            base = pl.multiple_of(2 * (c * width + g * lanes), 2 * lanes)
            prods[g % 2] = jnp.dot(by_class[...], part[:, pl.ds(base, 2 * lanes)], preferred_element_type=F32)

        multiply(0)
        for g in range(GROUPS):
            if g + 1 < GROUPS:
                multiply(g + 1)
            for j in range(lanes // 128):
                at = pl.ds(j * 128, 128)
                there = pl.ds(pl.multiple_of(c * width + g * lanes + j * 128, 128), 128)
                out_real = out_imag = None
                for t in range(shifts):
                    cosine = cos_tab[pl.ds(t, 1), there]
                    sine = sin_tab[pl.ds(t, 1), there]
                    re = prods[g % 2, pl.ds(t * slots, slots), at]
                    im = prods[g % 2, pl.ds(t * slots, slots), pl.ds(lanes + j * 128, 128)]
                    term_real = re * cosine - im * sine
                    term_imag = im * cosine + re * sine
                    out_real = term_real if t == 0 else out_real + term_real
                    out_imag = term_imag if t == 0 else out_imag + term_imag
                rows[g, :, at] = out_real
                rows[GROUPS + g, :, at] = out_imag

        for h in range(2):
            tiles = [rows[q, pl.ds(tile_row(odd, h, k), 8), :] for q in range(8) for k in range(4)]
            spread = jnp.dot(
                perm_t[odd], jnp.concatenate(tiles, axis=0).astype(BF16), preferred_element_type=F32
            ).astype(BF16)
            sends[c, pl.ds(16 * h, 16)] = spread.reshape(16, 16, lanes)

    def reduce0(c):
        odd, v, u = axes(c)
        for k, by in ((0, 1), (1, 3)):
            to = device(odd, step(v, by), u, my_z)
            send(sends.at[c, pl.ds(step(v, 2) * 8 + k * half, half)], far_in.at[c, k], rs_send.at[c], far_sem.at[c, k], to)
        for k, by in ((0, 1), (1, 3)):
            to = device(odd, step(v, by), u, my_z)
            other = (1 - k) * half
            send(
                sends.at[c, pl.ds(step(v, by) * 8 + other, half)], near_in.at[c, k, pl.ds(other, half)],
                rs_send.at[c], early_sem.at[c, k], to,
            )

    def reduce1(c):
        odd, v, u = axes(c)
        for k, by in ((0, 1), (1, 3)):
            wait(far_in.at[c, k], far_sem.at[c, k])
            at = step(v, by) * 8 + k * half

            def add(i, carry):
                sends[c, at + i] = (sends[c, at + i].astype(F32) + far_in[c, k, i].astype(F32)).astype(BF16)
                return carry

            lax.fori_loop(0, half, add, 0)
            send(
                sends.at[c, pl.ds(at, half)], near_in.at[c, k, pl.ds(k * half, half)], rs_send.at[c],
                late_sem.at[c, k], device(odd, step(v, by), u, my_z),
            )

    def reduce2(c):
        odd, v, u = axes(c)
        for k in range(2):
            wait(near_in.at[c, k, pl.ds((1 - k) * half, half)], early_sem.at[c, k])
            wait(near_in.at[c, k, pl.ds(k * half, half)], late_sem.at[c, k])

        def add(q, carry):
            send2[c, q] = (
                sends[c, v * 8 + q].astype(F32) + near_in[c, 0, q].astype(F32) + near_in[c, 1, q].astype(F32)
            ).astype(BF16)
            return carry

        lax.fori_loop(0, 8, add, 0)
        home = u * 2 + my_z

        def share(i, carry):
            q = (home + i) % 8
            send(send2.at[c, q], recv2.at[c, home], rs_send.at[c], rs_recv.at[c], device(odd, v, q // 2, q % 2))
            return carry

        lax.fori_loop(1, 8, share, 0)
        recv2[c, home] = send2[c, home]

    def sum_step(i, carry):
        @pl.when(i < CHUNKS)
        def _():
            sum_chunk(i)
            reduce0(i)

        @pl.when((i >= 1) & (i < CHUNKS + 1))
        def _():
            reduce1(i - 1)

        @pl.when(i >= 2)
        def _():
            reduce2(i - 2)

        return carry

    lax.fori_loop(0, CHUNKS + 2, sum_step, 0)

    for c in range(CHUNKS):
        wait(recv2.at[c, pl.ds(0, 7)], rs_recv.at[c])
        for j in range(lanes // 128):
            total = recv2[c, 0, :, pl.ds(j * 128, 128)].astype(F32)
            for q in range(1, 8):
                total += recv2[c, q, :, pl.ds(j * 128, 128)].astype(F32)
            for s in range(2):
                for r in range(2):
                    for g in range(GROUPS):
                        row = s * 8 + r * GROUPS + g
                        at = r * freqs + c * width + g * lanes + j * 128
                        out_ref[s, :, pl.ds(at, 128)] = total[row:row + 1, :]

    def drain(c, carry):
        wait(gath.at[c, pl.ds(0, n_dom - 1)], ag_send.at[c])
        wait(gath.at[c, pl.ds(0, 31)], rs_send.at[c])
        return carry

    lax.fori_loop(0, CHUNKS, drain, 0)


def per_device(n_dom, n_ori, particles, refs, inv_sigma2, offsets, owner_map, center):
    pcount, feat = particles.shape
    freqs = feat // 2
    shifts = offsets.shape[0]
    slots = 2 * n_dom
    lanes = freqs // (CHUNKS * GROUPS)
    vmem = pl.BlockSpec(memory_space=pltpu.VMEM)
    anywhere = pl.BlockSpec(memory_space=pl.ANY)
    dma = pltpu.SemaphoreType.DMA
    sums, loglik = pl.pallas_call(
        functools.partial(em_kernel, n_dom, n_ori, shifts),
        out_shape=(
            jax.ShapeDtypeStruct((2, 1, feat), F32),
            jax.ShapeDtypeStruct((1, pcount), F32),
        ),
        in_specs=[vmem, anywhere, anywhere, pl.BlockSpec(memory_space=pltpu.SMEM), anywhere, anywhere],
        out_specs=(vmem, vmem),
        scratch_shapes=[
            pltpu.VMEM((pcount, feat), BF16),
            pltpu.VMEM((lanes // 128, 16 * CHUNKS, 128), F32),
            pltpu.VMEM((CHUNKS, 16, lanes), BF16),
            pltpu.VMEM((CHUNKS, n_dom, 16, lanes), BF16),
            pltpu.VMEM((2 * GROUPS, slots, lanes), F32),
            pltpu.VMEM((2, 256, 256), BF16),
            pltpu.VMEM((2, 256, 256), BF16),
            pltpu.VMEM((shifts, freqs), F32),
            pltpu.VMEM((shifts, freqs), F32),
            pltpu.VMEM((2, shifts * slots, 2 * lanes), BF16),
            pltpu.VMEM((shifts * slots, pcount), F32),
            pltpu.VMEM((2, shifts * slots, 2 * lanes), F32),
            pltpu.VMEM((slots, 128), F32),
            pltpu.VMEM((1, freqs), F32),
            pltpu.VMEM((1, slots), jnp.int32),
            pltpu.VMEM((1, pcount), jnp.int32),
            pltpu.VMEM((8, pcount), F32),
            pltpu.VMEM((n_ori, 8, pcount), F32),
            pltpu.VMEM((shifts * slots, pcount), BF16),
            pltpu.VMEM((CHUNKS, n_dom, 16, lanes), BF16),
            pltpu.VMEM((CHUNKS, 2, RING, 16, lanes), BF16),
            pltpu.VMEM((CHUNKS, 2, 8, 16, lanes), BF16),
            pltpu.VMEM((CHUNKS, 8, 16, lanes), BF16),
            pltpu.VMEM((CHUNKS, 8, 16, lanes), BF16),
            dma((CHUNKS,)),
            dma((3,)),
            dma((CHUNKS,)),
            dma((CHUNKS, 9)),
            dma,
            dma,
            dma((CHUNKS,)),
            dma((CHUNKS, 2)),
            dma((CHUNKS, 2)),
            dma((CHUNKS, 2)),
            dma((CHUNKS,)),
        ],
        compiler_params=pltpu.CompilerParams(
            collective_id=0, has_side_effects=True, vmem_limit_bytes=56 * 1024 * 1024
        ),
        cost_estimate=pl.CostEstimate(
            flops=4 * shifts * slots * pcount * feat, bytes_accessed=2 * pcount * feat, transcendentals=0
        ),
    )(
        refs.reshape(2, feat), particles, inv_sigma2.reshape(1, freqs), offsets.T, owner_map.reshape(1, slots),
        center.reshape(1, pcount),
    )
    return sums, loglik.reshape(pcount)


def solution(mesh):
    return jax.shard_map(
        functools.partial(per_device, mesh.shape["dom"], mesh.shape["orient"]),
        mesh=mesh,
        in_specs=(P("dom", None), P("dom", "orient", None), P(), P(), P(), P("dom")),
        out_specs=(P("dom", "orient", None), P("dom")),
        check_vma=False,
    )
```

```python
import functools
import math

import jax
import jax.numpy as jnp
from jax import lax
from jax.experimental import pallas as pl
from jax.experimental.pallas import tpu as pltpu
from jax.sharding import PartitionSpec as P

BOX = 128
CHUNKS = 8
GROUPS = 4
PAIRS = CHUNKS // 2
LAG = CHUNKS // 4
RING = 4
NEG_FILL = -1e30
MESH = pl.DeviceIdType.MESH
BF16, F32 = jnp.bfloat16, jnp.float32


def unit_circle(phase):
    folded = ((phase + 64) & 127) - 64
    quarter = (folded + 16) >> 5
    x = (folded - quarter * 32).astype(F32) * (2.0 * math.pi / BOX)
    x2 = x * x
    sine = x * (1.0 + x2 * (-1 / 6 + x2 * (1 / 120 + x2 * (-1 / 5040 + x2 * (1 / 362880)))))
    cosine = 1.0 + x2 * (-0.5 + x2 * (1 / 24 + x2 * (-1 / 720 + x2 * (1 / 40320))))
    odd = (quarter & 1) == 1
    cos_sign = jnp.where(((quarter + 1) & 2) == 2, -1.0, 1.0)
    sin_sign = jnp.where((quarter & 2) == 2, -1.0, 1.0)
    return jnp.where(odd, sine, cosine) * cos_sign, jnp.where(odd, cosine, sine) * sin_sign


def em_kernel(
    n_dom, n_ori, shifts,
    refs_hbm, part_hbm, inv_hbm, off_hbm, omap_hbm, center_hbm,
    out_ref, loglik_ref,
    part, stage, mine, gath, rows, perm, perm_t, cos_tab, sin_tab, lhs, acc, prods, power, refs_ref, off_ref, inv_ref, omap_ref, center_ref,
    stat_out, stat_in, by_class, sends, far_in, near_in, send2, recv2,
    part_sem, small_sem, ag_send, ag_recv, ag_near, ag_far, st_send, st_recv, rs_send, far_sem, early_sem, late_sem, rs_recv,
):
    freqs = inv_ref.shape[1]
    slots = 2 * n_dom
    lanes = mine.shape[2]
    width = freqs // CHUNKS
    half = RING
    me = lax.axis_index("dom")
    my_ori = lax.axis_index("orient")
    my_y, my_x, my_z = me // 8, (me // 2) % 4, me % 2

    def axes(c):
        odd = c % 2
        return odd, my_y * (1 - odd) + my_x * odd, my_x * (1 - odd) + my_y * odd

    def device(odd, v, u, z):
        return {"dom": ((v * (1 - odd) + u * odd) * 4 + u * (1 - odd) + v * odd) * 2 + z}

    def step(a, by):
        return (a + by) % RING

    def tile_row(odd, h, k):
        return pl.multiple_of((32 * h + 8 * k) * (1 - odd) + (16 * k + 8 * h) * odd, 8)

    def send(src, dst, send_sem, recv_sem, to):
        pltpu.make_async_remote_copy(
            src_ref=src, dst_ref=dst, send_sem=send_sem, recv_sem=recv_sem, device_id=to, device_id_type=MESH
        ).start()

    def wait(ref, sem):
        pltpu.make_async_copy(ref, ref, sem).wait()

    smalls = [
        pltpu.make_async_copy(src, dst, small_sem.at[k])
        for k, (src, dst) in enumerate((
            (refs_hbm, refs_ref), (off_hbm, off_ref), (inv_hbm, inv_ref), (omap_hbm, omap_ref), (center_hbm, center_ref)
        ))
    ]

    def fetch(k, carry):
        for r, base in enumerate((0, freqs)):
            pltpu.make_async_copy(
                part_hbm.at[:, pl.ds(pl.multiple_of(base + k * 2 * lanes, 2 * lanes), 2 * lanes)],
                part.at[:, pl.ds(pl.multiple_of((2 * k + r) * 2 * lanes, 2 * lanes), 2 * lanes)],
                part_sem.at[k // (GROUPS // 2)],
            ).start()
        return carry

    for copy in smalls:
        copy.start()

    barrier = pltpu.get_barrier_semaphore()

    def greet(to):
        pl.semaphore_signal(barrier, inc=1, device_id=to, device_id_type=MESH)

    peers = [device(0, my_y, my_x, 1 - my_z)]
    for by in (1, 2, 3):
        for z in (my_z, 1 - my_z):
            peers.append(device(0, my_y, step(my_x, by), z))
            peers.append(device(0, step(my_y, by), my_x, z))
    for to in peers:
        greet(to)

    def greet_ori(i, carry):
        greet({"orient": lax.rem(my_ori + i, n_ori)})
        return carry

    lax.fori_loop(1, n_ori, greet_ori, 0)

    lax.fori_loop(0, CHUNKS * GROUPS // 2, fetch, 0)
    smalls[0].wait()

    def exchange(first, second):
        for odd in range(2):
            there = lax.broadcasted_iota(jnp.int32, (256, 256), 0)
            here = lax.broadcasted_iota(jnp.int32, (256, 256), 1)
            for ref, out, src in ((first, there, here), (second, here, there)):
                at, s, q = src >> 4, (src >> 3) & 1, src & 7
                if odd:
                    row = ((at >> 1) & 3) * 8 + (at >> 3) * 4 + (at & 1) * 2 + s
                else:
                    row = at * 2 + s
                ref[odd] = (out == q * 32 + row).astype(F32).astype(BF16)

    for c in range(CHUNKS):
        for r in range(2):
            for g in range(GROUPS):
                for j in range(lanes // 128):
                    at = r * freqs + c * width + g * lanes + j * 128
                    stage[j, pl.ds(c * 16 + r * GROUPS + g, 2, stride=8), :] = refs_ref[:, pl.ds(at, 128)].astype(F32)
        for j in range(lanes // 128):
            mine[c, :, pl.ds(j * 128, 128)] = stage[j, pl.ds(c * 16, 16), :].astype(BF16)

    pl.semaphore_wait(barrier, len(peers) + n_ori - 1)

    def gather0(c):
        odd, v, u = axes(c)
        home = u * 2 + my_z
        at = v * 8 + home

        def share(i, carry):
            q = (home + i) % 8
            send(mine.at[c], gath.at[c, at], ag_send.at[c], ag_recv.at[c], device(odd, v, q // 2, q % 2))
            return carry

        lax.fori_loop(1, 8, share, 0)
        gath[c, at] = mine[c]

    def gather1(c):
        odd, v, u = axes(c)
        wait(gath.at[c, pl.ds(0, 7)], ag_recv.at[c])
        for first in range(2):
            for k, by in ((0, 1), (1, 3)):
                h = k if first == 0 else 1 - k
                block = gath.at[c, pl.ds(v * 8 + h * half, half)]
                send(block, block, ag_send.at[c], ag_near.at[c, k, h], device(odd, step(v, by), u, my_z))

    def gather2(c):
        odd, v, u = axes(c)
        for k, by in ((0, 1), (1, 3)):
            block = gath.at[c, pl.ds(step(v, 4 - by) * 8 + k * half, half)]
            wait(block, ag_near.at[c, k, k])
            send(block, block, ag_send.at[c], ag_far.at[c, k], device(odd, step(v, by), u, my_z))

    def gather3(c):
        block = gath.at[c, pl.ds(0, half)]
        for k in range(2):
            wait(block, ag_near.at[c, k, 1 - k])
            wait(block, ag_far.at[c, k])

    def pair(k, stage):
        def one(i, carry):
            stage(2 * k + i)
            return carry

        lax.fori_loop(0, 2, one, 0)

    pair(0, gather0)
    pair(1, gather0)
    exchange(perm, perm_t)
    smalls[1].wait()

    shift_ids = lax.broadcasted_iota(jnp.int32, (shifts, 128), 0)
    off_x = jnp.zeros((shifts, 128), jnp.int32)
    off_y = jnp.zeros((shifts, 128), jnp.int32)
    for t in range(shifts):
        off_x = jnp.where(shift_ids == t, off_ref[0, t], off_x)
        off_y = jnp.where(shift_ids == t, off_ref[1, t], off_y)

    def tables(j, carry):
        for h in range(4):
            at = pl.multiple_of(j * 512 + h * 128, 128)
            freq = lax.broadcasted_iota(jnp.int32, (shifts, 128), 1) + at
            fx = freq & (BOX // 2 - 1)
            fy = freq >> 6
            fy = jnp.where(fy < BOX // 2, fy, fy - BOX)
            cosine, sine = unit_circle(off_x * fx + off_y * fy)
            cos_tab[:, pl.ds(at, 128)] = cosine
            sin_tab[:, pl.ds(at, 128)] = sine
        return carry

    lax.fori_loop(0, freqs // 1024, tables, 0)
    pair(0, gather1)
    pair(2, gather0)
    pair(3, gather0)
    pair(1, gather1)
    lax.fori_loop(freqs // 1024, freqs // 512, tables, 0)
    for copy in smalls[2:]:
        copy.wait()
    acc[...] = jnp.zeros_like(acc)
    power[...] = jnp.zeros_like(power)
    pair(0, gather2)
    pair(2, gather1)

    def score_chunk(c, carry):
        odd, v, u = axes(c)
        wait(part.at[:, pl.ds(0, 2 * width)], part_sem.at[c])
        gather3(c)

        for h in range(2):
            spread = jnp.dot(
                perm[odd], gath[c, pl.ds(16 * h, 16)].reshape(256, lanes), preferred_element_type=F32
            )
            for q in range(8):
                for k in range(4):
                    rows[q, pl.ds(tile_row(odd, h, k), 8), :] = spread[q * 32 + k * 8:q * 32 + k * 8 + 8, :]

        for g in range(GROUPS):
            for j in range(lanes // 128):
                col = g % 2 * lanes + j * 128
                there = pl.ds(pl.multiple_of(c * width + g * lanes + j * 128, 128), 128)
                real = rows[g, :, pl.ds(j * 128, 128)]
                imag = rows[GROUPS + g, :, pl.ds(j * 128, 128)]
                inv = inv_ref[:, there]
                re = real * inv
                im = imag * inv
                power[...] += re * real + im * imag
                for t in range(shifts):
                    cosine = cos_tab[pl.ds(t, 1), there]
                    sine = sin_tab[pl.ds(t, 1), there]
                    into = lhs.at[g // 2 % 2, pl.ds(t * slots, slots)]
                    into[:, pl.ds(col, 128)] = (re * cosine + im * sine).astype(BF16)
                    into[:, pl.ds(2 * lanes + col, 128)] = (im * cosine - re * sine).astype(BF16)
            if g % 2 == 1:
                base = pl.multiple_of(2 * (c * width + (g - 1) * lanes), 4 * lanes)
                acc[...] += lax.dot_general(
                    lhs[g // 2 % 2], part[:, pl.ds(base, 4 * lanes)],
                    (((1,), (1,)), ((), ())), preferred_element_type=F32,
                )

        @pl.when((c % 2 == 0) & (c < CHUNKS - 2))
        def _():
            pair(c // 2 + 1, gather2)

        @pl.when((c % 2 == 1) & (c < CHUNKS - 6))
        def _():
            pair(c // 2 + 3, gather1)

        return carry

    lax.fori_loop(0, CHUNKS, score_chunk, 0)

    power_col = 0.5 * jnp.sum(power[...], axis=1, keepdims=True)
    distance = jnp.abs(my_ori - center_ref[...])
    allowed = jnp.minimum(distance, n_ori - distance) <= n_ori // 4
    best = None
    for t in range(shifts):
        at = pl.ds(t * slots, slots)
        value = jnp.where(allowed, acc[at, :] - power_col, NEG_FILL)
        acc[at, :] = value
        top = jnp.max(value, axis=0, keepdims=True)
        best = top if best is None else jnp.maximum(best, top)
    total = jnp.zeros_like(best)
    for t in range(shifts):
        total += jnp.sum(jnp.exp(acc[pl.ds(t * slots, slots), :] - best), axis=0, keepdims=True)
    stat_out[0:1, :] = best
    stat_out[1:2, :] = total

    def stat_send(i, carry):
        send(stat_out, stat_in.at[my_ori], st_send, st_recv, {"orient": lax.rem(my_ori + i, n_ori)})
        return carry

    lax.fori_loop(1, n_ori, stat_send, 0)
    stat_in[my_ori] = stat_out[...]
    if n_ori > 1:
        others = stat_in.at[pl.ds(0, n_ori - 1)]
        wait(others, st_recv)
        wait(others, st_send)
    bests = [stat_in[o, 0:1, :] for o in range(n_ori)]
    best = functools.reduce(jnp.maximum, bests)
    total = sum(stat_in[o, 1:2, :] * jnp.exp(bests[o] - best) for o in range(n_ori))
    loglik_ref[...] = best + jnp.log(total)

    pick = (lax.broadcasted_iota(jnp.int32, (slots, slots), 0) == omap_ref[...]).astype(F32).astype(BF16)
    weights = jnp.concatenate(
        [(jnp.exp(acc[pl.ds(t * slots, slots), :] - best) / total).astype(BF16) for t in range(shifts)], axis=1
    )
    picked = lax.dot_general(pick, weights, (((0,), (0,)), ((), ())), preferred_element_type=F32).astype(BF16)
    pcount = acc.shape[1]
    for t in range(shifts):
        by_class[pl.ds(t * slots, slots), :] = picked[:, t * pcount:(t + 1) * pcount]

    def sum_chunk(c):
        odd, v, u = axes(c)

        def multiply(g):
            base = pl.multiple_of(2 * (c * width + 2 * g * lanes), 4 * lanes)
            prods[g % 2] = jnp.dot(by_class[...], part[:, pl.ds(base, 4 * lanes)], preferred_element_type=F32)

        multiply(0)
        for g in range(GROUPS):
            if g % 2 == 0 and g // 2 + 1 < GROUPS // 2:
                multiply(g // 2 + 1)
            for j in range(lanes // 128):
                at = pl.ds(j * 128, 128)
                col = g % 2 * lanes + j * 128
                there = pl.ds(pl.multiple_of(c * width + g * lanes + j * 128, 128), 128)
                out_real = out_imag = None
                for t in range(shifts):
                    cosine = cos_tab[pl.ds(t, 1), there]
                    sine = sin_tab[pl.ds(t, 1), there]
                    block = prods.at[g // 2 % 2, pl.ds(t * slots, slots)]
                    re = block[:, pl.ds(col, 128)]
                    im = block[:, pl.ds(2 * lanes + col, 128)]
                    term_real = re * cosine - im * sine
                    term_imag = im * cosine + re * sine
                    out_real = term_real if t == 0 else out_real + term_real
                    out_imag = term_imag if t == 0 else out_imag + term_imag
                rows[g, :, at] = out_real
                rows[GROUPS + g, :, at] = out_imag

        for h in range(2):
            tiles = [rows[q, pl.ds(tile_row(odd, h, k), 8), :] for q in range(8) for k in range(4)]
            spread = jnp.dot(
                perm_t[odd], jnp.concatenate(tiles, axis=0).astype(BF16), preferred_element_type=F32
            ).astype(BF16)
            sends[c, pl.ds(16 * h, 16)] = spread.reshape(16, 16, lanes)

    def reduce0(c):
        odd, v, u = axes(c)
        for k, by in ((0, 1), (1, 3)):
            to = device(odd, step(v, by), u, my_z)
            send(sends.at[c, pl.ds(step(v, 2) * 8 + k * half, half)], far_in.at[c, k], rs_send.at[c], far_sem.at[c, k], to)
        for k, by in ((0, 1), (1, 3)):
            to = device(odd, step(v, by), u, my_z)
            other = (1 - k) * half
            send(
                sends.at[c, pl.ds(step(v, by) * 8 + other, half)], near_in.at[c, k, pl.ds(other, half)],
                rs_send.at[c], early_sem.at[c, k], to,
            )

    def reduce1(c):
        odd, v, u = axes(c)
        for k, by in ((0, 1), (1, 3)):
            wait(far_in.at[c, k], far_sem.at[c, k])
            at = step(v, by) * 8 + k * half

            def add(i, carry):
                sends[c, at + i] = (sends[c, at + i].astype(F32) + far_in[c, k, i].astype(F32)).astype(BF16)
                return carry

            lax.fori_loop(0, half, add, 0)
            send(
                sends.at[c, pl.ds(at, half)], near_in.at[c, k, pl.ds(k * half, half)], rs_send.at[c],
                late_sem.at[c, k], device(odd, step(v, by), u, my_z),
            )

    def reduce2(c):
        odd, v, u = axes(c)
        for k in range(2):
            wait(near_in.at[c, k, pl.ds((1 - k) * half, half)], early_sem.at[c, k])
            wait(near_in.at[c, k, pl.ds(k * half, half)], late_sem.at[c, k])

        def add(q, carry):
            send2[c, q] = (
                sends[c, v * 8 + q].astype(F32) + near_in[c, 0, q].astype(F32) + near_in[c, 1, q].astype(F32)
            ).astype(BF16)
            return carry

        lax.fori_loop(0, 8, add, 0)
        home = u * 2 + my_z

        def share(i, carry):
            q = (home + i) % 8
            send(send2.at[c, q], recv2.at[c, home], rs_send.at[c], rs_recv.at[c], device(odd, v, q // 2, q % 2))
            return carry

        lax.fori_loop(1, 8, share, 0)
        recv2[c, home] = send2[c, home]

    def sum_step(i, carry):
        @pl.when(i < CHUNKS)
        def _():
            sum_chunk(i)
            reduce0(i)

        @pl.when((i >= LAG) & (i < CHUNKS + LAG))
        def _():
            reduce1(i - LAG)

        @pl.when(i >= 2 * LAG)
        def _():
            reduce2(i - 2 * LAG)

        return carry

    lax.fori_loop(0, CHUNKS + 2 * LAG, sum_step, 0)

    for c in range(CHUNKS):
        wait(recv2.at[c, pl.ds(0, 7)], rs_recv.at[c])
        for j in range(lanes // 128):
            total = recv2[c, 0, :, pl.ds(j * 128, 128)].astype(F32)
            for q in range(1, 8):
                total += recv2[c, q, :, pl.ds(j * 128, 128)].astype(F32)
            for s in range(2):
                for r in range(2):
                    for g in range(GROUPS):
                        row = s * 8 + r * GROUPS + g
                        at = r * freqs + c * width + g * lanes + j * 128
                        out_ref[s, :, pl.ds(at, 128)] = total[row:row + 1, :]

    def drain(c, carry):
        wait(gath.at[c, pl.ds(0, n_dom - 1)], ag_send.at[c])
        wait(gath.at[c, pl.ds(0, 31)], rs_send.at[c])
        return carry

    lax.fori_loop(0, CHUNKS, drain, 0)


def per_device(n_dom, n_ori, particles, refs, inv_sigma2, offsets, owner_map, center):
    pcount, feat = particles.shape
    freqs = feat // 2
    shifts = offsets.shape[0]
    slots = 2 * n_dom
    lanes = freqs // (CHUNKS * GROUPS)
    vmem = pl.BlockSpec(memory_space=pltpu.VMEM)
    far = pl.BlockSpec(memory_space=pltpu.HBM)
    dma = pltpu.SemaphoreType.DMA
    sums, loglik = pl.pallas_call(
        functools.partial(em_kernel, n_dom, n_ori, shifts),
        out_shape=(
            jax.ShapeDtypeStruct((2, 1, feat), F32),
            jax.ShapeDtypeStruct((1, pcount), F32),
        ),
        in_specs=[far] * 6,
        out_specs=(vmem, vmem),
        scratch_shapes=[
            pltpu.VMEM((pcount, feat), BF16),
            pltpu.VMEM((lanes // 128, 16 * CHUNKS, 128), F32),
            pltpu.VMEM((CHUNKS, 16, lanes), BF16),
            pltpu.VMEM((CHUNKS, n_dom, 16, lanes), BF16),
            pltpu.VMEM((2 * GROUPS, slots, lanes), F32),
            pltpu.VMEM((2, 256, 256), BF16),
            pltpu.VMEM((2, 256, 256), BF16),
            pltpu.VMEM((shifts, freqs), F32),
            pltpu.VMEM((shifts, freqs), F32),
            pltpu.VMEM((2, shifts * slots, 4 * lanes), BF16),
            pltpu.VMEM((shifts * slots, pcount), F32),
            pltpu.VMEM((2, shifts * slots, 4 * lanes), F32),
            pltpu.VMEM((slots, 128), F32),
            pltpu.VMEM((2, feat), BF16),
            pltpu.SMEM((2, shifts), jnp.int32),
            pltpu.VMEM((1, freqs), F32),
            pltpu.VMEM((1, slots), jnp.int32),
            pltpu.VMEM((1, pcount), jnp.int32),
            pltpu.VMEM((8, pcount), F32),
            pltpu.VMEM((n_ori, 8, pcount), F32),
            pltpu.VMEM((shifts * slots, pcount), BF16),
            pltpu.VMEM((CHUNKS, n_dom, 16, lanes), BF16),
            pltpu.VMEM((CHUNKS, 2, RING, 16, lanes), BF16),
            pltpu.VMEM((CHUNKS, 2, 8, 16, lanes), BF16),
            pltpu.VMEM((CHUNKS, 8, 16, lanes), BF16),
            pltpu.VMEM((CHUNKS, 8, 16, lanes), BF16),
            dma((CHUNKS,)),
            dma((5,)),
            dma((CHUNKS,)),
            dma((CHUNKS,)),
            dma((CHUNKS, 2, 2)),
            dma((CHUNKS, 2)),
            dma,
            dma,
            dma((CHUNKS,)),
            dma((CHUNKS, 2)),
            dma((CHUNKS, 2)),
            dma((CHUNKS, 2)),
            dma((CHUNKS,)),
        ],
        compiler_params=pltpu.CompilerParams(
            collective_id=0, has_side_effects=True, vmem_limit_bytes=56 * 1024 * 1024
        ),
        cost_estimate=pl.CostEstimate(
            flops=4 * shifts * slots * pcount * feat, bytes_accessed=2 * pcount * feat, transcendentals=0
        ),
    )(
        refs.reshape(2, feat), particles, inv_sigma2.reshape(1, freqs), offsets.T, owner_map.reshape(1, slots),
        center.reshape(1, pcount),
    )
    return sums, loglik.reshape(pcount)


def solution(mesh):
    return jax.shard_map(
        functools.partial(per_device, mesh.shape["dom"], mesh.shape["orient"]),
        mesh=mesh,
        in_specs=(P("dom", None), P("dom", "orient", None), P(), P(), P(), P("dom")),
        out_specs=(P("dom", "orient", None), P("dom")),
        check_vma=False,
    )
```

```python
import functools
import math

import jax
import jax.numpy as jnp
from jax import lax
from jax.experimental import pallas as pl
from jax.experimental.pallas import tpu as pltpu
from jax.sharding import PartitionSpec as P

BOX = 128
CHUNKS = 8
GROUPS = 4
PAIRS = CHUNKS // 2
LAG = CHUNKS // 4
RING = 4
NEG_FILL = -1e30
MESH = pl.DeviceIdType.MESH
BF16, F32 = jnp.bfloat16, jnp.float32


def unit_circle(phase):
    folded = ((phase + 64) & 127) - 64
    quarter = (folded + 16) >> 5
    x = (folded - quarter * 32).astype(F32) * (2.0 * math.pi / BOX)
    x2 = x * x
    sine = x * (1.0 + x2 * (-1 / 6 + x2 * (1 / 120 + x2 * (-1 / 5040 + x2 * (1 / 362880)))))
    cosine = 1.0 + x2 * (-0.5 + x2 * (1 / 24 + x2 * (-1 / 720 + x2 * (1 / 40320))))
    odd = (quarter & 1) == 1
    cos_sign = jnp.where(((quarter + 1) & 2) == 2, -1.0, 1.0)
    sin_sign = jnp.where((quarter & 2) == 2, -1.0, 1.0)
    return jnp.where(odd, sine, cosine) * cos_sign, jnp.where(odd, cosine, sine) * sin_sign


def em_kernel(
    n_dom, n_ori, shifts,
    refs_hbm, part_hbm, inv_hbm, off_hbm, omap_hbm, center_hbm,
    out_ref, loglik_ref,
    part, part_t, stage, mine, gath, rows, perm, perm_t, cos_tab, sin_tab, lhs, acc, prods, power, refs_ref, off_ref, inv_ref, omap_ref, center_ref,
    stat_out, stat_in, by_class, sends, far_in, near_in, send2, recv2,
    part_sem, small_sem, ag_send, ag_recv, ag_near, ag_far, st_send, st_recv, rs_send, far_sem, early_sem, late_sem, rs_recv,
):
    freqs = inv_ref.shape[1]
    slots = 2 * n_dom
    lanes = mine.shape[2]
    width = freqs // CHUNKS
    half = RING
    me = lax.axis_index("dom")
    my_ori = lax.axis_index("orient")
    my_y, my_x, my_z = me // 8, (me // 2) % 4, me % 2

    def axes(c):
        odd = c % 2
        return odd, my_y * (1 - odd) + my_x * odd, my_x * (1 - odd) + my_y * odd

    def device(odd, v, u, z):
        return {"dom": ((v * (1 - odd) + u * odd) * 4 + u * (1 - odd) + v * odd) * 2 + z}

    def step(a, by):
        return (a + by) % RING

    def tile_row(odd, h, k):
        return pl.multiple_of((32 * h + 8 * k) * (1 - odd) + (16 * k + 8 * h) * odd, 8)

    def send(src, dst, send_sem, recv_sem, to):
        pltpu.make_async_remote_copy(
            src_ref=src, dst_ref=dst, send_sem=send_sem, recv_sem=recv_sem, device_id=to, device_id_type=MESH
        ).start()

    def wait(ref, sem):
        pltpu.make_async_copy(ref, ref, sem).wait()

    smalls = [
        pltpu.make_async_copy(src, dst, small_sem.at[k])
        for k, (src, dst) in enumerate((
            (refs_hbm, refs_ref), (off_hbm, off_ref), (inv_hbm, inv_ref), (omap_hbm, omap_ref), (center_hbm, center_ref)
        ))
    ]

    def fetch(k, carry):
        for r, base in enumerate((0, freqs)):
            pltpu.make_async_copy(
                part_hbm.at[:, pl.ds(pl.multiple_of(base + k * 2 * lanes, 2 * lanes), 2 * lanes)],
                part.at[:, pl.ds(pl.multiple_of((2 * k + r) * 2 * lanes, 2 * lanes), 2 * lanes)],
                part_sem.at[k // (GROUPS // 2)],
            ).start()
        return carry

    for copy in smalls:
        copy.start()

    barrier = pltpu.get_barrier_semaphore()

    def greet(to):
        pl.semaphore_signal(barrier, inc=1, device_id=to, device_id_type=MESH)

    peers = [device(0, my_y, my_x, 1 - my_z)]
    for by in (1, 2, 3):
        for z in (my_z, 1 - my_z):
            peers.append(device(0, my_y, step(my_x, by), z))
            peers.append(device(0, step(my_y, by), my_x, z))
    for to in peers:
        greet(to)

    def greet_ori(i, carry):
        greet({"orient": lax.rem(my_ori + i, n_ori)})
        return carry

    lax.fori_loop(1, n_ori, greet_ori, 0)

    lax.fori_loop(0, CHUNKS * GROUPS // 2, fetch, 0)
    smalls[0].wait()

    def exchange(first, second):
        for odd in range(2):
            there = lax.broadcasted_iota(jnp.int32, (256, 256), 0)
            here = lax.broadcasted_iota(jnp.int32, (256, 256), 1)
            for ref, out, src in ((first, there, here), (second, here, there)):
                at, s, q = src >> 4, (src >> 3) & 1, src & 7
                if odd:
                    row = ((at >> 1) & 3) * 8 + (at >> 3) * 4 + (at & 1) * 2 + s
                else:
                    row = at * 2 + s
                ref[odd] = (out == q * 32 + row).astype(F32).astype(BF16)

    for c in range(CHUNKS):
        for r in range(2):
            for g in range(GROUPS):
                for j in range(lanes // 128):
                    at = r * freqs + c * width + g * lanes + j * 128
                    stage[j, pl.ds(c * 16 + r * GROUPS + g, 2, stride=8), :] = refs_ref[:, pl.ds(at, 128)].astype(F32)
        for j in range(lanes // 128):
            mine[c, :, pl.ds(j * 128, 128)] = stage[j, pl.ds(c * 16, 16), :].astype(BF16)

    pl.semaphore_wait(barrier, len(peers) + n_ori - 1)

    def gather0(c):
        odd, v, u = axes(c)
        home = u * 2 + my_z
        at = v * 8 + home

        def share(i, carry):
            q = (home + i) % 8
            send(mine.at[c], gath.at[c, at], ag_send.at[c], ag_recv.at[c], device(odd, v, q // 2, q % 2))
            return carry

        lax.fori_loop(1, 8, share, 0)
        gath[c, at] = mine[c]

    def gather1(c):
        odd, v, u = axes(c)
        wait(gath.at[c, pl.ds(0, 7)], ag_recv.at[c])
        for first in range(2):
            for k, by in ((0, 1), (1, 3)):
                h = k if first == 0 else 1 - k
                block = gath.at[c, pl.ds(v * 8 + h * half, half)]
                send(block, block, ag_send.at[c], ag_near.at[c, k, h], device(odd, step(v, by), u, my_z))

    def gather2(c):
        odd, v, u = axes(c)
        for k, by in ((0, 1), (1, 3)):
            block = gath.at[c, pl.ds(step(v, 4 - by) * 8 + k * half, half)]
            wait(block, ag_near.at[c, k, k])
            send(block, block, ag_send.at[c], ag_far.at[c, k], device(odd, step(v, by), u, my_z))

    def gather3(c):
        block = gath.at[c, pl.ds(0, half)]
        for k in range(2):
            wait(block, ag_near.at[c, k, 1 - k])
            wait(block, ag_far.at[c, k])

    def pair(k, stage):
        def one(i, carry):
            stage(2 * k + i)
            return carry

        lax.fori_loop(0, 2, one, 0)

    def turn(k, carry):
        at = pl.ds(pl.multiple_of(k * 4 * lanes, 4 * lanes), 4 * lanes)
        part_t[at, :] = part[:, at].T
        return carry

    def turn_pair(k):
        for c in (2 * k, 2 * k + 1):
            wait(part.at[:, pl.ds(0, 2 * width)], part_sem.at[c])
        lax.fori_loop(2 * k * GROUPS // 2, (2 * k + 2) * GROUPS // 2, turn, 0)

    pair(0, gather0)
    pair(1, gather0)
    exchange(perm, perm_t)
    smalls[1].wait()

    shift_ids = lax.broadcasted_iota(jnp.int32, (shifts, 128), 0)
    off_x = jnp.zeros((shifts, 128), jnp.int32)
    off_y = jnp.zeros((shifts, 128), jnp.int32)
    for t in range(shifts):
        off_x = jnp.where(shift_ids == t, off_ref[0, t], off_x)
        off_y = jnp.where(shift_ids == t, off_ref[1, t], off_y)

    def tables(j, carry):
        for h in range(4):
            at = pl.multiple_of(j * 512 + h * 128, 128)
            freq = lax.broadcasted_iota(jnp.int32, (shifts, 128), 1) + at
            fx = freq & (BOX // 2 - 1)
            fy = freq >> 6
            fy = jnp.where(fy < BOX // 2, fy, fy - BOX)
            cosine, sine = unit_circle(off_x * fx + off_y * fy)
            cos_tab[:, pl.ds(at, 128)] = cosine
            sin_tab[:, pl.ds(at, 128)] = sine
        return carry

    lax.fori_loop(0, freqs // 1024, tables, 0)
    turn_pair(0)
    pair(0, gather1)
    pair(2, gather0)
    pair(3, gather0)
    pair(1, gather1)
    lax.fori_loop(freqs // 1024, freqs // 512, tables, 0)
    turn_pair(1)
    for copy in smalls[2:]:
        copy.wait()
    acc[...] = jnp.zeros_like(acc)
    power[...] = jnp.zeros_like(power)
    pair(0, gather2)
    turn_pair(2)
    pair(2, gather1)
    turn_pair(3)

    def score_chunk(c, carry):
        odd, v, u = axes(c)
        gather3(c)

        for h in range(2):
            spread = jnp.dot(
                perm[odd], gath[c, pl.ds(16 * h, 16)].reshape(256, lanes), preferred_element_type=F32
            )
            for q in range(8):
                for k in range(4):
                    rows[q, pl.ds(tile_row(odd, h, k), 8), :] = spread[q * 32 + k * 8:q * 32 + k * 8 + 8, :]

        for g in range(GROUPS):
            for j in range(lanes // 128):
                col = g % 2 * lanes + j * 128
                there = pl.ds(pl.multiple_of(c * width + g * lanes + j * 128, 128), 128)
                real = rows[g, :, pl.ds(j * 128, 128)]
                imag = rows[GROUPS + g, :, pl.ds(j * 128, 128)]
                inv = inv_ref[:, there]
                re = real * inv
                im = imag * inv
                power[...] += re * real + im * imag
                for t in range(shifts):
                    cosine = cos_tab[pl.ds(t, 1), there]
                    sine = sin_tab[pl.ds(t, 1), there]
                    into = lhs.at[g // 2 % 2, pl.ds(t * slots, slots)]
                    into[:, pl.ds(col, 128)] = (re * cosine + im * sine).astype(BF16)
                    into[:, pl.ds(2 * lanes + col, 128)] = (im * cosine - re * sine).astype(BF16)
            if g % 2 == 1:
                base = pl.multiple_of(2 * (c * width + (g - 1) * lanes), 4 * lanes)
                acc[...] += jnp.dot(lhs[g // 2 % 2], part_t[pl.ds(base, 4 * lanes), :], preferred_element_type=F32)

        @pl.when((c % 2 == 0) & (c < CHUNKS - 2))
        def _():
            pair(c // 2 + 1, gather2)

        @pl.when((c % 2 == 1) & (c < CHUNKS - 6))
        def _():
            pair(c // 2 + 3, gather1)

        return carry

    lax.fori_loop(0, CHUNKS, score_chunk, 0)

    power_col = 0.5 * jnp.sum(power[...], axis=1, keepdims=True)
    distance = jnp.abs(my_ori - center_ref[...])
    allowed = jnp.minimum(distance, n_ori - distance) <= n_ori // 4
    best = None
    for t in range(shifts):
        at = pl.ds(t * slots, slots)
        value = jnp.where(allowed, acc[at, :] - power_col, NEG_FILL)
        acc[at, :] = value
        top = jnp.max(value, axis=0, keepdims=True)
        best = top if best is None else jnp.maximum(best, top)
    total = jnp.zeros_like(best)
    for t in range(shifts):
        total += jnp.sum(jnp.exp(acc[pl.ds(t * slots, slots), :] - best), axis=0, keepdims=True)
    stat_out[0:1, :] = best
    stat_out[1:2, :] = total

    def stat_send(i, carry):
        send(stat_out, stat_in.at[my_ori], st_send, st_recv, {"orient": lax.rem(my_ori + i, n_ori)})
        return carry

    lax.fori_loop(1, n_ori, stat_send, 0)
    stat_in[my_ori] = stat_out[...]
    if n_ori > 1:
        others = stat_in.at[pl.ds(0, n_ori - 1)]
        wait(others, st_recv)
        wait(others, st_send)
    bests = [stat_in[o, 0:1, :] for o in range(n_ori)]
    best = functools.reduce(jnp.maximum, bests)
    total = sum(stat_in[o, 1:2, :] * jnp.exp(bests[o] - best) for o in range(n_ori))
    loglik_ref[...] = best + jnp.log(total)

    pick = (lax.broadcasted_iota(jnp.int32, (slots, slots), 0) == omap_ref[...]).astype(F32).astype(BF16)
    weights = jnp.concatenate(
        [(jnp.exp(acc[pl.ds(t * slots, slots), :] - best) / total).astype(BF16) for t in range(shifts)], axis=1
    )
    picked = lax.dot_general(pick, weights, (((0,), (0,)), ((), ())), preferred_element_type=F32).astype(BF16)
    pcount = acc.shape[1]
    for t in range(shifts):
        by_class[pl.ds(t * slots, slots), :] = picked[:, t * pcount:(t + 1) * pcount]

    def sum_chunk(c):
        odd, v, u = axes(c)

        def multiply(g):
            base = pl.multiple_of(2 * (c * width + 2 * g * lanes), 4 * lanes)
            prods[g % 2] = jnp.dot(by_class[...], part[:, pl.ds(base, 4 * lanes)], preferred_element_type=F32)

        multiply(0)
        for g in range(GROUPS):
            if g % 2 == 0 and g // 2 + 1 < GROUPS // 2:
                multiply(g // 2 + 1)
            for j in range(lanes // 128):
                at = pl.ds(j * 128, 128)
                col = g % 2 * lanes + j * 128
                there = pl.ds(pl.multiple_of(c * width + g * lanes + j * 128, 128), 128)
                out_real = out_imag = None
                for t in range(shifts):
                    cosine = cos_tab[pl.ds(t, 1), there]
                    sine = sin_tab[pl.ds(t, 1), there]
                    block = prods.at[g // 2 % 2, pl.ds(t * slots, slots)]
                    re = block[:, pl.ds(col, 128)]
                    im = block[:, pl.ds(2 * lanes + col, 128)]
                    term_real = re * cosine - im * sine
                    term_imag = im * cosine + re * sine
                    out_real = term_real if t == 0 else out_real + term_real
                    out_imag = term_imag if t == 0 else out_imag + term_imag
                rows[g, :, at] = out_real
                rows[GROUPS + g, :, at] = out_imag

        for h in range(2):
            tiles = [rows[q, pl.ds(tile_row(odd, h, k), 8), :] for q in range(8) for k in range(4)]
            spread = jnp.dot(
                perm_t[odd], jnp.concatenate(tiles, axis=0).astype(BF16), preferred_element_type=F32
            ).astype(BF16)
            sends[c, pl.ds(16 * h, 16)] = spread.reshape(16, 16, lanes)

    def reduce0(c):
        odd, v, u = axes(c)
        for k, by in ((0, 1), (1, 3)):
            to = device(odd, step(v, by), u, my_z)
            send(sends.at[c, pl.ds(step(v, 2) * 8 + k * half, half)], far_in.at[c, k], rs_send.at[c], far_sem.at[c, k], to)
        for k, by in ((0, 1), (1, 3)):
            to = device(odd, step(v, by), u, my_z)
            other = (1 - k) * half
            send(
                sends.at[c, pl.ds(step(v, by) * 8 + other, half)], near_in.at[c, k, pl.ds(other, half)],
                rs_send.at[c], early_sem.at[c, k], to,
            )

    def reduce1(c):
        odd, v, u = axes(c)
        for k, by in ((0, 1), (1, 3)):
            wait(far_in.at[c, k], far_sem.at[c, k])
            at = step(v, by) * 8 + k * half

            def add(i, carry):
                sends[c, at + i] = (sends[c, at + i].astype(F32) + far_in[c, k, i].astype(F32)).astype(BF16)
                return carry

            lax.fori_loop(0, half, add, 0)
            send(
                sends.at[c, pl.ds(at, half)], near_in.at[c, k, pl.ds(k * half, half)], rs_send.at[c],
                late_sem.at[c, k], device(odd, step(v, by), u, my_z),
            )

    def reduce2(c):
        odd, v, u = axes(c)
        for k in range(2):
            wait(near_in.at[c, k, pl.ds((1 - k) * half, half)], early_sem.at[c, k])
            wait(near_in.at[c, k, pl.ds(k * half, half)], late_sem.at[c, k])

        def add(q, carry):
            send2[c, q] = (
                sends[c, v * 8 + q].astype(F32) + near_in[c, 0, q].astype(F32) + near_in[c, 1, q].astype(F32)
            ).astype(BF16)
            return carry

        lax.fori_loop(0, 8, add, 0)
        home = u * 2 + my_z

        def share(i, carry):
            q = (home + i) % 8
            send(send2.at[c, q], recv2.at[c, home], rs_send.at[c], rs_recv.at[c], device(odd, v, q // 2, q % 2))
            return carry

        lax.fori_loop(1, 8, share, 0)
        recv2[c, home] = send2[c, home]

    def sum_step(i, carry):
        @pl.when(i < CHUNKS)
        def _():
            sum_chunk(i)
            reduce0(i)

        @pl.when((i >= LAG) & (i < CHUNKS + LAG))
        def _():
            reduce1(i - LAG)

        @pl.when(i >= 2 * LAG)
        def _():
            reduce2(i - 2 * LAG)

        return carry

    lax.fori_loop(0, CHUNKS + 2 * LAG, sum_step, 0)

    for c in range(CHUNKS):
        wait(recv2.at[c, pl.ds(0, 7)], rs_recv.at[c])
        for j in range(lanes // 128):
            total = recv2[c, 0, :, pl.ds(j * 128, 128)].astype(F32)
            for q in range(1, 8):
                total += recv2[c, q, :, pl.ds(j * 128, 128)].astype(F32)
            for s in range(2):
                for r in range(2):
                    for g in range(GROUPS):
                        row = s * 8 + r * GROUPS + g
                        at = r * freqs + c * width + g * lanes + j * 128
                        out_ref[s, :, pl.ds(at, 128)] = total[row:row + 1, :]

    def drain(c, carry):
        wait(gath.at[c, pl.ds(0, n_dom - 1)], ag_send.at[c])
        wait(gath.at[c, pl.ds(0, 31)], rs_send.at[c])
        return carry

    lax.fori_loop(0, CHUNKS, drain, 0)


def per_device(n_dom, n_ori, particles, refs, inv_sigma2, offsets, owner_map, center):
    pcount, feat = particles.shape
    freqs = feat // 2
    shifts = offsets.shape[0]
    slots = 2 * n_dom
    lanes = freqs // (CHUNKS * GROUPS)
    vmem = pl.BlockSpec(memory_space=pltpu.VMEM)
    far = pl.BlockSpec(memory_space=pltpu.HBM)
    dma = pltpu.SemaphoreType.DMA
    sums, loglik = pl.pallas_call(
        functools.partial(em_kernel, n_dom, n_ori, shifts),
        out_shape=(
            jax.ShapeDtypeStruct((2, 1, feat), F32),
            jax.ShapeDtypeStruct((1, pcount), F32),
        ),
        in_specs=[far] * 6,
        out_specs=(vmem, vmem),
        scratch_shapes=[
            pltpu.VMEM((pcount, feat), BF16),
            pltpu.VMEM((feat, pcount), BF16),
            pltpu.VMEM((lanes // 128, 16 * CHUNKS, 128), F32),
            pltpu.VMEM((CHUNKS, 16, lanes), BF16),
            pltpu.VMEM((CHUNKS, n_dom, 16, lanes), BF16),
            pltpu.VMEM((2 * GROUPS, slots, lanes), F32),
            pltpu.VMEM((2, 256, 256), BF16),
            pltpu.VMEM((2, 256, 256), BF16),
            pltpu.VMEM((shifts, freqs), F32),
            pltpu.VMEM((shifts, freqs), F32),
            pltpu.VMEM((2, shifts * slots, 4 * lanes), BF16),
            pltpu.VMEM((shifts * slots, pcount), F32),
            pltpu.VMEM((2, shifts * slots, 4 * lanes), F32),
            pltpu.VMEM((slots, 128), F32),
            pltpu.VMEM((2, feat), BF16),
            pltpu.SMEM((2, shifts), jnp.int32),
            pltpu.VMEM((1, freqs), F32),
            pltpu.VMEM((1, slots), jnp.int32),
            pltpu.VMEM((1, pcount), jnp.int32),
            pltpu.VMEM((8, pcount), F32),
            pltpu.VMEM((n_ori, 8, pcount), F32),
            pltpu.VMEM((shifts * slots, pcount), BF16),
            pltpu.VMEM((CHUNKS, n_dom, 16, lanes), BF16),
            pltpu.VMEM((CHUNKS, 2, RING, 16, lanes), BF16),
            pltpu.VMEM((CHUNKS, 2, 8, 16, lanes), BF16),
            pltpu.VMEM((CHUNKS, 8, 16, lanes), BF16),
            pltpu.VMEM((CHUNKS, 8, 16, lanes), BF16),
            dma((CHUNKS,)),
            dma((5,)),
            dma((CHUNKS,)),
            dma((CHUNKS,)),
            dma((CHUNKS, 2, 2)),
            dma((CHUNKS, 2)),
            dma,
            dma,
            dma((CHUNKS,)),
            dma((CHUNKS, 2)),
            dma((CHUNKS, 2)),
            dma((CHUNKS, 2)),
            dma((CHUNKS,)),
        ],
        compiler_params=pltpu.CompilerParams(
            collective_id=0, has_side_effects=True, vmem_limit_bytes=56 * 1024 * 1024
        ),
        cost_estimate=pl.CostEstimate(
            flops=4 * shifts * slots * pcount * feat, bytes_accessed=2 * pcount * feat, transcendentals=0
        ),
    )(
        refs.reshape(2, feat), particles, inv_sigma2.reshape(1, freqs), offsets.T, owner_map.reshape(1, slots),
        center.reshape(1, pcount),
    )
    return sums, loglik.reshape(pcount)


def solution(mesh):
    return jax.shard_map(
        functools.partial(per_device, mesh.shape["dom"], mesh.shape["orient"]),
        mesh=mesh,
        in_specs=(P("dom", None), P("dom", "orient", None), P(), P(), P(), P("dom")),
        out_specs=(P("dom", "orient", None), P("dom")),
        check_vma=False,
    )
```

```python
import functools
import math

import jax
import jax.numpy as jnp
from jax import lax
from jax.experimental import pallas as pl
from jax.experimental.pallas import tpu as pltpu
from jax.sharding import PartitionSpec as P

BOX = 128
CHUNKS = 8
GROUPS = 4
PAIRS = CHUNKS // 2
LAG = CHUNKS // 4
RING = 4
NEG_FILL = -1e30
MESH = pl.DeviceIdType.MESH
BF16, F32 = jnp.bfloat16, jnp.float32


def unit_circle(phase):
    folded = ((phase + 64) & 127) - 64
    quarter = (folded + 16) >> 5
    x = (folded - quarter * 32).astype(F32) * (2.0 * math.pi / BOX)
    x2 = x * x
    sine = x * (1.0 + x2 * (-1 / 6 + x2 * (1 / 120 + x2 * (-1 / 5040 + x2 * (1 / 362880)))))
    cosine = 1.0 + x2 * (-0.5 + x2 * (1 / 24 + x2 * (-1 / 720 + x2 * (1 / 40320))))
    odd = (quarter & 1) == 1
    cos_sign = jnp.where(((quarter + 1) & 2) == 2, -1.0, 1.0)
    sin_sign = jnp.where((quarter & 2) == 2, -1.0, 1.0)
    return jnp.where(odd, sine, cosine) * cos_sign, jnp.where(odd, cosine, sine) * sin_sign


class Torus:
    def __init__(self):
        self.me = lax.axis_index("dom")
        self.y, self.x, self.z = self.me // 8, (self.me // 2) % 4, self.me % 2

    def axes(self, c, odd=None):
        odd = c % 2 if odd is None else odd
        return odd, self.y * (1 - odd) + self.x * odd, self.x * (1 - odd) + self.y * odd

    def peers(self):
        near = [device(0, self.y, self.x, 1 - self.z)]
        for by in (1, 2, 3):
            for z in (self.z, 1 - self.z):
                near.append(device(0, self.y, step(self.x, by), z))
                near.append(device(0, step(self.y, by), self.x, z))
        return near


def device(odd, v, u, z):
    return {"dom": ((v * (1 - odd) + u * odd) * 4 + u * (1 - odd) + v * odd) * 2 + z}


def step(a, by):
    return (a + by) % RING


def tile_row(odd, h, k):
    return pl.multiple_of((32 * h + 8 * k) * (1 - odd) + (16 * k + 8 * h) * odd, 8)


def greet(barrier, to):
    pl.semaphore_signal(barrier, inc=1, device_id=to, device_id_type=MESH)


def send(src, dst, send_sem, recv_sem, to):
    pltpu.make_async_remote_copy(
        src_ref=src, dst_ref=dst, send_sem=send_sem, recv_sem=recv_sem, device_id=to, device_id_type=MESH
    ).start()


def wait(ref, sem):
    pltpu.make_async_copy(ref, ref, sem).wait()


def fetch_particles(part_hbm, part, part_sem, freqs):
    width = freqs // CHUNKS
    for c in range(CHUNKS):
        for base in (0, freqs):
            cols = pl.ds(base + c * width, width)
            pltpu.make_async_copy(part_hbm.at[:, cols], part.at[:, cols], part_sem.at[c]).start()


def exchange(perm, perm_t):
    for odd, ref, inverse in ((0, perm, 0), (1, perm, 0), (0, perm_t, 1), (1, perm_t, 1)):
        there = lax.broadcasted_iota(jnp.int32, (256, 256), 0)
        here = lax.broadcasted_iota(jnp.int32, (256, 256), 1)
        out, src = (here, there) if inverse else (there, here)
        at, s, q = src >> 4, (src >> 3) & 1, src & 7
        if odd:
            row = ((at >> 1) & 3) * 8 + (at >> 3) * 4 + (at & 1) * 2 + s
        else:
            row = at * 2 + s
        ref[odd] = (out == q * 32 + row).astype(F32).astype(BF16)


def em_kernel(
    n_dom, n_ori, shifts,
    refs_hbm, part_hbm, inv_hbm, off_hbm, omap_hbm, center_hbm,
    recv2, loglik_ref,
    part, part_t, stage, mine, gath, rows, perm, perm_t, cos_tab, sin_tab, lhs_a, lhs_b, acc, prods_a, prods_b, power,
    refs_ref, off_ref, inv_ref, omap_ref, center_ref, stat_out, stat_in, by_class, sends, far_in, near_in, send2,
    part_sem, small_sem, ag_send, ag_recv, ag_near, ag_far, st_send, st_recv,
    rs_send, far_sem, early_sem, late_sem, rs_recv,
):
    freqs = inv_ref.shape[1]
    slots = 2 * n_dom
    lanes = mine.shape[2]
    width = freqs // CHUNKS
    half = RING
    here = Torus()
    axes, my_z = here.axes, here.z
    my_ori = lax.axis_index("orient")

    smalls = [
        pltpu.make_async_copy(src, dst, small_sem.at[k])
        for k, (src, dst) in enumerate((
            (refs_hbm, refs_ref), (off_hbm, off_ref), (inv_hbm, inv_ref), (omap_hbm, omap_ref), (center_hbm, center_ref)
        ))
    ]

    for copy in smalls:
        copy.start()

    barrier = pltpu.get_barrier_semaphore()
    peers = here.peers()
    for to in peers:
        greet(barrier, to)

    def greet_ori(i, carry):
        greet(barrier, {"orient": lax.rem(my_ori + i, n_ori)})
        return carry

    lax.fori_loop(1, n_ori, greet_ori, 0)
    fetch_particles(part_hbm, part, part_sem, freqs)
    smalls[0].wait()

    for c in range(CHUNKS):
        for r in range(2):
            for g in range(GROUPS):
                for j in range(lanes // 128):
                    at = r * freqs + c * width + g * lanes + j * 128
                    stage[j, pl.ds(c * 16 + r * GROUPS + g, 2, stride=8), :] = refs_ref[:, pl.ds(at, 128)].astype(F32)
        for j in range(lanes // 128):
            mine[c, :, pl.ds(j * 128, 128)] = stage[j, pl.ds(c * 16, 16), :].astype(BF16)

    pl.semaphore_wait(barrier, len(peers) + n_ori - 1)

    def gather0(c):
        odd, v, u = axes(c)
        home = u * 2 + my_z
        at = v * 8 + home

        def share(i, carry):
            q = (home + i) % 8
            send(mine.at[c], gath.at[c, at], ag_send.at[c], ag_recv.at[c], device(odd, v, q // 2, q % 2))
            return carry

        lax.fori_loop(1, 8, share, 0)
        gath[c, at] = mine[c]

    def gather1(c):
        odd, v, u = axes(c)
        wait(gath.at[c, pl.ds(0, 7)], ag_recv.at[c])
        for first in range(2):
            for k, by in ((0, 1), (1, 3)):
                h = k if first == 0 else 1 - k
                block = gath.at[c, pl.ds(v * 8 + h * half, half)]
                send(block, block, ag_send.at[c], ag_near.at[c, k, h], device(odd, step(v, by), u, my_z))

    def gather2(c):
        odd, v, u = axes(c)
        for k, by in ((0, 1), (1, 3)):
            block = gath.at[c, pl.ds(step(v, 4 - by) * 8 + k * half, half)]
            wait(block, ag_near.at[c, k, k])
            send(block, block, ag_send.at[c], ag_far.at[c, k], device(odd, step(v, by), u, my_z))

    def gather3(c):
        block = gath.at[c, pl.ds(0, half)]
        for k in range(2):
            wait(block, ag_near.at[c, k, 1 - k])
            wait(block, ag_far.at[c, k])

    def pair(k, stage):
        def one(i, carry):
            stage(2 * k + i)
            return carry

        lax.fori_loop(0, 2, one, 0)

    def turn_pair(k):
        for c in (2 * k, 2 * k + 1):
            wait(part.at[:, pl.ds(0, 2 * width)], part_sem.at[c])

        def turn(i, carry):
            at = pl.ds(pl.multiple_of(i // 4 * freqs + k * 2 * width + i % 4 * (width // 2), width // 2), width // 2)
            part_t[at, :] = part[:, at].T
            return carry

        lax.fori_loop(0, 8, turn, 0)

    pair(0, gather0)
    pair(1, gather0)
    exchange(perm, perm_t)
    smalls[1].wait()

    shift_ids = lax.broadcasted_iota(jnp.int32, (shifts, 128), 0)
    off_x = jnp.zeros((shifts, 128), jnp.int32)
    off_y = jnp.zeros((shifts, 128), jnp.int32)
    for t in range(shifts):
        off_x = jnp.where(shift_ids == t, off_ref[0, t], off_x)
        off_y = jnp.where(shift_ids == t, off_ref[1, t], off_y)

    def tables(j, carry):
        for h in range(4):
            at = pl.multiple_of(j * 512 + h * 128, 128)
            freq = lax.broadcasted_iota(jnp.int32, (shifts, 128), 1) + at
            fx = freq & (BOX // 2 - 1)
            fy = freq >> 6
            fy = jnp.where(fy < BOX // 2, fy, fy - BOX)
            cosine, sine = unit_circle(off_x * fx + off_y * fy)
            cos_tab[:, pl.ds(at, 128)] = cosine
            sin_tab[:, pl.ds(at, 128)] = sine
        return carry

    lax.fori_loop(0, freqs // 1024, tables, 0)
    pair(0, gather1)
    pair(2, gather0)
    lax.fori_loop(freqs // 1024, freqs // 512, tables, 0)
    pair(1, gather1)
    turn_pair(0)
    pair(0, gather2)
    pair(3, gather0)
    turn_pair(1)
    pair(2, gather1)
    for copy in smalls[2:]:
        copy.wait()
    acc[...] = jnp.zeros_like(acc)
    power[...] = jnp.zeros_like(power)
    lhs_b[...] = jnp.zeros_like(lhs_b)

    def columns(group):
        at = pl.multiple_of(group * lanes, lanes)
        return pl.ds(at, lanes), pl.ds(pl.multiple_of(freqs + at, lanes), lanes)

    def score_product(lhs, group):
        block = jnp.concatenate([part_t[at, :] for at in columns(group)], axis=0)
        acc[...] += jnp.dot(lhs[...], block, preferred_element_type=F32)

    def shift(lhs, c, g):
        for j in range(lanes // 128):
            there = pl.ds(pl.multiple_of((c * GROUPS + g) * lanes + j * 128, 128), 128)
            real = rows[g, :, pl.ds(j * 128, 128)]
            imag = rows[GROUPS + g, :, pl.ds(j * 128, 128)]
            inv = inv_ref[:, there]
            re = real * inv
            im = imag * inv
            power[...] += re * real + im * imag
            for t in range(shifts):
                cosine = cos_tab[pl.ds(t, 1), there]
                sine = sin_tab[pl.ds(t, 1), there]
                into = lhs.at[pl.ds(t * slots, slots)]
                into[:, pl.ds(j * 128, 128)] = (re * cosine + im * sine).astype(BF16)
                into[:, pl.ds(lanes + j * 128, 128)] = (im * cosine - re * sine).astype(BF16)

    def score_chunk(c, carry):
        odd = c % 2
        gather3(c)
        for h in range(2):
            spread = jnp.dot(
                perm[odd], gath[c, pl.ds(16 * h, 16)].reshape(256, lanes), preferred_element_type=F32
            )
            for q in range(8):
                for k in range(4):
                    rows[q, pl.ds(tile_row(odd, h, k), 8), :] = spread[q * 32 + k * 8:q * 32 + k * 8 + 8, :]

        def two_groups(i, carry):
            first = c * GROUPS + 2 * i
            score_product(lhs_b, jnp.maximum(first - 1, 0))
            shift(lhs_a, c, 2 * i)
            score_product(lhs_a, first)
            shift(lhs_b, c, 2 * i + 1)
            return carry

        lax.fori_loop(0, GROUPS // 2, two_groups, 0)

        for k in range(PAIRS - 1):
            @pl.when(c == 2 * k)
            def _():
                pair(k + 1, gather2)

        @pl.when(c == 1)
        def _():
            pair(PAIRS - 1, gather1)

        for k in range(2, PAIRS):
            @pl.when(c == 2 * k - 3)
            def _():
                turn_pair(k)

        return carry

    lax.fori_loop(0, CHUNKS, score_chunk, 0)
    score_product(lhs_b, CHUNKS * GROUPS - 1)

    power_col = 0.5 * jnp.sum(power[...], axis=1, keepdims=True)
    distance = jnp.abs(my_ori - center_ref[...])
    allowed = jnp.minimum(distance, n_ori - distance) <= n_ori // 4
    best = None
    for t in range(shifts):
        at = pl.ds(t * slots, slots)
        value = jnp.where(allowed, acc[at, :] - power_col, NEG_FILL)
        acc[at, :] = value
        top = jnp.max(value, axis=0, keepdims=True)
        best = top if best is None else jnp.maximum(best, top)
    total = jnp.zeros_like(best)
    for t in range(shifts):
        total += jnp.sum(jnp.exp(acc[pl.ds(t * slots, slots), :] - best), axis=0, keepdims=True)
    stat_out[0:1, :] = best
    stat_out[1:2, :] = total

    def stat_send(i, carry):
        send(stat_out, stat_in.at[my_ori], st_send, st_recv, {"orient": lax.rem(my_ori + i, n_ori)})
        return carry

    lax.fori_loop(1, n_ori, stat_send, 0)
    stat_in[my_ori] = stat_out[...]
    if n_ori > 1:
        others = stat_in.at[pl.ds(0, n_ori - 1)]
        wait(others, st_recv)
        wait(others, st_send)
    bests = [stat_in[o, 0:1, :] for o in range(n_ori)]
    best = functools.reduce(jnp.maximum, bests)
    total = sum(stat_in[o, 1:2, :] * jnp.exp(bests[o] - best) for o in range(n_ori))
    loglik_ref[...] = best + jnp.log(total)

    pick = (lax.broadcasted_iota(jnp.int32, (slots, slots), 0) == omap_ref[...]).astype(F32).astype(BF16)
    weights = jnp.concatenate(
        [(jnp.exp(acc[pl.ds(t * slots, slots), :] - best) / total).astype(BF16) for t in range(shifts)], axis=1
    )
    picked = lax.dot_general(pick, weights, (((0,), (0,)), ((), ())), preferred_element_type=F32).astype(BF16)
    pcount = acc.shape[1]
    for t in range(shifts):
        by_class[pl.ds(t * slots, slots), :] = picked[:, t * pcount:(t + 1) * pcount]

    def multiply(prods, group):
        block = jnp.concatenate([part[:, at] for at in columns(group)], axis=1)
        prods[...] = jnp.dot(by_class[...], block, preferred_element_type=F32)

    def rotate(prods, c, g):
        for j in range(lanes // 128):
            at = pl.ds(j * 128, 128)
            there = pl.ds(pl.multiple_of((c * GROUPS + g) * lanes + j * 128, 128), 128)
            out_real = out_imag = None
            for t in range(shifts):
                cosine = cos_tab[pl.ds(t, 1), there]
                sine = sin_tab[pl.ds(t, 1), there]
                re = prods[pl.ds(t * slots, slots), at]
                im = prods[pl.ds(t * slots, slots), pl.ds(lanes + j * 128, 128)]
                term_real = re * cosine - im * sine
                term_imag = im * cosine + re * sine
                out_real = term_real if t == 0 else out_real + term_real
                out_imag = term_imag if t == 0 else out_imag + term_imag
            rows[g, :, at] = out_real
            rows[GROUPS + g, :, at] = out_imag

    def sum_chunk(c):
        odd = c % 2

        def two_groups(i, carry):
            first = c * GROUPS + 2 * i
            multiply(prods_b, first + 1)
            rotate(prods_a, c, 2 * i)
            multiply(prods_a, jnp.minimum(first + 2, CHUNKS * GROUPS - 1))
            rotate(prods_b, c, 2 * i + 1)
            return carry

        lax.fori_loop(0, GROUPS // 2, two_groups, 0)
        for h in range(2):
            tiles = [rows[q, pl.ds(tile_row(odd, h, k), 8), :] for q in range(8) for k in range(4)]
            spread = jnp.dot(
                perm_t[odd], jnp.concatenate(tiles, axis=0).astype(BF16), preferred_element_type=F32
            ).astype(BF16)
            sends[c, pl.ds(16 * h, 16)] = spread.reshape(16, 16, lanes)

    def reduce0(c):
        odd, v, u = axes(c)
        for k, by in ((0, 1), (1, 3)):
            to = device(odd, step(v, by), u, my_z)
            send(sends.at[c, pl.ds(step(v, 2) * 8 + k * half, half)], far_in.at[c, k], rs_send.at[c], far_sem.at[c, k], to)
        for k, by in ((0, 1), (1, 3)):
            to = device(odd, step(v, by), u, my_z)
            other = (1 - k) * half
            send(
                sends.at[c, pl.ds(step(v, by) * 8 + other, half)], near_in.at[c, k, pl.ds(other, half)],
                rs_send.at[c], early_sem.at[c, k], to,
            )

    def reduce1(c):
        odd, v, u = axes(c)
        for k, by in ((0, 1), (1, 3)):
            wait(far_in.at[c, k], far_sem.at[c, k])
            at = step(v, by) * 8 + k * half

            def add(i, carry):
                sends[c, at + i] = (sends[c, at + i].astype(F32) + far_in[c, k, i].astype(F32)).astype(BF16)
                return carry

            lax.fori_loop(0, half, add, 0)
            send(
                sends.at[c, pl.ds(at, half)], near_in.at[c, k, pl.ds(k * half, half)], rs_send.at[c],
                late_sem.at[c, k], device(odd, step(v, by), u, my_z),
            )

    def reduce2(c):
        odd, v, u = axes(c)
        for k in range(2):
            wait(near_in.at[c, k, pl.ds((1 - k) * half, half)], early_sem.at[c, k])
            wait(near_in.at[c, k, pl.ds(k * half, half)], late_sem.at[c, k])

        def add(q, carry):
            send2[c, q] = (
                sends[c, v * 8 + q].astype(F32) + near_in[c, 0, q].astype(F32) + near_in[c, 1, q].astype(F32)
            ).astype(BF16)
            return carry

        lax.fori_loop(0, 8, add, 0)
        home = u * 2 + my_z

        def share(i, carry):
            q = (home + i) % 8
            send(send2.at[c, q], recv2.at[c, home], rs_send.at[c], rs_recv.at[c], device(odd, v, q // 2, q % 2))
            return carry

        lax.fori_loop(1, 8, share, 0)
        recv2[c, home] = send2[c, home]

    def progress(c):
        @pl.when((c >= LAG) & (c < CHUNKS + LAG))
        def _():
            reduce1(c - LAG)

        @pl.when(c >= 2 * LAG)
        def _():
            reduce2(c - 2 * LAG)

    def sum_step(c, carry):
        @pl.when(c < CHUNKS)
        def _():
            sum_chunk(c)
            reduce0(c)

        progress(c)
        return carry

    multiply(prods_a, 0)
    lax.fori_loop(0, CHUNKS + 2 * LAG, sum_step, 0)

    def drain(c, carry):
        wait(recv2.at[c, pl.ds(0, 7)], rs_recv.at[c])
        wait(gath.at[c, pl.ds(0, n_dom - 1)], ag_send.at[c])
        wait(sends.at[c, pl.ds(0, 31)], rs_send.at[c])
        return carry

    lax.fori_loop(0, CHUNKS, drain, 0)


def last_kernel(recv2, loglik_in, out_ref, loglik_ref):
    lanes = recv2.shape[3]
    freqs = CHUNKS * GROUPS * lanes
    loglik_ref[...] = loglik_in[...]
    for c in range(CHUNKS):
        for j in range(lanes // 128):
            total = recv2[c, 0, :, pl.ds(j * 128, 128)].astype(F32)
            for q in range(1, 8):
                total += recv2[c, q, :, pl.ds(j * 128, 128)].astype(F32)
            for s in range(2):
                for r in range(2):
                    for g in range(GROUPS):
                        row = s * 8 + r * GROUPS + g
                        at = r * freqs + c * GROUPS * lanes + g * lanes + j * 128
                        out_ref[s, :, pl.ds(at, 128)] = total[row:row + 1, :]


def per_device(n_dom, n_ori, particles, refs, inv_sigma2, offsets, owner_map, center):
    pcount, feat = particles.shape
    freqs = feat // 2
    shifts = offsets.shape[0]
    slots = 2 * n_dom
    lanes = freqs // (CHUNKS * GROUPS)
    vmem = pl.BlockSpec(memory_space=pltpu.VMEM)
    far = pl.BlockSpec(memory_space=pltpu.HBM)
    dma = pltpu.SemaphoreType.DMA
    grant = 56 * 1024 * 1024
    partial, loglik = pl.pallas_call(
        functools.partial(em_kernel, n_dom, n_ori, shifts),
        out_shape=(
            jax.ShapeDtypeStruct((CHUNKS, 8, 16, lanes), BF16),
            jax.ShapeDtypeStruct((1, pcount), F32),
        ),
        in_specs=[far] * 6,
        out_specs=(vmem, vmem),
        scratch_shapes=[
            pltpu.VMEM((pcount, feat), BF16),
            pltpu.VMEM((feat, pcount), BF16),
            pltpu.VMEM((lanes // 128, 16 * CHUNKS, 128), F32),
            pltpu.VMEM((CHUNKS, 16, lanes), BF16),
            pltpu.VMEM((CHUNKS, n_dom, 16, lanes), BF16),
            pltpu.VMEM((2 * GROUPS, slots, lanes), F32),
            pltpu.VMEM((2, 256, 256), BF16),
            pltpu.VMEM((2, 256, 256), BF16),
            pltpu.VMEM((shifts, freqs), F32),
            pltpu.VMEM((shifts, freqs), F32),
            pltpu.VMEM((shifts * slots, 2 * lanes), BF16),
            pltpu.VMEM((shifts * slots, 2 * lanes), BF16),
            pltpu.VMEM((shifts * slots, pcount), F32),
            pltpu.VMEM((shifts * slots, 2 * lanes), F32),
            pltpu.VMEM((shifts * slots, 2 * lanes), F32),
            pltpu.VMEM((slots, 128), F32),
            pltpu.VMEM((2, feat), BF16),
            pltpu.SMEM((2, shifts), jnp.int32),
            pltpu.VMEM((1, freqs), F32),
            pltpu.VMEM((1, slots), jnp.int32),
            pltpu.VMEM((1, pcount), jnp.int32),
            pltpu.VMEM((8, pcount), F32),
            pltpu.VMEM((n_ori, 8, pcount), F32),
            pltpu.VMEM((shifts * slots, pcount), BF16),
            pltpu.VMEM((CHUNKS, n_dom, 16, lanes), BF16),
            pltpu.VMEM((CHUNKS, 2, RING, 16, lanes), BF16),
            pltpu.VMEM((CHUNKS, 2, 8, 16, lanes), BF16),
            pltpu.VMEM((CHUNKS, 8, 16, lanes), BF16),
            dma((CHUNKS,)),
            dma((5,)),
            dma((CHUNKS,)),
            dma((CHUNKS,)),
            dma((CHUNKS, 2, 2)),
            dma((CHUNKS, 2)),
            dma,
            dma,
            dma((CHUNKS,)),
            dma((CHUNKS, 2)),
            dma((CHUNKS, 2)),
            dma((CHUNKS, 2)),
            dma((CHUNKS,)),
        ],
        compiler_params=pltpu.CompilerParams(collective_id=0, has_side_effects=True, vmem_limit_bytes=grant),
        cost_estimate=pl.CostEstimate(
            flops=4 * shifts * slots * pcount * feat, bytes_accessed=2 * pcount * feat, transcendentals=0
        ),
    )(
        refs.reshape(2, feat), particles, inv_sigma2.reshape(1, freqs), offsets.T, owner_map.reshape(1, slots),
        center.reshape(1, pcount),
    )
    sums, loglik = pl.pallas_call(
        last_kernel,
        out_shape=(jax.ShapeDtypeStruct((2, 1, feat), F32), jax.ShapeDtypeStruct((1, pcount), F32)),
        in_specs=[vmem, vmem],
        out_specs=(vmem, vmem),
        compiler_params=pltpu.CompilerParams(vmem_limit_bytes=grant),
    )(partial, loglik)
    return sums, loglik.reshape(pcount)


def solution(mesh):
    return jax.shard_map(
        functools.partial(per_device, mesh.shape["dom"], mesh.shape["orient"]),
        mesh=mesh,
        in_specs=(P("dom", None), P("dom", "orient", None), P(), P(), P(), P("dom")),
        out_specs=(P("dom", "orient", None), P("dom")),
        check_vma=False,
    )
```

```python
import functools
import math

import jax
import jax.numpy as jnp
from jax import lax
from jax.experimental import pallas as pl
from jax.experimental.pallas import tpu as pltpu
from jax.sharding import PartitionSpec as P

BOX = 128
CHUNKS = 8
GROUPS = 4
PAIRS = CHUNKS // 2
LAG = CHUNKS // 4
RING = 4
NEG_FILL = -1e30
MESH = pl.DeviceIdType.MESH
BF16, F32 = jnp.bfloat16, jnp.float32


def unit_circle(phase):
    folded = ((phase + 64) & 127) - 64
    quarter = (folded + 16) >> 5
    x = (folded - quarter * 32).astype(F32) * (2.0 * math.pi / BOX)
    x2 = x * x
    sine = x * (1.0 + x2 * (-1 / 6 + x2 * (1 / 120 + x2 * (-1 / 5040 + x2 * (1 / 362880)))))
    cosine = 1.0 + x2 * (-0.5 + x2 * (1 / 24 + x2 * (-1 / 720 + x2 * (1 / 40320))))
    odd = (quarter & 1) == 1
    cos_sign = jnp.where(((quarter + 1) & 2) == 2, -1.0, 1.0)
    sin_sign = jnp.where((quarter & 2) == 2, -1.0, 1.0)
    return jnp.where(odd, sine, cosine) * cos_sign, jnp.where(odd, cosine, sine) * sin_sign


class Torus:
    def __init__(self):
        self.me = lax.axis_index("dom")
        self.y, self.x, self.z = self.me // 8, (self.me // 2) % 4, self.me % 2

    def axes(self, c, odd=None):
        odd = c % 2 if odd is None else odd
        return odd, self.y * (1 - odd) + self.x * odd, self.x * (1 - odd) + self.y * odd

    def peers(self):
        near = [device(0, self.y, self.x, 1 - self.z)]
        for by in (1, 2, 3):
            for z in (self.z, 1 - self.z):
                near.append(device(0, self.y, step(self.x, by), z))
                near.append(device(0, step(self.y, by), self.x, z))
        return near


def device(odd, v, u, z):
    return {"dom": ((v * (1 - odd) + u * odd) * 4 + u * (1 - odd) + v * odd) * 2 + z}


def step(a, by):
    return (a + by) % RING


def greet(barrier, to):
    pl.semaphore_signal(barrier, inc=1, device_id=to, device_id_type=MESH)


def send(src, dst, send_sem, recv_sem, to):
    pltpu.make_async_remote_copy(
        src_ref=src, dst_ref=dst, send_sem=send_sem, recv_sem=recv_sem, device_id=to, device_id_type=MESH
    ).start()


def wait(ref, sem):
    pltpu.make_async_copy(ref, ref, sem).wait()


def fetch_particles(part_hbm, part, part_sem, freqs):
    width = freqs // CHUNKS
    for c in range(CHUNKS):
        for base in (0, freqs):
            cols = pl.ds(base + c * width, width)
            pltpu.make_async_copy(part_hbm.at[:, cols], part.at[:, cols], part_sem.at[c]).start()


def exchange(perm, perm_t):
    there = lax.broadcasted_iota(jnp.int32, (128, 128), 0)
    here = lax.broadcasted_iota(jnp.int32, (128, 128), 1)
    for ref, out, src in ((perm, there, here), (perm_t, here, there)):
        q, s, r = src >> 4, (src >> 3) & 1, src & 7
        ref[...] = (out == r * 16 + q * 2 + s).astype(F32).astype(BF16)


def em_kernel(
    n_dom, n_ori, shifts,
    refs_hbm, part_hbm, inv_hbm, off_hbm, omap_hbm, center_hbm,
    recv2, loglik_ref,
    part, part_t, stage, mine, pieces, gath, perm, perm_t, cos_tab, sin_tab, lhs_a, lhs_b, acc, prods_a, prods_b, power,
    refs_ref, off_ref, inv_ref, omap_ref, center_ref, stat_out, stat_in, by_class, sends, far_in, near_in, send2,
    part_sem, small_sem, ag_send, ag_recv, ring_send, ag_near, ag_far, st_send, st_recv,
    rs_send, share_send, far_sem, early_sem, late_sem, rs_recv,
):
    freqs = inv_ref.shape[1]
    slots = 2 * n_dom
    lanes = mine.shape[3]
    width = freqs // CHUNKS
    half = 4
    here = Torus()
    axes, my_z = here.axes, here.z
    my_ori = lax.axis_index("orient")

    smalls = [
        pltpu.make_async_copy(src, dst, small_sem.at[k])
        for k, (src, dst) in enumerate((
            (refs_hbm, refs_ref), (off_hbm, off_ref), (inv_hbm, inv_ref), (omap_hbm, omap_ref), (center_hbm, center_ref)
        ))
    ]

    for copy in smalls:
        copy.start()

    barrier = pltpu.get_barrier_semaphore()
    peers = here.peers()
    for to in peers:
        greet(barrier, to)

    def greet_ori(i, carry):
        greet(barrier, {"orient": lax.rem(my_ori + i, n_ori)})
        return carry

    lax.fori_loop(1, n_ori, greet_ori, 0)
    fetch_particles(part_hbm, part, part_sem, freqs)
    smalls[0].wait()

    for c in range(CHUNKS):
        for r in range(2):
            for g in range(GROUPS):
                for j in range(lanes // 128):
                    at = r * freqs + c * width + g * lanes + j * 128
                    stage[j, pl.ds(c * 16 + r * GROUPS + g, 2, stride=8), :] = refs_ref[:, pl.ds(at, 128)].astype(F32)
        for j in range(lanes // 128):
            mine[c % 2, c // 2, :, pl.ds(j * 128, 128)] = stage[j, pl.ds(c * 16, 16), :].astype(BF16)

    pl.semaphore_wait(barrier, len(peers) + n_ori - 1)

    batches = ((0, 1), (1, 1), (2, PAIRS - 2))

    def gather0(b):
        for odd in range(2):
            _, v, u = axes(0, odd)
            home = u * 2 + my_z
            ks = pl.ds(*batches[b])

            def share(i, carry):
                q = (home + i) % 8
                send(
                    mine.at[odd, ks], pieces.at[odd, home, ks], ag_send.at[b, odd], ag_recv.at[b, odd],
                    device(odd, v, q // 2, q % 2),
                )
                return carry

            lax.fori_loop(1, 8, share, 0)
            pieces[odd, home, ks] = mine[odd, ks]

    def gather0_wait(b):
        for odd in range(2):
            wait(pieces.at[odd, pl.ds(0, 7), pl.ds(*batches[b])], ag_recv.at[b, odd])

    def gather1(c):
        odd, v, u = axes(c)
        joined = jnp.dot(
            perm[...], pieces[odd, :, c // 2].reshape(128, lanes), preferred_element_type=F32
        ).astype(BF16)
        gath[c, v] = joined.reshape(8, 16, lanes)
        for first in range(2):
            for k, by in ((0, 1), (1, 3)):
                h = k if first == 0 else 1 - k
                block = gath.at[c, v, pl.ds(h * half, half)]
                send(block, block, ring_send.at[c], ag_near.at[c, k, h], device(odd, step(v, by), u, my_z))

    def gather2(c):
        odd, v, u = axes(c)
        for k, by in ((0, 1), (1, 3)):
            block = gath.at[c, step(v, 4 - by), pl.ds(k * half, half)]
            wait(block, ag_near.at[c, k, k])
            send(block, block, ring_send.at[c], ag_far.at[c, k], device(odd, step(v, by), u, my_z))

    def gather3(c):
        block = gath.at[c, 0, pl.ds(0, half)]
        for k in range(2):
            wait(block, ag_near.at[c, k, 1 - k])
            wait(block, ag_far.at[c, k])

    def pair(k, stage):
        def one(i, carry):
            stage(2 * k + i)
            return carry

        lax.fori_loop(0, 2, one, 0)

    def turn_pair(k):
        for c in (2 * k, 2 * k + 1):
            wait(part.at[:, pl.ds(0, 2 * width)], part_sem.at[c])

        def turn(i, carry):
            at = pl.ds(pl.multiple_of(i // 4 * freqs + k * 2 * width + i % 4 * (width // 2), width // 2), width // 2)
            part_t[at, :] = part[:, at].T
            return carry

        lax.fori_loop(0, 8, turn, 0)

    gather0(0)
    gather0(1)
    exchange(perm, perm_t)
    smalls[1].wait()

    shift_ids = lax.broadcasted_iota(jnp.int32, (shifts, 128), 0)
    off_x = jnp.zeros((shifts, 128), jnp.int32)
    off_y = jnp.zeros((shifts, 128), jnp.int32)
    for t in range(shifts):
        off_x = jnp.where(shift_ids == t, off_ref[0, t], off_x)
        off_y = jnp.where(shift_ids == t, off_ref[1, t], off_y)

    def tables(j, carry):
        for h in range(4):
            at = pl.multiple_of(j * 512 + h * 128, 128)
            freq = lax.broadcasted_iota(jnp.int32, (shifts, 128), 1) + at
            fx = freq & (BOX // 2 - 1)
            fy = freq >> 6
            fy = jnp.where(fy < BOX // 2, fy, fy - BOX)
            cosine, sine = unit_circle(off_x * fx + off_y * fy)
            cos_tab[:, pl.ds(at, 128)] = cosine
            sin_tab[:, pl.ds(at, 128)] = sine
        return carry

    lax.fori_loop(0, freqs // 1024, tables, 0)
    gather0_wait(0)
    pair(0, gather1)
    gather0(2)
    lax.fori_loop(freqs // 1024, freqs // 512, tables, 0)
    gather0_wait(1)
    pair(1, gather1)
    turn_pair(0)
    pair(0, gather2)
    turn_pair(1)
    gather0_wait(2)
    pair(2, gather1)
    for copy in smalls[2:]:
        copy.wait()
    acc[...] = jnp.zeros_like(acc)
    power[...] = jnp.zeros_like(power)
    lhs_b[...] = jnp.zeros_like(lhs_b)

    def columns(group):
        at = pl.multiple_of(group * lanes, lanes)
        return pl.ds(at, lanes), pl.ds(pl.multiple_of(freqs + at, lanes), lanes)

    def score_product(lhs, c, half_chunk):
        at = pl.multiple_of((2 * c + half_chunk) * 2 * lanes, 2 * lanes)
        block = jnp.concatenate(
            [part_t[pl.ds(at, 2 * lanes), :], part_t[pl.ds(pl.multiple_of(freqs + at, 2 * lanes), 2 * lanes), :]], axis=0
        )
        acc[c % 2] += jnp.dot(lhs[...], block, preferred_element_type=F32)

    def shift(lhs, c, g):
        for j in range(lanes // 128):
            at = pl.ds(j * 128, 128)
            col = g % 2 * lanes + j * 128
            there = pl.ds(pl.multiple_of((c * GROUPS + g) * lanes + j * 128, 128), 128)
            real = jnp.concatenate([gath[c, w, g, :, at] for w in range(RING)], axis=0).astype(F32)
            imag = jnp.concatenate([gath[c, w, GROUPS + g, :, at] for w in range(RING)], axis=0).astype(F32)
            inv = inv_ref[:, there]
            re = real * inv
            im = imag * inv
            power[c % 2] += re * real + im * imag
            for t in range(shifts):
                cosine = cos_tab[pl.ds(t, 1), there]
                sine = sin_tab[pl.ds(t, 1), there]
                into = lhs.at[pl.ds(t * slots, slots)]
                into[:, pl.ds(col, 128)] = (re * cosine + im * sine).astype(BF16)
                into[:, pl.ds(2 * lanes + col, 128)] = (im * cosine - re * sine).astype(BF16)

    def score_chunk(c, carry):
        gather3(c)
        score_product(lhs_b, jnp.maximum(c - 1, 0), 1)
        shift(lhs_a, c, 0)
        shift(lhs_a, c, 1)
        score_product(lhs_a, c, 0)
        shift(lhs_b, c, 2)
        shift(lhs_b, c, 3)

        for k in range(PAIRS - 1):
            @pl.when(c == 2 * k)
            def _():
                pair(k + 1, gather2)

        @pl.when(c == 1)
        def _():
            pair(PAIRS - 1, gather1)

        for k in range(2, PAIRS):
            @pl.when(c == 2 * k - 3)
            def _():
                turn_pair(k)

        return carry

    lax.fori_loop(0, CHUNKS, score_chunk, 0)
    score_product(lhs_b, CHUNKS - 1, 1)

    for base, ref in [(t * slots, acc) for t in range(shifts)] + [(0, power)]:
        for y in range(4):
            for x in range(4):
                ref[0, pl.ds(base + y * 16 + x * 4, 4), :] += ref[1, pl.ds(base + x * 16 + y * 4, 4), :]

    power_col = 0.5 * jnp.sum(power[0], axis=1, keepdims=True)
    distance = jnp.abs(my_ori - center_ref[...])
    allowed = jnp.minimum(distance, n_ori - distance) <= n_ori // 4
    best = None
    for t in range(shifts):
        at = pl.ds(t * slots, slots)
        value = jnp.where(allowed, acc[0, at, :] - power_col, NEG_FILL)
        acc[0, at, :] = value
        top = jnp.max(value, axis=0, keepdims=True)
        best = top if best is None else jnp.maximum(best, top)
    total = jnp.zeros_like(best)
    for t in range(shifts):
        at = pl.ds(t * slots, slots)
        value = jnp.exp(acc[0, at, :] - best)
        acc[0, at, :] = value
        total += jnp.sum(value, axis=0, keepdims=True)
    mine_best = best
    stat_out[0:1, :] = best
    stat_out[1:2, :] = total

    def stat_send(i, carry):
        send(stat_out, stat_in.at[my_ori], st_send, st_recv, {"orient": lax.rem(my_ori + i, n_ori)})
        return carry

    lax.fori_loop(1, n_ori, stat_send, 0)
    stat_in[my_ori] = stat_out[...]
    if n_ori > 1:
        others = stat_in.at[pl.ds(0, n_ori - 1)]
        wait(others, st_recv)
        wait(others, st_send)
    bests = [stat_in[o, 0:1, :] for o in range(n_ori)]
    best = functools.reduce(jnp.maximum, bests)
    total = sum(stat_in[o, 1:2, :] * jnp.exp(bests[o] - best) for o in range(n_ori))
    loglik_ref[...] = best + jnp.log(total)
    scale = jnp.exp(mine_best - best) / total

    pick = (lax.broadcasted_iota(jnp.int32, (slots, slots), 0) == omap_ref[...]).astype(F32).astype(BF16)
    weights = jnp.concatenate(
        [(acc[0, pl.ds(t * slots, slots), :] * scale).astype(BF16) for t in range(shifts)], axis=1
    )
    row = lax.broadcasted_iota(jnp.int32, (slots, slots), 1)
    swapped = ((row >> 2) & 3) * 16 + (row >> 4) * 4 + (row & 3)
    swap = (lax.broadcasted_iota(jnp.int32, (slots, slots), 0) == swapped).astype(F32).astype(BF16)
    picks = jnp.concatenate([pick, jnp.dot(pick, swap, preferred_element_type=F32).astype(BF16)], axis=1)
    picked = lax.dot_general(picks, weights, (((0,), (0,)), ((), ())), preferred_element_type=F32).astype(BF16)
    pcount = acc.shape[2]
    for odd in range(2):
        for t in range(shifts):
            by_class[odd, pl.ds(t * slots, slots), :] = picked[
                odd * slots:(odd + 1) * slots, t * pcount:(t + 1) * pcount
            ]

    def multiply(prods, group):
        block = jnp.concatenate([part[:, at] for at in columns(group)], axis=1)
        prods[...] = jnp.dot(by_class[group // GROUPS % 2], block, preferred_element_type=F32)

    def rotate(prods, c, g):
        for j in range(lanes // 128):
            at = pl.ds(j * 128, 128)
            there = pl.ds(pl.multiple_of((c * GROUPS + g) * lanes + j * 128, 128), 128)
            out_real = out_imag = None
            for t in range(shifts):
                cosine = cos_tab[pl.ds(t, 1), there]
                sine = sin_tab[pl.ds(t, 1), there]
                re = prods[pl.ds(t * slots, slots), at]
                im = prods[pl.ds(t * slots, slots), pl.ds(lanes + j * 128, 128)]
                term_real = re * cosine - im * sine
                term_imag = im * cosine + re * sine
                out_real = term_real if t == 0 else out_real + term_real
                out_imag = term_imag if t == 0 else out_imag + term_imag
            for w in range(RING):
                sends[c, w, g, :, at] = out_real[w * 16:(w + 1) * 16].astype(BF16)
                sends[c, w, GROUPS + g, :, at] = out_imag[w * 16:(w + 1) * 16].astype(BF16)

    def sum_chunk(c):
        def two_groups(i, carry):
            first = c * GROUPS + 2 * i
            multiply(prods_b, first + 1)
            rotate(prods_a, c, 2 * i)
            multiply(prods_a, jnp.minimum(first + 2, CHUNKS * GROUPS - 1))
            rotate(prods_b, c, 2 * i + 1)
            return carry

        lax.fori_loop(0, GROUPS // 2, two_groups, 0)

    def reduce0(c):
        odd, v, u = axes(c)
        for k, by in ((0, 1), (1, 3)):
            to = device(odd, step(v, by), u, my_z)
            send(sends.at[c, step(v, 2), pl.ds(k * half, half)], far_in.at[c, k], rs_send.at[c], far_sem.at[c, k], to)
        for k, by in ((0, 1), (1, 3)):
            to = device(odd, step(v, by), u, my_z)
            other = pl.ds((1 - k) * half, half)
            send(sends.at[c, step(v, by), other], near_in.at[c, k, other], rs_send.at[c], early_sem.at[c, k], to)

    def reduce1(c):
        odd, v, u = axes(c)
        for k, by in ((0, 1), (1, 3)):
            wait(far_in.at[c, k], far_sem.at[c, k])
            w, part_of = step(v, by), pl.ds(k * half, half)
            sends[c, w, part_of] = (sends[c, w, part_of].astype(F32) + far_in[c, k].astype(F32)).astype(BF16)
            send(
                sends.at[c, w, part_of], near_in.at[c, k, part_of], rs_send.at[c], late_sem.at[c, k],
                device(odd, w, u, my_z),
            )

    def reduce2(c):
        odd, v, u = axes(c)
        for k in range(2):
            wait(near_in.at[c, k, pl.ds((1 - k) * half, half)], early_sem.at[c, k])
            wait(near_in.at[c, k, pl.ds(k * half, half)], late_sem.at[c, k])
        total = sends[c, v].astype(F32) + near_in[c, 0].astype(F32) + near_in[c, 1].astype(F32)
        apart = jnp.dot(
            perm_t[...], total.astype(BF16).reshape(128, lanes), preferred_element_type=F32
        ).astype(BF16)
        send2[c] = apart.reshape(8, 16, lanes)
        home = u * 2 + my_z

        def share(i, carry):
            q = (home + i) % 8
            send(send2.at[c, q], recv2.at[c, home], share_send.at[c], rs_recv.at[c], device(odd, v, q // 2, q % 2))
            return carry

        lax.fori_loop(1, 8, share, 0)
        recv2[c, home] = send2[c, home]

    def progress(c):
        @pl.when((c >= LAG) & (c < CHUNKS + LAG))
        def _():
            reduce1(c - LAG)

        @pl.when(c >= 2 * LAG)
        def _():
            reduce2(c - 2 * LAG)

    def sum_step(c, carry):
        @pl.when(c < CHUNKS)
        def _():
            sum_chunk(c)
            reduce0(c)

        progress(c)
        return carry

    multiply(prods_a, 0)
    lax.fori_loop(0, CHUNKS + 2 * LAG, sum_step, 0)

    for b in range(3):
        for odd in range(2):
            wait(pieces.at[odd, pl.ds(0, 7), pl.ds(*batches[b])], ag_send.at[b, odd])

    def drain(c, carry):
        wait(recv2.at[c, pl.ds(0, 7)], rs_recv.at[c])
        wait(gath.at[c, pl.ds(0, 3)], ring_send.at[c])
        wait(sends.at[c, pl.ds(0, 3)], rs_send.at[c])
        wait(send2.at[c, pl.ds(0, 7)], share_send.at[c])
        return carry

    lax.fori_loop(0, CHUNKS, drain, 0)


def last_kernel(recv2, loglik_in, out_ref, loglik_ref):
    lanes = recv2.shape[3]
    freqs = CHUNKS * GROUPS * lanes
    loglik_ref[...] = loglik_in[...]
    for c in range(CHUNKS):
        for j in range(lanes // 128):
            total = recv2[c, 0, :, pl.ds(j * 128, 128)].astype(F32)
            for q in range(1, 8):
                total += recv2[c, q, :, pl.ds(j * 128, 128)].astype(F32)
            for s in range(2):
                for r in range(2):
                    for g in range(GROUPS):
                        row = s * 8 + r * GROUPS + g
                        at = r * freqs + c * GROUPS * lanes + g * lanes + j * 128
                        out_ref[s, :, pl.ds(at, 128)] = total[row:row + 1, :]


def per_device(n_dom, n_ori, particles, refs, inv_sigma2, offsets, owner_map, center):
    pcount, feat = particles.shape
    freqs = feat // 2
    shifts = offsets.shape[0]
    slots = 2 * n_dom
    lanes = freqs // (CHUNKS * GROUPS)
    vmem = pl.BlockSpec(memory_space=pltpu.VMEM)
    far = pl.BlockSpec(memory_space=pltpu.HBM)
    dma = pltpu.SemaphoreType.DMA
    grant = 56 * 1024 * 1024
    partial, loglik = pl.pallas_call(
        functools.partial(em_kernel, n_dom, n_ori, shifts),
        out_shape=(
            jax.ShapeDtypeStruct((CHUNKS, 8, 16, lanes), BF16),
            jax.ShapeDtypeStruct((1, pcount), F32),
        ),
        in_specs=[far] * 6,
        out_specs=(vmem, vmem),
        scratch_shapes=[
            pltpu.VMEM((pcount, feat), BF16),
            pltpu.VMEM((feat, pcount), BF16),
            pltpu.VMEM((lanes // 128, 16 * CHUNKS, 128), F32),
            pltpu.VMEM((2, PAIRS, 16, lanes), BF16),
            pltpu.VMEM((2, 8, PAIRS, 16, lanes), BF16),
            pltpu.VMEM((CHUNKS, RING, 8, 16, lanes), BF16),
            pltpu.VMEM((128, 128), BF16),
            pltpu.VMEM((128, 128), BF16),
            pltpu.VMEM((shifts, freqs), F32),
            pltpu.VMEM((shifts, freqs), F32),
            pltpu.VMEM((shifts * slots, 4 * lanes), BF16),
            pltpu.VMEM((shifts * slots, 4 * lanes), BF16),
            pltpu.VMEM((2, shifts * slots, pcount), F32),
            pltpu.VMEM((shifts * slots, 2 * lanes), F32),
            pltpu.VMEM((shifts * slots, 2 * lanes), F32),
            pltpu.VMEM((2, slots, 128), F32),
            pltpu.VMEM((2, feat), BF16),
            pltpu.SMEM((2, shifts), jnp.int32),
            pltpu.VMEM((1, freqs), F32),
            pltpu.VMEM((1, slots), jnp.int32),
            pltpu.VMEM((1, pcount), jnp.int32),
            pltpu.VMEM((2, pcount), F32),
            pltpu.VMEM((n_ori, 2, pcount), F32),
            pltpu.VMEM((2, shifts * slots, pcount), BF16),
            pltpu.VMEM((CHUNKS, RING, 8, 16, lanes), BF16),
            pltpu.VMEM((CHUNKS, 2, 4, 16, lanes), BF16),
            pltpu.VMEM((CHUNKS, 2, 8, 16, lanes), BF16),
            pltpu.VMEM((CHUNKS, 8, 16, lanes), BF16),
            dma((CHUNKS,)),
            dma((5,)),
            dma((3, 2)),
            dma((3, 2)),
            dma((CHUNKS,)),
            dma((CHUNKS, 2, 2)),
            dma((CHUNKS, 2)),
            dma,
            dma,
            dma((CHUNKS,)),
            dma((CHUNKS,)),
            dma((CHUNKS, 2)),
            dma((CHUNKS, 2)),
            dma((CHUNKS, 2)),
            dma((CHUNKS,)),
        ],
        compiler_params=pltpu.CompilerParams(collective_id=0, has_side_effects=True, vmem_limit_bytes=grant),
        cost_estimate=pl.CostEstimate(
            flops=4 * shifts * slots * pcount * feat, bytes_accessed=2 * pcount * feat, transcendentals=0
        ),
    )(
        refs.reshape(2, feat), particles, inv_sigma2.reshape(1, freqs), offsets.T, owner_map.reshape(1, slots),
        center.reshape(1, pcount),
    )
    sums, loglik = pl.pallas_call(
        last_kernel,
        out_shape=(jax.ShapeDtypeStruct((2, 1, feat), F32), jax.ShapeDtypeStruct((1, pcount), F32)),
        in_specs=[vmem, vmem],
        out_specs=(vmem, vmem),
        compiler_params=pltpu.CompilerParams(vmem_limit_bytes=grant),
    )(partial, loglik)
    return sums, loglik.reshape(pcount)


def solution(mesh):
    return jax.shard_map(
        functools.partial(per_device, mesh.shape["dom"], mesh.shape["orient"]),
        mesh=mesh,
        in_specs=(P("dom", None), P("dom", "orient", None), P(), P(), P(), P("dom")),
        out_specs=(P("dom", "orient", None), P("dom")),
        check_vma=False,
    )
```

```python
import functools
import math

import jax
import jax.numpy as jnp
from jax import lax
from jax.experimental import pallas as pl
from jax.experimental.pallas import tpu as pltpu
from jax.sharding import PartitionSpec as P

BOX = 128
CHUNKS = 4
GROUPS = 4
PAIRS = CHUNKS // 2
LAG = CHUNKS // 4
RING = 4
NEG_FILL = -1e30
MESH = pl.DeviceIdType.MESH
BF16, F32 = jnp.bfloat16, jnp.float32


def unit_circle(phase):
    folded = ((phase + 64) & 127) - 64
    quarter = (folded + 16) >> 5
    x = (folded - quarter * 32).astype(F32) * (2.0 * math.pi / BOX)
    x2 = x * x
    sine = x * (1.0 + x2 * (-1 / 6 + x2 * (1 / 120 + x2 * (-1 / 5040 + x2 * (1 / 362880)))))
    cosine = 1.0 + x2 * (-0.5 + x2 * (1 / 24 + x2 * (-1 / 720 + x2 * (1 / 40320))))
    odd = (quarter & 1) == 1
    cos_sign = jnp.where(((quarter + 1) & 2) == 2, -1.0, 1.0)
    sin_sign = jnp.where((quarter & 2) == 2, -1.0, 1.0)
    return jnp.where(odd, sine, cosine) * cos_sign, jnp.where(odd, cosine, sine) * sin_sign


class Torus:
    def __init__(self):
        self.me = lax.axis_index("dom")
        self.y, self.x, self.z = self.me // 8, (self.me // 2) % 4, self.me % 2

    def axes(self, c, odd=None):
        odd = c % 2 if odd is None else odd
        return odd, self.y * (1 - odd) + self.x * odd, self.x * (1 - odd) + self.y * odd

    def peers(self):
        near = [device(0, self.y, self.x, 1 - self.z)]
        for by in (1, 2, 3):
            for z in (self.z, 1 - self.z):
                near.append(device(0, self.y, step(self.x, by), z))
                near.append(device(0, step(self.y, by), self.x, z))
        return near


def device(odd, v, u, z):
    return {"dom": ((v * (1 - odd) + u * odd) * 4 + u * (1 - odd) + v * odd) * 2 + z}


def step(a, by):
    return (a + by) % RING


def greet(barrier, to):
    pl.semaphore_signal(barrier, inc=1, device_id=to, device_id_type=MESH)


def send(src, dst, send_sem, recv_sem, to):
    pltpu.make_async_remote_copy(
        src_ref=src, dst_ref=dst, send_sem=send_sem, recv_sem=recv_sem, device_id=to, device_id_type=MESH
    ).start()


def wait(ref, sem):
    pltpu.make_async_copy(ref, ref, sem).wait()


def fetch_particles(part_hbm, part, part_sem, freqs):
    width = freqs // CHUNKS
    for c in range(CHUNKS):
        for base in (0, freqs):
            cols = pl.ds(base + c * width, width)
            pltpu.make_async_copy(part_hbm.at[:, cols], part.at[:, cols], part_sem.at[c]).start()


def exchange(perm, perm_t):
    there = lax.broadcasted_iota(jnp.int32, (128, 128), 0)
    here = lax.broadcasted_iota(jnp.int32, (128, 128), 1)
    for ref, out, src in ((perm, there, here), (perm_t, here, there)):
        q, s, r = src >> 4, (src >> 3) & 1, src & 7
        ref[...] = (out == r * 16 + q * 2 + s).astype(F32).astype(BF16)


def em_kernel(
    n_dom, n_ori, shifts,
    refs_hbm, part_hbm, inv_hbm, off_hbm, omap_hbm, center_hbm,
    recv2, loglik_ref,
    part, part_t, stage, mine, pieces, gath, perm, perm_t, cos_tab, sin_tab, lhs_a, lhs_b, acc, prods_a, prods_b, power,
    refs_ref, off_ref, inv_ref, omap_ref, center_ref, stat_out, stat_in, by_class, sends, far_in, near_in, send2,
    part_sem, small_sem, ag_send, ag_recv, ring_send, ag_near, ag_far, st_send, st_recv,
    rs_send, share_send, far_sem, early_sem, late_sem, rs_recv,
):
    freqs = inv_ref.shape[1]
    slots = 2 * n_dom
    lanes = mine.shape[3]
    width = freqs // CHUNKS
    half = 4
    here = Torus()
    axes, my_z = here.axes, here.z
    my_ori = lax.axis_index("orient")

    smalls = [
        pltpu.make_async_copy(src, dst, small_sem.at[k])
        for k, (src, dst) in enumerate((
            (refs_hbm, refs_ref), (off_hbm, off_ref), (inv_hbm, inv_ref), (omap_hbm, omap_ref), (center_hbm, center_ref)
        ))
    ]

    for copy in smalls:
        copy.start()

    barrier = pltpu.get_barrier_semaphore()
    peers = here.peers()
    for to in peers:
        greet(barrier, to)

    def greet_ori(i, carry):
        greet(barrier, {"orient": lax.rem(my_ori + i, n_ori)})
        return carry

    lax.fori_loop(1, n_ori, greet_ori, 0)
    fetch_particles(part_hbm, part, part_sem, freqs)
    smalls[0].wait()

    for c in range(CHUNKS):
        for r in range(2):
            for g in range(GROUPS):
                for j in range(lanes // 128):
                    at = r * freqs + c * width + g * lanes + j * 128
                    stage[j, pl.ds(c * 16 + r * GROUPS + g, 2, stride=8), :] = refs_ref[:, pl.ds(at, 128)].astype(F32)
        for j in range(lanes // 128):
            mine[c % 2, c // 2, :, pl.ds(j * 128, 128)] = stage[j, pl.ds(c * 16, 16), :].astype(BF16)

    pl.semaphore_wait(barrier, len(peers) + n_ori - 1)

    batches = ((0, 1), (1, 1))

    def gather0(b):
        for odd in range(2):
            _, v, u = axes(0, odd)
            home = u * 2 + my_z
            ks = pl.ds(*batches[b])

            def share(i, carry):
                q = (home + i) % 8
                send(
                    mine.at[odd, ks], pieces.at[odd, home, ks], ag_send.at[b, odd], ag_recv.at[b, odd],
                    device(odd, v, q // 2, q % 2),
                )
                return carry

            lax.fori_loop(1, 8, share, 0)
            pieces[odd, home, ks] = mine[odd, ks]

    def gather0_wait(b):
        for odd in range(2):
            wait(pieces.at[odd, pl.ds(0, 7), pl.ds(*batches[b])], ag_recv.at[b, odd])

    def gather1(c):
        odd, v, u = axes(c)
        joined = jnp.dot(
            perm[...], pieces[odd, :, c // 2].reshape(128, lanes), preferred_element_type=F32
        ).astype(BF16)
        gath[c, v] = joined.reshape(8, 16, lanes)
        for first in range(2):
            for k, by in ((0, 1), (1, 3)):
                h = k if first == 0 else 1 - k
                block = gath.at[c, v, pl.ds(h * half, half)]
                send(block, block, ring_send.at[c], ag_near.at[c, k, h], device(odd, step(v, by), u, my_z))

    def gather2(c):
        odd, v, u = axes(c)
        for k, by in ((0, 1), (1, 3)):
            block = gath.at[c, step(v, 4 - by), pl.ds(k * half, half)]
            wait(block, ag_near.at[c, k, k])
            send(block, block, ring_send.at[c], ag_far.at[c, k], device(odd, step(v, by), u, my_z))

    def gather3(c):
        block = gath.at[c, 0, pl.ds(0, half)]
        for k in range(2):
            wait(block, ag_near.at[c, k, 1 - k])
            wait(block, ag_far.at[c, k])

    def pair(k, stage):
        def one(i, carry):
            stage(2 * k + i)
            return carry

        lax.fori_loop(0, 2, one, 0)

    def turn_pair(k):
        for c in (2 * k, 2 * k + 1):
            wait(part.at[:, pl.ds(0, 2 * width)], part_sem.at[c])

        def turn(i, carry):
            at = pl.ds(pl.multiple_of(i // 4 * freqs + k * 2 * width + i % 4 * (width // 2), width // 2), width // 2)
            part_t[at, :] = part[:, at].T
            return carry

        lax.fori_loop(0, 8, turn, 0)

    gather0(0)
    gather0(1)
    exchange(perm, perm_t)
    smalls[1].wait()

    shift_ids = lax.broadcasted_iota(jnp.int32, (shifts, 128), 0)
    off_x = jnp.zeros((shifts, 128), jnp.int32)
    off_y = jnp.zeros((shifts, 128), jnp.int32)
    for t in range(shifts):
        off_x = jnp.where(shift_ids == t, off_ref[0, t], off_x)
        off_y = jnp.where(shift_ids == t, off_ref[1, t], off_y)

    def tables(j, carry):
        for h in range(4):
            at = pl.multiple_of(j * 512 + h * 128, 128)
            freq = lax.broadcasted_iota(jnp.int32, (shifts, 128), 1) + at
            fx = freq & (BOX // 2 - 1)
            fy = freq >> 6
            fy = jnp.where(fy < BOX // 2, fy, fy - BOX)
            cosine, sine = unit_circle(off_x * fx + off_y * fy)
            cos_tab[:, pl.ds(at, 128)] = cosine
            sin_tab[:, pl.ds(at, 128)] = sine
        return carry

    lax.fori_loop(0, freqs // 1024, tables, 0)
    gather0_wait(0)
    pair(0, gather1)
    lax.fori_loop(freqs // 1024, freqs // 512, tables, 0)
    gather0_wait(1)
    pair(1, gather1)
    turn_pair(0)
    pair(0, gather2)
    turn_pair(1)
    for copy in smalls[2:]:
        copy.wait()
    acc[...] = jnp.zeros_like(acc)
    power[...] = jnp.zeros_like(power)
    lhs_b[...] = jnp.zeros_like(lhs_b)

    def columns(group):
        at = pl.multiple_of(group * lanes, lanes)
        return pl.ds(at, lanes), pl.ds(pl.multiple_of(freqs + at, lanes), lanes)

    def score_product(lhs, c, half_chunk):
        at = pl.multiple_of((2 * c + half_chunk) * 2 * lanes, 2 * lanes)
        block = jnp.concatenate(
            [part_t[pl.ds(at, 2 * lanes), :], part_t[pl.ds(pl.multiple_of(freqs + at, 2 * lanes), 2 * lanes), :]], axis=0
        )
        acc[c % 2] += jnp.dot(lhs[...], block, preferred_element_type=F32)

    def shift(lhs, c, g):
        for j in range(lanes // 128):
            at = pl.ds(j * 128, 128)
            col = g % 2 * lanes + j * 128
            there = pl.ds(pl.multiple_of((c * GROUPS + g) * lanes + j * 128, 128), 128)
            real = jnp.concatenate([gath[c, w, g, :, at] for w in range(RING)], axis=0).astype(F32)
            imag = jnp.concatenate([gath[c, w, GROUPS + g, :, at] for w in range(RING)], axis=0).astype(F32)
            inv = inv_ref[:, there]
            re = real * inv
            im = imag * inv
            power[c % 2] += re * real + im * imag
            for t in range(shifts):
                cosine = cos_tab[pl.ds(t, 1), there]
                sine = sin_tab[pl.ds(t, 1), there]
                into = lhs.at[pl.ds(t * slots, slots)]
                into[:, pl.ds(col, 128)] = (re * cosine + im * sine).astype(BF16)
                into[:, pl.ds(2 * lanes + col, 128)] = (im * cosine - re * sine).astype(BF16)

    def score_chunk(c, carry):
        gather3(c)
        score_product(lhs_b, jnp.maximum(c - 1, 0), 1)
        shift(lhs_a, c, 0)
        shift(lhs_a, c, 1)
        score_product(lhs_a, c, 0)
        shift(lhs_b, c, 2)
        shift(lhs_b, c, 3)

        @pl.when(c == 0)
        def _():
            pair(1, gather2)

        return carry

    lax.fori_loop(0, CHUNKS, score_chunk, 0)
    score_product(lhs_b, CHUNKS - 1, 1)

    for base, ref in [(t * slots, acc) for t in range(shifts)] + [(0, power)]:
        for y in range(4):
            for x in range(4):
                ref[0, pl.ds(base + y * 16 + x * 4, 4), :] += ref[1, pl.ds(base + x * 16 + y * 4, 4), :]

    power_col = 0.5 * jnp.sum(power[0], axis=1, keepdims=True)
    distance = jnp.abs(my_ori - center_ref[...])
    allowed = jnp.minimum(distance, n_ori - distance) <= n_ori // 4
    best = None
    for t in range(shifts):
        at = pl.ds(t * slots, slots)
        value = jnp.where(allowed, acc[0, at, :] - power_col, NEG_FILL)
        acc[0, at, :] = value
        top = jnp.max(value, axis=0, keepdims=True)
        best = top if best is None else jnp.maximum(best, top)
    total = jnp.zeros_like(best)
    for t in range(shifts):
        at = pl.ds(t * slots, slots)
        value = jnp.exp(acc[0, at, :] - best)
        acc[0, at, :] = value
        total += jnp.sum(value, axis=0, keepdims=True)
    mine_best = best
    stat_out[0:1, :] = best
    stat_out[1:2, :] = total

    def stat_send(i, carry):
        send(stat_out, stat_in.at[my_ori], st_send, st_recv, {"orient": lax.rem(my_ori + i, n_ori)})
        return carry

    lax.fori_loop(1, n_ori, stat_send, 0)
    stat_in[my_ori] = stat_out[...]
    if n_ori > 1:
        others = stat_in.at[pl.ds(0, n_ori - 1)]
        wait(others, st_recv)
        wait(others, st_send)
    bests = [stat_in[o, 0:1, :] for o in range(n_ori)]
    best = functools.reduce(jnp.maximum, bests)
    total = sum(stat_in[o, 1:2, :] * jnp.exp(bests[o] - best) for o in range(n_ori))
    loglik_ref[...] = best + jnp.log(total)
    scale = jnp.exp(mine_best - best) / total

    pick = (lax.broadcasted_iota(jnp.int32, (slots, slots), 0) == omap_ref[...]).astype(F32).astype(BF16)
    weights = jnp.concatenate(
        [(acc[0, pl.ds(t * slots, slots), :] * scale).astype(BF16) for t in range(shifts)], axis=1
    )
    row = lax.broadcasted_iota(jnp.int32, (slots, slots), 1)
    swapped = ((row >> 2) & 3) * 16 + (row >> 4) * 4 + (row & 3)
    swap = (lax.broadcasted_iota(jnp.int32, (slots, slots), 0) == swapped).astype(F32).astype(BF16)
    picks = jnp.concatenate([pick, jnp.dot(pick, swap, preferred_element_type=F32).astype(BF16)], axis=1)
    picked = lax.dot_general(picks, weights, (((0,), (0,)), ((), ())), preferred_element_type=F32).astype(BF16)
    pcount = acc.shape[2]
    for odd in range(2):
        for t in range(shifts):
            by_class[odd, pl.ds(t * slots, slots), :] = picked[
                odd * slots:(odd + 1) * slots, t * pcount:(t + 1) * pcount
            ]

    def multiply(prods, group):
        block = jnp.concatenate([part[:, at] for at in columns(group)], axis=1)
        prods[...] = jnp.dot(by_class[group // GROUPS % 2], block, preferred_element_type=F32)

    def rotate(prods, c, g):
        for j in range(lanes // 128):
            at = pl.ds(j * 128, 128)
            there = pl.ds(pl.multiple_of((c * GROUPS + g) * lanes + j * 128, 128), 128)
            out_real = out_imag = None
            for t in range(shifts):
                cosine = cos_tab[pl.ds(t, 1), there]
                sine = sin_tab[pl.ds(t, 1), there]
                re = prods[pl.ds(t * slots, slots), at]
                im = prods[pl.ds(t * slots, slots), pl.ds(lanes + j * 128, 128)]
                term_real = re * cosine - im * sine
                term_imag = im * cosine + re * sine
                out_real = term_real if t == 0 else out_real + term_real
                out_imag = term_imag if t == 0 else out_imag + term_imag
            for w in range(RING):
                sends[c, w, g, :, at] = out_real[w * 16:(w + 1) * 16].astype(BF16)
                sends[c, w, GROUPS + g, :, at] = out_imag[w * 16:(w + 1) * 16].astype(BF16)

    def sum_chunk(c):
        def two_groups(i, carry):
            first = c * GROUPS + 2 * i
            multiply(prods_b, first + 1)
            rotate(prods_a, c, 2 * i)
            multiply(prods_a, jnp.minimum(first + 2, CHUNKS * GROUPS - 1))
            rotate(prods_b, c, 2 * i + 1)
            return carry

        lax.fori_loop(0, GROUPS // 2, two_groups, 0)

    def reduce0(c):
        odd, v, u = axes(c)
        for k, by in ((0, 1), (1, 3)):
            to = device(odd, step(v, by), u, my_z)
            send(sends.at[c, step(v, 2), pl.ds(k * half, half)], far_in.at[c, k], rs_send.at[c], far_sem.at[c, k], to)
        for k, by in ((0, 1), (1, 3)):
            to = device(odd, step(v, by), u, my_z)
            other = pl.ds((1 - k) * half, half)
            send(sends.at[c, step(v, by), other], near_in.at[c, k, other], rs_send.at[c], early_sem.at[c, k], to)

    def reduce1(c):
        odd, v, u = axes(c)
        for k, by in ((0, 1), (1, 3)):
            wait(far_in.at[c, k], far_sem.at[c, k])
            w, part_of = step(v, by), pl.ds(k * half, half)
            sends[c, w, part_of] = (sends[c, w, part_of].astype(F32) + far_in[c, k].astype(F32)).astype(BF16)
            send(
                sends.at[c, w, part_of], near_in.at[c, k, part_of], rs_send.at[c], late_sem.at[c, k],
                device(odd, w, u, my_z),
            )

    def reduce2(c):
        odd, v, u = axes(c)
        for k in range(2):
            wait(near_in.at[c, k, pl.ds((1 - k) * half, half)], early_sem.at[c, k])
            wait(near_in.at[c, k, pl.ds(k * half, half)], late_sem.at[c, k])
        total = sends[c, v].astype(F32) + near_in[c, 0].astype(F32) + near_in[c, 1].astype(F32)
        apart = jnp.dot(
            perm_t[...], total.astype(BF16).reshape(128, lanes), preferred_element_type=F32
        ).astype(BF16)
        send2[c] = apart.reshape(8, 16, lanes)
        home = u * 2 + my_z

        def share(i, carry):
            q = (home + i) % 8
            send(send2.at[c, q], recv2.at[c, home], share_send.at[c], rs_recv.at[c], device(odd, v, q // 2, q % 2))
            return carry

        lax.fori_loop(1, 8, share, 0)
        recv2[c, home] = send2[c, home]

    def progress(c):
        @pl.when((c >= LAG) & (c < CHUNKS + LAG))
        def _():
            reduce1(c - LAG)

        @pl.when(c >= 2 * LAG)
        def _():
            reduce2(c - 2 * LAG)

    def sum_step(c, carry):
        @pl.when(c < CHUNKS)
        def _():
            sum_chunk(c)
            reduce0(c)

        progress(c)
        return carry

    multiply(prods_a, 0)
    lax.fori_loop(0, CHUNKS + 2 * LAG, sum_step, 0)

    for b in range(2):
        for odd in range(2):
            wait(pieces.at[odd, pl.ds(0, 7), pl.ds(*batches[b])], ag_send.at[b, odd])

    def drain(c, carry):
        wait(recv2.at[c, pl.ds(0, 7)], rs_recv.at[c])
        wait(gath.at[c, pl.ds(0, 3)], ring_send.at[c])
        wait(sends.at[c, pl.ds(0, 3)], rs_send.at[c])
        wait(send2.at[c, pl.ds(0, 7)], share_send.at[c])
        return carry

    lax.fori_loop(0, CHUNKS, drain, 0)


def last_kernel(recv2, loglik_in, out_ref, loglik_ref):
    lanes = recv2.shape[3]
    freqs = CHUNKS * GROUPS * lanes
    loglik_ref[...] = loglik_in[...]
    for c in range(CHUNKS):
        for j in range(lanes // 128):
            total = recv2[c, 0, :, pl.ds(j * 128, 128)].astype(F32)
            for q in range(1, 8):
                total += recv2[c, q, :, pl.ds(j * 128, 128)].astype(F32)
            for s in range(2):
                for r in range(2):
                    for g in range(GROUPS):
                        row = s * 8 + r * GROUPS + g
                        at = r * freqs + c * GROUPS * lanes + g * lanes + j * 128
                        out_ref[s, :, pl.ds(at, 128)] = total[row:row + 1, :]


def per_device(n_dom, n_ori, particles, refs, inv_sigma2, offsets, owner_map, center):
    pcount, feat = particles.shape
    freqs = feat // 2
    shifts = offsets.shape[0]
    slots = 2 * n_dom
    lanes = freqs // (CHUNKS * GROUPS)
    vmem = pl.BlockSpec(memory_space=pltpu.VMEM)
    far = pl.BlockSpec(memory_space=pltpu.HBM)
    dma = pltpu.SemaphoreType.DMA
    grant = 56 * 1024 * 1024
    partial, loglik = pl.pallas_call(
        functools.partial(em_kernel, n_dom, n_ori, shifts),
        out_shape=(
            jax.ShapeDtypeStruct((CHUNKS, 8, 16, lanes), BF16),
            jax.ShapeDtypeStruct((1, pcount), F32),
        ),
        in_specs=[far] * 6,
        out_specs=(vmem, vmem),
        scratch_shapes=[
            pltpu.VMEM((pcount, feat), BF16),
            pltpu.VMEM((feat, pcount), BF16),
            pltpu.VMEM((lanes // 128, 16 * CHUNKS, 128), F32),
            pltpu.VMEM((2, PAIRS, 16, lanes), BF16),
            pltpu.VMEM((2, 8, PAIRS, 16, lanes), BF16),
            pltpu.VMEM((CHUNKS, RING, 8, 16, lanes), BF16),
            pltpu.VMEM((128, 128), BF16),
            pltpu.VMEM((128, 128), BF16),
            pltpu.VMEM((shifts, freqs), F32),
            pltpu.VMEM((shifts, freqs), F32),
            pltpu.VMEM((shifts * slots, 4 * lanes), BF16),
            pltpu.VMEM((shifts * slots, 4 * lanes), BF16),
            pltpu.VMEM((2, shifts * slots, pcount), F32),
            pltpu.VMEM((shifts * slots, 2 * lanes), F32),
            pltpu.VMEM((shifts * slots, 2 * lanes), F32),
            pltpu.VMEM((2, slots, 128), F32),
            pltpu.VMEM((2, feat), BF16),
            pltpu.SMEM((2, shifts), jnp.int32),
            pltpu.VMEM((1, freqs), F32),
            pltpu.VMEM((1, slots), jnp.int32),
            pltpu.VMEM((1, pcount), jnp.int32),
            pltpu.VMEM((2, pcount), F32),
            pltpu.VMEM((n_ori, 2, pcount), F32),
            pltpu.VMEM((2, shifts * slots, pcount), BF16),
            pltpu.VMEM((CHUNKS, RING, 8, 16, lanes), BF16),
            pltpu.VMEM((CHUNKS, 2, 4, 16, lanes), BF16),
            pltpu.VMEM((CHUNKS, 2, 8, 16, lanes), BF16),
            pltpu.VMEM((CHUNKS, 8, 16, lanes), BF16),
            dma((CHUNKS,)),
            dma((5,)),
            dma((2, 2)),
            dma((2, 2)),
            dma((CHUNKS,)),
            dma((CHUNKS, 2, 2)),
            dma((CHUNKS, 2)),
            dma,
            dma,
            dma((CHUNKS,)),
            dma((CHUNKS,)),
            dma((CHUNKS, 2)),
            dma((CHUNKS, 2)),
            dma((CHUNKS, 2)),
            dma((CHUNKS,)),
        ],
        compiler_params=pltpu.CompilerParams(collective_id=0, has_side_effects=True, vmem_limit_bytes=grant),
        cost_estimate=pl.CostEstimate(
            flops=4 * shifts * slots * pcount * feat, bytes_accessed=2 * pcount * feat, transcendentals=0
        ),
    )(
        refs.reshape(2, feat), particles, inv_sigma2.reshape(1, freqs), offsets.T, owner_map.reshape(1, slots),
        center.reshape(1, pcount),
    )
    sums, loglik = pl.pallas_call(
        last_kernel,
        out_shape=(jax.ShapeDtypeStruct((2, 1, feat), F32), jax.ShapeDtypeStruct((1, pcount), F32)),
        in_specs=[vmem, vmem],
        out_specs=(vmem, vmem),
        compiler_params=pltpu.CompilerParams(vmem_limit_bytes=grant),
    )(partial, loglik)
    return sums, loglik.reshape(pcount)


def solution(mesh):
    return jax.shard_map(
        functools.partial(per_device, mesh.shape["dom"], mesh.shape["orient"]),
        mesh=mesh,
        in_specs=(P("dom", None), P("dom", "orient", None), P(), P(), P(), P("dom")),
        out_specs=(P("dom", "orient", None), P("dom")),
        check_vma=False,
    )
```

```python
import functools
import math

import jax
import jax.numpy as jnp
from jax import lax
from jax.experimental import pallas as pl
from jax.experimental.pallas import tpu as pltpu
from jax.sharding import PartitionSpec as P

BOX = 128
CHUNKS = 4
GROUPS = 4
PAIRS = CHUNKS // 2
RING = 4
NEG_FILL = -1e30
MESH = pl.DeviceIdType.MESH
BF16, F32 = jnp.bfloat16, jnp.float32


def unit_circle(phase):
    folded = ((phase + 64) & 127) - 64
    quarter = (folded + 16) >> 5
    x = (folded - quarter * 32).astype(F32) * (2.0 * math.pi / BOX)
    x2 = x * x
    sine = x * (1.0 + x2 * (-1 / 6 + x2 * (1 / 120 + x2 * (-1 / 5040 + x2 * (1 / 362880)))))
    cosine = 1.0 + x2 * (-0.5 + x2 * (1 / 24 + x2 * (-1 / 720 + x2 * (1 / 40320))))
    odd = (quarter & 1) == 1
    cos_sign = jnp.where(((quarter + 1) & 2) == 2, -1.0, 1.0)
    sin_sign = jnp.where((quarter & 2) == 2, -1.0, 1.0)
    return jnp.where(odd, sine, cosine) * cos_sign, jnp.where(odd, cosine, sine) * sin_sign


class Torus:
    def __init__(self):
        self.me = lax.axis_index("dom")
        self.y, self.x, self.z = self.me // 8, (self.me // 2) % 4, self.me % 2

    def axes(self, c, odd=None):
        odd = c % 2 if odd is None else odd
        return odd, self.y * (1 - odd) + self.x * odd, self.x * (1 - odd) + self.y * odd

    def peers(self):
        near = [device(0, self.y, self.x, 1 - self.z)]
        for by in (1, 2, 3):
            for z in (self.z, 1 - self.z):
                near.append(device(0, self.y, step(self.x, by), z))
                near.append(device(0, step(self.y, by), self.x, z))
        return near


def device(odd, v, u, z):
    return {"dom": ((v * (1 - odd) + u * odd) * 4 + u * (1 - odd) + v * odd) * 2 + z}


def step(a, by):
    return (a + by) % RING


def greet(barrier, to):
    pl.semaphore_signal(barrier, inc=1, device_id=to, device_id_type=MESH)


def send(src, dst, send_sem, recv_sem, to):
    pltpu.make_async_remote_copy(
        src_ref=src, dst_ref=dst, send_sem=send_sem, recv_sem=recv_sem, device_id=to, device_id_type=MESH
    ).start()


def wait(ref, sem):
    pltpu.make_async_copy(ref, ref, sem).wait()


def fetch_particles(part_hbm, part, part_sem, freqs):
    width = freqs // CHUNKS
    for c in range(CHUNKS):
        for base in (0, freqs):
            cols = pl.ds(base + c * width, width)
            pltpu.make_async_copy(part_hbm.at[:, cols], part.at[:, cols], part_sem.at[c]).start()


def exchange(perm, perm_t):
    there = lax.broadcasted_iota(jnp.int32, (128, 128), 0)
    here = lax.broadcasted_iota(jnp.int32, (128, 128), 1)
    for ref, out, src in ((perm, there, here), (perm_t, here, there)):
        q, s, r = src >> 4, (src >> 3) & 1, src & 7
        ref[...] = (out == r * 16 + q * 2 + s).astype(F32).astype(BF16)


def em_kernel(
    n_dom, n_ori, shifts,
    refs_hbm, part_hbm, inv_hbm, off_hbm, omap_hbm, center_hbm,
    recv2, loglik_ref,
    part, part_t, stage, mine, pieces, gath, perm, perm_t, cos_tab, sin_tab, lhs_a, lhs_b, acc, prods_a, prods_b, power,
    refs_ref, off_ref, inv_ref, omap_ref, center_ref, stat_out, stat_in, by_class, sends, far_in, near_in, send2,
    part_sem, small_sem, ag_send, ag_recv, ring_send, ag_near, ag_far, st_send, st_recv,
    rs_send, share_send, far_sem, early_sem, late_sem, rs_recv,
):
    freqs = inv_ref.shape[1]
    slots = 2 * n_dom
    lanes = mine.shape[3]
    width = freqs // CHUNKS
    half = 4
    here = Torus()
    axes, my_z = here.axes, here.z
    my_ori = lax.axis_index("orient")

    smalls = [
        pltpu.make_async_copy(src, dst, small_sem.at[k])
        for k, (src, dst) in enumerate((
            (refs_hbm, refs_ref), (off_hbm, off_ref), (inv_hbm, inv_ref), (omap_hbm, omap_ref), (center_hbm, center_ref)
        ))
    ]

    for copy in smalls:
        copy.start()

    barrier = pltpu.get_barrier_semaphore()
    peers = here.peers()
    for to in peers:
        greet(barrier, to)

    def greet_ori(i, carry):
        greet(barrier, {"orient": lax.rem(my_ori + i, n_ori)})
        return carry

    lax.fori_loop(1, n_ori, greet_ori, 0)
    fetch_particles(part_hbm, part, part_sem, freqs)
    smalls[0].wait()

    for c in range(CHUNKS):
        for r in range(2):
            for g in range(GROUPS):
                for j in range(lanes // 128):
                    at = r * freqs + c * width + g * lanes + j * 128
                    stage[j, pl.ds(c * 16 + g * 2 + r, 2, stride=8), :] = refs_ref[:, pl.ds(at, 128)].astype(F32)
        for j in range(lanes // 128):
            mine[c % 2, c // 2, :, pl.ds(j * 128, 128)] = stage[j, pl.ds(c * 16, 16), :].astype(BF16)

    pl.semaphore_wait(barrier, len(peers) + n_ori - 1)

    batches = ((0, 1), (1, 1))

    def gather0(b):
        for odd in range(2):
            _, v, u = axes(0, odd)
            home = u * 2 + my_z
            ks = pl.ds(*batches[b])

            def share(i, carry):
                q = (home + i) % 8
                send(
                    mine.at[odd, ks], pieces.at[odd, home, ks], ag_send.at[b, odd], ag_recv.at[b, odd],
                    device(odd, v, q // 2, q % 2),
                )
                return carry

            lax.fori_loop(1, 8, share, 0)
            pieces[odd, home, ks] = mine[odd, ks]

    def gather0_wait(b):
        for odd in range(2):
            wait(pieces.at[odd, pl.ds(0, 7), pl.ds(*batches[b])], ag_recv.at[b, odd])

    def gather1(c):
        odd, v, u = axes(c)
        joined = jnp.dot(
            perm[...], pieces[odd, :, c // 2].reshape(128, lanes), preferred_element_type=F32
        ).astype(BF16)
        gath[c, v] = joined.reshape(8, 16, lanes)
        for first in range(2):
            for k, by in ((0, 1), (1, 3)):
                h = k if first == 0 else 1 - k
                block = gath.at[c, v, pl.ds(h * half, half)]
                send(block, block, ring_send.at[c], ag_near.at[c, k, h], device(odd, step(v, by), u, my_z))

    def gather2(c):
        odd, v, u = axes(c)
        for k, by in ((0, 1), (1, 3)):
            block = gath.at[c, step(v, 4 - by), pl.ds(k * half, half)]
            wait(block, ag_near.at[c, k, k])
            send(block, block, ring_send.at[c], ag_far.at[c, k], device(odd, step(v, by), u, my_z))

    def gather3(c, h):
        block = gath.at[c, 0, pl.ds(0, half)]
        wait(block, ag_near.at[c, 1 - h, h])
        wait(block, ag_far.at[c, h])

    def pair(k, stage):
        def one(i, carry):
            stage(2 * k + i)
            return carry

        lax.fori_loop(0, 2, one, 0)

    def turn_pair(k):
        for c in (2 * k, 2 * k + 1):
            wait(part.at[:, pl.ds(0, 2 * width)], part_sem.at[c])

        def turn(i, carry):
            at = pl.ds(pl.multiple_of(i // 4 * freqs + k * 2 * width + i % 4 * (width // 2), width // 2), width // 2)
            part_t[at, :] = part[:, at].T
            return carry

        lax.fori_loop(0, 8, turn, 0)

    gather0(0)
    gather0(1)
    exchange(perm, perm_t)
    smalls[1].wait()

    shift_ids = lax.broadcasted_iota(jnp.int32, (shifts, 128), 0)
    off_x = jnp.zeros((shifts, 128), jnp.int32)
    off_y = jnp.zeros((shifts, 128), jnp.int32)
    for t in range(shifts):
        off_x = jnp.where(shift_ids == t, off_ref[0, t], off_x)
        off_y = jnp.where(shift_ids == t, off_ref[1, t], off_y)

    def tables(j, carry):
        for h in range(4):
            at = pl.multiple_of(j * 512 + h * 128, 128)
            freq = lax.broadcasted_iota(jnp.int32, (shifts, 128), 1) + at
            fx = freq & (BOX // 2 - 1)
            fy = freq >> 6
            fy = jnp.where(fy < BOX // 2, fy, fy - BOX)
            cosine, sine = unit_circle(off_x * fx + off_y * fy)
            cos_tab[:, pl.ds(at, 128)] = cosine
            sin_tab[:, pl.ds(at, 128)] = sine
        return carry

    lax.fori_loop(0, freqs // 1024, tables, 0)
    gather0_wait(0)
    pair(0, gather1)
    lax.fori_loop(freqs // 1024, freqs // 512, tables, 0)
    gather0_wait(1)
    pair(1, gather1)
    turn_pair(0)
    pair(0, gather2)
    turn_pair(1)
    for copy in smalls[2:]:
        copy.wait()
    acc[...] = jnp.zeros_like(acc)
    power[...] = jnp.zeros_like(power)
    lhs_b[...] = jnp.zeros_like(lhs_b)

    def columns(group):
        at = pl.multiple_of(group * lanes, lanes)
        return pl.ds(at, lanes), pl.ds(pl.multiple_of(freqs + at, lanes), lanes)

    def score_product(lhs, c, half_chunk):
        at = pl.multiple_of((2 * c + half_chunk) * 2 * lanes, 2 * lanes)
        block = jnp.concatenate(
            [part_t[pl.ds(at, 2 * lanes), :], part_t[pl.ds(pl.multiple_of(freqs + at, 2 * lanes), 2 * lanes), :]], axis=0
        )
        for m in range(0, shifts * slots, shifts * slots // 2):
            rows = pl.ds(m, shifts * slots // 2)
            acc[c % 2, rows, :] += jnp.dot(lhs[rows, :], block, preferred_element_type=F32)

    def shift(lhs, c, g):
        for j in range(lanes // 128):
            at = pl.ds(j * 128, 128)
            col = g % 2 * lanes + j * 128
            there = pl.ds(pl.multiple_of((c * GROUPS + g) * lanes + j * 128, 128), 128)
            real = jnp.concatenate([gath[c, w, 2 * g, :, at] for w in range(RING)], axis=0).astype(F32)
            imag = jnp.concatenate([gath[c, w, 2 * g + 1, :, at] for w in range(RING)], axis=0).astype(F32)
            inv = inv_ref[:, there]
            re = real * inv
            im = imag * inv
            power[c % 2] += re * real + im * imag
            for t in range(shifts):
                cosine = cos_tab[pl.ds(t, 1), there]
                sine = sin_tab[pl.ds(t, 1), there]
                into = lhs.at[pl.ds(t * slots, slots)]
                into[:, pl.ds(col, 128)] = (re * cosine + im * sine).astype(BF16)
                into[:, pl.ds(2 * lanes + col, 128)] = (im * cosine - re * sine).astype(BF16)

    def score_chunk(c, carry):
        gather3(c, 0)
        score_product(lhs_b, jnp.maximum(c - 1, 0), 1)
        shift(lhs_a, c, 0)
        shift(lhs_a, c, 1)
        gather3(c, 1)
        score_product(lhs_a, c, 0)
        shift(lhs_b, c, 2)
        shift(lhs_b, c, 3)

        @pl.when(c == 0)
        def _():
            pair(1, gather2)

        return carry

    lax.fori_loop(0, CHUNKS, score_chunk, 0)
    score_product(lhs_b, CHUNKS - 1, 1)

    for base, ref in [(t * slots, acc) for t in range(shifts)] + [(0, power)]:
        for y in range(4):
            for x in range(4):
                ref[0, pl.ds(base + y * 16 + x * 4, 4), :] += ref[1, pl.ds(base + x * 16 + y * 4, 4), :]

    power_col = 0.5 * jnp.sum(power[0], axis=1, keepdims=True)
    distance = jnp.abs(my_ori - center_ref[...])
    allowed = jnp.minimum(distance, n_ori - distance) <= n_ori // 4
    best = None
    for t in range(shifts):
        at = pl.ds(t * slots, slots)
        value = jnp.where(allowed, acc[0, at, :] - power_col, NEG_FILL)
        acc[0, at, :] = value
        top = jnp.max(value, axis=0, keepdims=True)
        best = top if best is None else jnp.maximum(best, top)
    total = jnp.zeros_like(best)
    for t in range(shifts):
        at = pl.ds(t * slots, slots)
        value = jnp.exp(acc[0, at, :] - best)
        acc[0, at, :] = value
        total += jnp.sum(value, axis=0, keepdims=True)
    mine_best = best
    stat_out[0:1, :] = best
    stat_out[1:2, :] = total

    def stat_send(i, carry):
        send(stat_out, stat_in.at[my_ori], st_send, st_recv, {"orient": lax.rem(my_ori + i, n_ori)})
        return carry

    lax.fori_loop(1, n_ori, stat_send, 0)
    stat_in[my_ori] = stat_out[...]
    if n_ori > 1:
        others = stat_in.at[pl.ds(0, n_ori - 1)]
        wait(others, st_recv)
        wait(others, st_send)
    bests = [stat_in[o, 0:1, :] for o in range(n_ori)]
    best = functools.reduce(jnp.maximum, bests)
    total = sum(stat_in[o, 1:2, :] * jnp.exp(bests[o] - best) for o in range(n_ori))
    loglik_ref[...] = best + jnp.log(total)
    scale = jnp.exp(mine_best - best) / total

    pick = (lax.broadcasted_iota(jnp.int32, (slots, slots), 0) == omap_ref[...]).astype(F32).astype(BF16)
    weights = jnp.concatenate(
        [(acc[0, pl.ds(t * slots, slots), :] * scale).astype(BF16) for t in range(shifts)], axis=1
    )
    row = lax.broadcasted_iota(jnp.int32, (slots, slots), 1)
    swapped = ((row >> 2) & 3) * 16 + (row >> 4) * 4 + (row & 3)
    swap = (lax.broadcasted_iota(jnp.int32, (slots, slots), 0) == swapped).astype(F32).astype(BF16)
    picks = jnp.concatenate([pick, jnp.dot(pick, swap, preferred_element_type=F32).astype(BF16)], axis=1)
    picked = lax.dot_general(picks, weights, (((0,), (0,)), ((), ())), preferred_element_type=F32).astype(BF16)
    pcount = acc.shape[2]
    for odd in range(2):
        for t in range(shifts):
            by_class[odd, pl.ds(t * slots, slots), :] = picked[
                odd * slots:(odd + 1) * slots, t * pcount:(t + 1) * pcount
            ]

    def multiply(prods, group):
        block = jnp.concatenate([part[:, at] for at in columns(group)], axis=1)
        prods[...] = jnp.dot(by_class[group // GROUPS % 2], block, preferred_element_type=F32)

    def rotate(prods, c, g):
        for j in range(lanes // 128):
            at = pl.ds(j * 128, 128)
            there = pl.ds(pl.multiple_of((c * GROUPS + g) * lanes + j * 128, 128), 128)
            out_real = out_imag = None
            for t in range(shifts):
                cosine = cos_tab[pl.ds(t, 1), there]
                sine = sin_tab[pl.ds(t, 1), there]
                re = prods[pl.ds(t * slots, slots), at]
                im = prods[pl.ds(t * slots, slots), pl.ds(lanes + j * 128, 128)]
                term_real = re * cosine - im * sine
                term_imag = im * cosine + re * sine
                out_real = term_real if t == 0 else out_real + term_real
                out_imag = term_imag if t == 0 else out_imag + term_imag
            for w in range(RING):
                sends[c, w, 2 * g, :, at] = out_real[w * 16:(w + 1) * 16].astype(BF16)
                sends[c, w, 2 * g + 1, :, at] = out_imag[w * 16:(w + 1) * 16].astype(BF16)

    def sum_half(c, h):
        first = c * GROUPS + 2 * h
        multiply(prods_b, first + 1)
        rotate(prods_a, c, 2 * h)
        multiply(prods_a, jnp.minimum(first + 2, CHUNKS * GROUPS - 1))
        rotate(prods_b, c, 2 * h + 1)

    def reduce0(c, h):
        odd, v, u = axes(c)
        part_of = pl.ds(h * half, half)
        to = device(odd, step(v, 1 + 2 * h), u, my_z)
        send(sends.at[c, step(v, 2), part_of], far_in.at[c, h], rs_send.at[c], far_sem.at[c, h], to)
        w = step(v, 3 - 2 * h)
        send(
            sends.at[c, w, part_of], near_in.at[c, 1 - h, part_of], rs_send.at[c], early_sem.at[c, 1 - h],
            device(odd, w, u, my_z),
        )

    def reduce1(c, ks):
        odd, v, u = axes(c)
        for k in ks:
            by = 1 + 2 * k
            wait(far_in.at[c, k], far_sem.at[c, k])
            w, part_of = step(v, by), pl.ds(k * half, half)
            sends[c, w, part_of] = (sends[c, w, part_of].astype(F32) + far_in[c, k].astype(F32)).astype(BF16)
            send(
                sends.at[c, w, part_of], near_in.at[c, k, part_of], rs_send.at[c], late_sem.at[c, k],
                device(odd, w, u, my_z),
            )

    def reduce2(c):
        odd, v, u = axes(c)
        for k in range(2):
            wait(near_in.at[c, k, pl.ds((1 - k) * half, half)], early_sem.at[c, k])
            wait(near_in.at[c, k, pl.ds(k * half, half)], late_sem.at[c, k])
        total = sends[c, v].astype(F32) + near_in[c, 0].astype(F32) + near_in[c, 1].astype(F32)
        apart = jnp.dot(
            perm_t[...], total.astype(BF16).reshape(128, lanes), preferred_element_type=F32
        ).astype(BF16)
        send2[c] = apart.reshape(8, 16, lanes)
        home = u * 2 + my_z

        def share(i, carry):
            q = (home + i) % 8
            send(send2.at[c, q], recv2.at[c, home], share_send.at[c], rs_recv.at[c], device(odd, v, q // 2, q % 2))
            return carry

        lax.fori_loop(1, 8, share, 0)
        recv2[c, home] = send2[c, home]

    def sum_step(i, carry):
        c, h = i // 2, i % 2
        sum_half(c, h)
        reduce0(c, h)
        for k in range(2):
            @pl.when((h == k) & (c >= 1))
            def _():
                reduce1(c - 1, (k,))

        @pl.when((h == 1) & (c >= 2))
        def _():
            reduce2(c - 2)

        return carry

    multiply(prods_a, 0)
    lax.fori_loop(0, 2 * CHUNKS, sum_step, 0)
    reduce1(CHUNKS - 1, (0, 1))
    reduce2(CHUNKS - 2)
    reduce2(CHUNKS - 1)

    for b in range(2):
        for odd in range(2):
            wait(pieces.at[odd, pl.ds(0, 7), pl.ds(*batches[b])], ag_send.at[b, odd])

    def drain(c, carry):
        wait(recv2.at[c, pl.ds(0, 7)], rs_recv.at[c])
        wait(gath.at[c, pl.ds(0, 3)], ring_send.at[c])
        wait(sends.at[c, pl.ds(0, 3)], rs_send.at[c])
        wait(send2.at[c, pl.ds(0, 7)], share_send.at[c])
        return carry

    lax.fori_loop(0, CHUNKS, drain, 0)


def last_kernel(recv2, loglik_in, out_ref, loglik_ref):
    lanes = recv2.shape[3]
    freqs = CHUNKS * GROUPS * lanes
    loglik_ref[...] = loglik_in[...]
    for c in range(CHUNKS):
        for j in range(lanes // 128):
            total = recv2[c, 0, :, pl.ds(j * 128, 128)].astype(F32)
            for q in range(1, 8):
                total += recv2[c, q, :, pl.ds(j * 128, 128)].astype(F32)
            for s in range(2):
                for r in range(2):
                    for g in range(GROUPS):
                        row = s * 8 + g * 2 + r
                        at = r * freqs + c * GROUPS * lanes + g * lanes + j * 128
                        out_ref[s, :, pl.ds(at, 128)] = total[row:row + 1, :]


def per_device(n_dom, n_ori, particles, refs, inv_sigma2, offsets, owner_map, center):
    pcount, feat = particles.shape
    freqs = feat // 2
    shifts = offsets.shape[0]
    slots = 2 * n_dom
    lanes = freqs // (CHUNKS * GROUPS)
    vmem = pl.BlockSpec(memory_space=pltpu.VMEM)
    far = pl.BlockSpec(memory_space=pltpu.HBM)
    dma = pltpu.SemaphoreType.DMA
    grant = 56 * 1024 * 1024
    partial, loglik = pl.pallas_call(
        functools.partial(em_kernel, n_dom, n_ori, shifts),
        out_shape=(
            jax.ShapeDtypeStruct((CHUNKS, 8, 16, lanes), BF16),
            jax.ShapeDtypeStruct((1, pcount), F32),
        ),
        in_specs=[far] * 6,
        out_specs=(vmem, vmem),
        scratch_shapes=[
            pltpu.VMEM((pcount, feat), BF16),
            pltpu.VMEM((feat, pcount), BF16),
            pltpu.VMEM((lanes // 128, 16 * CHUNKS, 128), F32),
            pltpu.VMEM((2, PAIRS, 16, lanes), BF16),
            pltpu.VMEM((2, 8, PAIRS, 16, lanes), BF16),
            pltpu.VMEM((CHUNKS, RING, 8, 16, lanes), BF16),
            pltpu.VMEM((128, 128), BF16),
            pltpu.VMEM((128, 128), BF16),
            pltpu.VMEM((shifts, freqs), F32),
            pltpu.VMEM((shifts, freqs), F32),
            pltpu.VMEM((shifts * slots, 4 * lanes), BF16),
            pltpu.VMEM((shifts * slots, 4 * lanes), BF16),
            pltpu.VMEM((2, shifts * slots, pcount), F32),
            pltpu.VMEM((shifts * slots, 2 * lanes), F32),
            pltpu.VMEM((shifts * slots, 2 * lanes), F32),
            pltpu.VMEM((2, slots, 128), F32),
            pltpu.VMEM((2, feat), BF16),
            pltpu.SMEM((2, shifts), jnp.int32),
            pltpu.VMEM((1, freqs), F32),
            pltpu.VMEM((1, slots), jnp.int32),
            pltpu.VMEM((1, pcount), jnp.int32),
            pltpu.VMEM((2, pcount), F32),
            pltpu.VMEM((n_ori, 2, pcount), F32),
            pltpu.VMEM((2, shifts * slots, pcount), BF16),
            pltpu.VMEM((CHUNKS, RING, 8, 16, lanes), BF16),
            pltpu.VMEM((CHUNKS, 2, 4, 16, lanes), BF16),
            pltpu.VMEM((CHUNKS, 2, 8, 16, lanes), BF16),
            pltpu.VMEM((CHUNKS, 8, 16, lanes), BF16),
            dma((CHUNKS,)),
            dma((5,)),
            dma((2, 2)),
            dma((2, 2)),
            dma((CHUNKS,)),
            dma((CHUNKS, 2, 2)),
            dma((CHUNKS, 2)),
            dma,
            dma,
            dma((CHUNKS,)),
            dma((CHUNKS,)),
            dma((CHUNKS, 2)),
            dma((CHUNKS, 2)),
            dma((CHUNKS, 2)),
            dma((CHUNKS,)),
        ],
        compiler_params=pltpu.CompilerParams(collective_id=0, has_side_effects=True, vmem_limit_bytes=grant),
        cost_estimate=pl.CostEstimate(
            flops=4 * shifts * slots * pcount * feat, bytes_accessed=2 * pcount * feat, transcendentals=0
        ),
    )(
        refs.reshape(2, feat), particles, inv_sigma2.reshape(1, freqs), offsets.T, owner_map.reshape(1, slots),
        center.reshape(1, pcount),
    )
    sums, loglik = pl.pallas_call(
        last_kernel,
        out_shape=(jax.ShapeDtypeStruct((2, 1, feat), F32), jax.ShapeDtypeStruct((1, pcount), F32)),
        in_specs=[vmem, vmem],
        out_specs=(vmem, vmem),
        compiler_params=pltpu.CompilerParams(vmem_limit_bytes=grant),
    )(partial, loglik)
    return sums, loglik.reshape(pcount)


def solution(mesh):
    return jax.shard_map(
        functools.partial(per_device, mesh.shape["dom"], mesh.shape["orient"]),
        mesh=mesh,
        in_specs=(P("dom", None), P("dom", "orient", None), P(), P(), P(), P("dom")),
        out_specs=(P("dom", "orient", None), P("dom")),
        check_vma=False,
    )
```

```python
import functools
import math

import jax
import jax.numpy as jnp
from jax import lax
from jax.experimental import pallas as pl
from jax.experimental.pallas import tpu as pltpu
from jax.sharding import PartitionSpec as P

BOX = 128
CHUNKS = 4
GROUPS = 4
PAIRS = CHUNKS // 2
RING = 4
NEG_FILL = -1e30
MESH = pl.DeviceIdType.MESH
BF16, F32 = jnp.bfloat16, jnp.float32


def unit_circle(phase):
    folded = ((phase + 64) & 127) - 64
    quarter = (folded + 16) >> 5
    x = (folded - quarter * 32).astype(F32) * (2.0 * math.pi / BOX)
    x2 = x * x
    sine = x * (1.0 + x2 * (-1 / 6 + x2 * (1 / 120 + x2 * (-1 / 5040 + x2 * (1 / 362880)))))
    cosine = 1.0 + x2 * (-0.5 + x2 * (1 / 24 + x2 * (-1 / 720 + x2 * (1 / 40320))))
    odd = (quarter & 1) == 1
    cos_sign = jnp.where(((quarter + 1) & 2) == 2, -1.0, 1.0)
    sin_sign = jnp.where((quarter & 2) == 2, -1.0, 1.0)
    return jnp.where(odd, sine, cosine) * cos_sign, jnp.where(odd, cosine, sine) * sin_sign


class Torus:
    def __init__(self):
        self.me = lax.axis_index("dom")
        self.core = lax.axis_index("orient") % 2
        self.y, self.x, self.z = self.me // 8, (self.me // 2) % 4, self.me % 2

    def turned(self, c):
        return (c + self.core) % 2

    def axes(self, c):
        odd = self.turned(c)
        return odd, self.y * (1 - odd) + self.x * odd, self.x * (1 - odd) + self.y * odd

    def peers(self):
        near = [device(0, self.y, self.x, 1 - self.z)]
        for by in (1, 2, 3):
            for z in (self.z, 1 - self.z):
                near.append(device(0, self.y, step(self.x, by), z))
                near.append(device(0, step(self.y, by), self.x, z))
        return near


def device(odd, v, u, z):
    return {"dom": ((v * (1 - odd) + u * odd) * 4 + u * (1 - odd) + v * odd) * 2 + z}


def step(a, by):
    return (a + by) % RING


def greet(barrier, to):
    pl.semaphore_signal(barrier, inc=1, device_id=to, device_id_type=MESH)


def send(src, dst, send_sem, recv_sem, to):
    pltpu.make_async_remote_copy(
        src_ref=src, dst_ref=dst, send_sem=send_sem, recv_sem=recv_sem, device_id=to, device_id_type=MESH
    ).start()


def wait(ref, sem):
    pltpu.make_async_copy(ref, ref, sem).wait()


def fetch_particles(part_hbm, part, part_sem, freqs, c):
    width = freqs // CHUNKS
    for base in (0, freqs):
        cols = pl.ds(base + c * width, width)
        pltpu.make_async_copy(part_hbm.at[:, cols], part.at[:, cols], part_sem.at[c]).start()


def exchange(perm, perm_t):
    there = lax.broadcasted_iota(jnp.int32, (128, 128), 0)
    here = lax.broadcasted_iota(jnp.int32, (128, 128), 1)
    for ref, out, src in ((perm, there, here), (perm_t, here, there)):
        q, s, r = src >> 4, (src >> 3) & 1, src & 7
        ref[...] = (out == r * 16 + q * 2 + s).astype(F32).astype(BF16)


def em_kernel(
    n_dom, n_ori, shifts,
    refs_hbm, part_hbm, inv_hbm, off_hbm, omap_hbm, center_hbm,
    recv2, loglik_ref,
    part, part_t, stage, mine, pieces, gath, perm, perm_t, cos_tab, sin_tab, lhs_a, lhs_b, acc, prods_a, prods_b, power,
    refs_ref, off_ref, inv_ref, omap_ref, center_ref, stat_out, stat_in, by_class, sends, far_in, near_in, send2,
    part_sem, small_sem, ag_send, ag_recv, ring_send, ag_near, ag_far, st_send, st_recv,
    rs_send, share_send, far_sem, early_sem, late_sem, rs_recv,
):
    freqs = inv_ref.shape[1]
    slots = 2 * n_dom
    lanes = mine.shape[3]
    width = freqs // CHUNKS
    half = 4
    here = Torus()
    axes, turned, my_z = here.axes, here.turned, here.z
    my_ori = lax.axis_index("orient")

    smalls = [
        pltpu.make_async_copy(src, dst, small_sem.at[k])
        for k, (src, dst) in enumerate((
            (refs_hbm, refs_ref), (off_hbm, off_ref), (inv_hbm, inv_ref), (omap_hbm, omap_ref), (center_hbm, center_ref)
        ))
    ]

    for copy in smalls:
        copy.start()

    barrier = pltpu.get_barrier_semaphore()
    peers = here.peers()
    for to in peers:
        greet(barrier, to)

    def greet_ori(i, carry):
        greet(barrier, {"orient": lax.rem(my_ori + i, n_ori)})
        return carry

    lax.fori_loop(1, n_ori, greet_ori, 0)
    smalls[0].wait()

    for c in range(CHUNKS):
        for r in range(2):
            for g in range(GROUPS):
                for j in range(lanes // 128):
                    at = r * freqs + c * width + g * lanes + j * 128
                    stage[j, pl.ds(c * 16 + g * 2 + r, 2, stride=8), :] = refs_ref[:, pl.ds(at, 128)].astype(F32)
        for j in range(lanes // 128):
            mine[c % 2, c // 2, :, pl.ds(j * 128, 128)] = stage[j, pl.ds(c * 16, 16), :].astype(BF16)

    pl.semaphore_wait(barrier, len(peers) + n_ori - 1)

    batches = ((0, 1), (1, 1))

    def gather0(b):
        for kind in range(2):
            odd, v, u = axes(kind)
            home = u * 2 + my_z
            ks = pl.ds(*batches[b])

            def share(i, carry):
                q = (home + i) % 8
                send(
                    mine.at[kind, ks], pieces.at[kind, home, ks], ag_send.at[b, kind], ag_recv.at[b, kind],
                    device(odd, v, q // 2, q % 2),
                )
                return carry

            lax.fori_loop(1, 8, share, 0)
            pieces[kind, home, ks] = mine[kind, ks]

    def gather0_wait(b):
        for kind in range(2):
            wait(pieces.at[kind, pl.ds(0, 7), pl.ds(*batches[b])], ag_recv.at[b, kind])

    def gather1(c):
        odd, v, u = axes(c)
        joined = jnp.dot(
            perm[...], pieces[c % 2, :, c // 2].reshape(128, lanes), preferred_element_type=F32
        ).astype(BF16)
        gath[c, v] = joined.reshape(8, 16, lanes)
        for first in range(2):
            for k, by in ((0, 1), (1, 3)):
                h = k if first == 0 else 1 - k
                block = gath.at[c, v, pl.ds(h * half, half)]
                send(block, block, ring_send.at[c], ag_near.at[c, k, h], device(odd, step(v, by), u, my_z))

    def gather2(c):
        odd, v, u = axes(c)
        for k, by in ((0, 1), (1, 3)):
            block = gath.at[c, step(v, 4 - by), pl.ds(k * half, half)]
            wait(block, ag_near.at[c, k, k])
            send(block, block, ring_send.at[c], ag_far.at[c, k], device(odd, step(v, by), u, my_z))

    def gather3(c, h):
        block = gath.at[c, 0, pl.ds(0, half)]
        wait(block, ag_near.at[c, 1 - h, h])
        wait(block, ag_far.at[c, h])

    def pair(k, stage):
        def one(i, carry):
            stage(2 * k + i)
            return carry

        lax.fori_loop(0, 2, one, 0)

    def turn_pair(k):
        for c in (2 * k, 2 * k + 1):
            wait(part.at[:, pl.ds(0, 2 * width)], part_sem.at[c])

        def turn(i, carry):
            at = pl.ds(pl.multiple_of(i // 4 * freqs + k * 2 * width + i % 4 * (width // 2), width // 2), width // 2)
            part_t[at, :] = part[:, at].T
            return carry

        lax.fori_loop(0, 8, turn, 0)

    gather0(0)
    gather0(1)
    for c in range(2):
        fetch_particles(part_hbm, part, part_sem, freqs, c)
    exchange(perm, perm_t)
    smalls[1].wait()

    shift_ids = lax.broadcasted_iota(jnp.int32, (shifts, 128), 0)
    off_x = jnp.zeros((shifts, 128), jnp.int32)
    off_y = jnp.zeros((shifts, 128), jnp.int32)
    for t in range(shifts):
        off_x = jnp.where(shift_ids == t, off_ref[0, t], off_x)
        off_y = jnp.where(shift_ids == t, off_ref[1, t], off_y)

    def tables(j, carry):
        for h in range(4):
            at = pl.multiple_of(j * 512 + h * 128, 128)
            freq = lax.broadcasted_iota(jnp.int32, (shifts, 128), 1) + at
            fx = freq & (BOX // 2 - 1)
            fy = freq >> 6
            fy = jnp.where(fy < BOX // 2, fy, fy - BOX)
            cosine, sine = unit_circle(off_x * fx + off_y * fy)
            cos_tab[:, pl.ds(at, 128)] = cosine
            sin_tab[:, pl.ds(at, 128)] = sine
        return carry

    lax.fori_loop(0, freqs // 1024, tables, 0)
    gather0_wait(0)
    pair(0, gather1)
    lax.fori_loop(freqs // 1024, freqs // 512, tables, 0)
    gather0_wait(1)
    pair(1, gather1)
    for c in range(2, CHUNKS):
        fetch_particles(part_hbm, part, part_sem, freqs, c)
    turn_pair(0)
    pair(0, gather2)
    turn_pair(1)
    for copy in smalls[2:]:
        copy.wait()
    acc[...] = jnp.zeros_like(acc)
    power[...] = jnp.zeros_like(power)
    lhs_b[...] = jnp.zeros_like(lhs_b)

    def columns(group):
        at = pl.multiple_of(group * lanes, lanes)
        return pl.ds(at, lanes), pl.ds(pl.multiple_of(freqs + at, lanes), lanes)

    def score_product(lhs, c, half_chunk):
        at = pl.multiple_of((2 * c + half_chunk) * 2 * lanes, 2 * lanes)
        block = jnp.concatenate(
            [part_t[pl.ds(at, 2 * lanes), :], part_t[pl.ds(pl.multiple_of(freqs + at, 2 * lanes), 2 * lanes), :]], axis=0
        )
        for m in range(0, shifts * slots, shifts * slots // 2):
            rows = pl.ds(m, shifts * slots // 2)
            acc[turned(c), rows, :] += jnp.dot(lhs[rows, :], block, preferred_element_type=F32)

    def shift(lhs, c, g):
        for j in range(lanes // 128):
            at = pl.ds(j * 128, 128)
            col = g % 2 * lanes + j * 128
            there = pl.ds(pl.multiple_of((c * GROUPS + g) * lanes + j * 128, 128), 128)
            real = jnp.concatenate([gath[c, w, 2 * g, :, at] for w in range(RING)], axis=0).astype(F32)
            imag = jnp.concatenate([gath[c, w, 2 * g + 1, :, at] for w in range(RING)], axis=0).astype(F32)
            inv = inv_ref[:, there]
            re = real * inv
            im = imag * inv
            power[turned(c)] += re * real + im * imag
            for t in range(shifts):
                cosine = cos_tab[pl.ds(t, 1), there]
                sine = sin_tab[pl.ds(t, 1), there]
                into = lhs.at[pl.ds(t * slots, slots)]
                into[:, pl.ds(col, 128)] = (re * cosine + im * sine).astype(BF16)
                into[:, pl.ds(2 * lanes + col, 128)] = (im * cosine - re * sine).astype(BF16)

    def score_chunk(c, carry):
        gather3(c, 0)
        score_product(lhs_b, jnp.maximum(c - 1, 0), 1)
        shift(lhs_a, c, 0)
        shift(lhs_a, c, 1)
        gather3(c, 1)
        score_product(lhs_a, c, 0)
        shift(lhs_b, c, 2)
        shift(lhs_b, c, 3)

        @pl.when(c == 0)
        def _():
            pair(1, gather2)

        return carry

    lax.fori_loop(0, CHUNKS, score_chunk, 0)
    score_product(lhs_b, CHUNKS - 1, 1)

    for base, ref in [(t * slots, acc) for t in range(shifts)] + [(0, power)]:
        for y in range(4):
            for x in range(4):
                ref[0, pl.ds(base + y * 16 + x * 4, 4), :] += ref[1, pl.ds(base + x * 16 + y * 4, 4), :]

    power_col = 0.5 * jnp.sum(power[0], axis=1, keepdims=True)
    distance = jnp.abs(my_ori - center_ref[...])
    allowed = jnp.minimum(distance, n_ori - distance) <= n_ori // 4
    best = None
    for t in range(shifts):
        at = pl.ds(t * slots, slots)
        value = jnp.where(allowed, acc[0, at, :] - power_col, NEG_FILL)
        acc[0, at, :] = value
        top = jnp.max(value, axis=0, keepdims=True)
        best = top if best is None else jnp.maximum(best, top)
    total = jnp.zeros_like(best)
    for t in range(shifts):
        at = pl.ds(t * slots, slots)
        value = jnp.exp(acc[0, at, :] - best)
        acc[0, at, :] = value
        total += jnp.sum(value, axis=0, keepdims=True)
    mine_best = best
    stat_out[0:1, :] = best
    stat_out[1:2, :] = total

    def stat_send(i, carry):
        send(stat_out, stat_in.at[my_ori], st_send, st_recv, {"orient": lax.rem(my_ori + i, n_ori)})
        return carry

    lax.fori_loop(1, n_ori, stat_send, 0)
    stat_in[my_ori] = stat_out[...]
    if n_ori > 1:
        others = stat_in.at[pl.ds(0, n_ori - 1)]
        wait(others, st_recv)
        wait(others, st_send)
    bests = [stat_in[o, 0:1, :] for o in range(n_ori)]
    best = functools.reduce(jnp.maximum, bests)
    total = sum(stat_in[o, 1:2, :] * jnp.exp(bests[o] - best) for o in range(n_ori))
    loglik_ref[...] = best + jnp.log(total)
    scale = jnp.exp(mine_best - best) / total

    pick = (lax.broadcasted_iota(jnp.int32, (slots, slots), 0) == omap_ref[...]).astype(F32).astype(BF16)
    weights = jnp.concatenate(
        [(acc[0, pl.ds(t * slots, slots), :] * scale).astype(BF16) for t in range(shifts)], axis=1
    )
    row = lax.broadcasted_iota(jnp.int32, (slots, slots), 1)
    swapped = ((row >> 2) & 3) * 16 + (row >> 4) * 4 + (row & 3)
    swap = (lax.broadcasted_iota(jnp.int32, (slots, slots), 0) == swapped).astype(F32).astype(BF16)
    picks = jnp.concatenate([pick, jnp.dot(pick, swap, preferred_element_type=F32).astype(BF16)], axis=1)
    picked = lax.dot_general(picks, weights, (((0,), (0,)), ((), ())), preferred_element_type=F32).astype(BF16)
    pcount = acc.shape[2]
    for odd in range(2):
        for t in range(shifts):
            by_class[odd, pl.ds(t * slots, slots), :] = picked[
                odd * slots:(odd + 1) * slots, t * pcount:(t + 1) * pcount
            ]

    def multiply(prods, group):
        block = jnp.concatenate([part[:, at] for at in columns(group)], axis=1)
        prods[...] = jnp.dot(by_class[turned(group // GROUPS)], block, preferred_element_type=F32)

    def rotate(prods, c, g):
        for j in range(lanes // 128):
            at = pl.ds(j * 128, 128)
            there = pl.ds(pl.multiple_of((c * GROUPS + g) * lanes + j * 128, 128), 128)
            out_real = out_imag = None
            for t in range(shifts):
                cosine = cos_tab[pl.ds(t, 1), there]
                sine = sin_tab[pl.ds(t, 1), there]
                re = prods[pl.ds(t * slots, slots), at]
                im = prods[pl.ds(t * slots, slots), pl.ds(lanes + j * 128, 128)]
                term_real = re * cosine - im * sine
                term_imag = im * cosine + re * sine
                out_real = term_real if t == 0 else out_real + term_real
                out_imag = term_imag if t == 0 else out_imag + term_imag
            for w in range(RING):
                sends[c, w, 2 * g, :, at] = out_real[w * 16:(w + 1) * 16].astype(BF16)
                sends[c, w, 2 * g + 1, :, at] = out_imag[w * 16:(w + 1) * 16].astype(BF16)

    def sum_half(c, h):
        first = c * GROUPS + 2 * h
        multiply(prods_b, first + 1)
        rotate(prods_a, c, 2 * h)
        multiply(prods_a, jnp.minimum(first + 2, CHUNKS * GROUPS - 1))
        rotate(prods_b, c, 2 * h + 1)

    def reduce0(c, h):
        odd, v, u = axes(c)
        part_of = pl.ds(h * half, half)
        to = device(odd, step(v, 1 + 2 * h), u, my_z)
        send(sends.at[c, step(v, 2), part_of], far_in.at[c, h], rs_send.at[c], far_sem.at[c, h], to)
        w = step(v, 3 - 2 * h)
        send(
            sends.at[c, w, part_of], near_in.at[c, 1 - h, part_of], rs_send.at[c], early_sem.at[c, 1 - h],
            device(odd, w, u, my_z),
        )

    def reduce1(c, ks):
        odd, v, u = axes(c)
        for k in ks:
            by = 1 + 2 * k
            wait(far_in.at[c, k], far_sem.at[c, k])
            w, part_of = step(v, by), pl.ds(k * half, half)
            sends[c, w, part_of] = (sends[c, w, part_of].astype(F32) + far_in[c, k].astype(F32)).astype(BF16)
            send(
                sends.at[c, w, part_of], near_in.at[c, k, part_of], rs_send.at[c], late_sem.at[c, k],
                device(odd, w, u, my_z),
            )

    def reduce2(c):
        odd, v, u = axes(c)
        for k in range(2):
            wait(near_in.at[c, k, pl.ds((1 - k) * half, half)], early_sem.at[c, k])
            wait(near_in.at[c, k, pl.ds(k * half, half)], late_sem.at[c, k])
        total = sends[c, v].astype(F32) + near_in[c, 0].astype(F32) + near_in[c, 1].astype(F32)
        apart = jnp.dot(
            perm_t[...], total.astype(BF16).reshape(128, lanes), preferred_element_type=F32
        ).astype(BF16)
        send2[c] = apart.reshape(8, 16, lanes)
        home = u * 2 + my_z

        def share(i, carry):
            q = (home + i) % 8
            send(send2.at[c, q], recv2.at[c, home], share_send.at[c], rs_recv.at[c], device(odd, v, q // 2, q % 2))
            return carry

        lax.fori_loop(1, 8, share, 0)
        recv2[c, home] = send2[c, home]

    def sum_step(i, carry):
        c, h = i // 2, i % 2
        sum_half(c, h)
        reduce0(c, h)
        for k in range(2):
            @pl.when((h == k) & (c >= 1))
            def _():
                reduce1(c - 1, (k,))

        @pl.when((h == 1) & (c >= 2))
        def _():
            reduce2(c - 2)

        return carry

    multiply(prods_a, 0)
    lax.fori_loop(0, 2 * CHUNKS, sum_step, 0)
    reduce1(CHUNKS - 1, (0, 1))
    reduce2(CHUNKS - 2)
    reduce2(CHUNKS - 1)

    for b in range(2):
        for odd in range(2):
            wait(pieces.at[odd, pl.ds(0, 7), pl.ds(*batches[b])], ag_send.at[b, odd])

    def drain(c, carry):
        wait(recv2.at[c, pl.ds(0, 7)], rs_recv.at[c])
        wait(gath.at[c, pl.ds(0, 3)], ring_send.at[c])
        wait(sends.at[c, pl.ds(0, 3)], rs_send.at[c])
        wait(send2.at[c, pl.ds(0, 7)], share_send.at[c])
        return carry

    lax.fori_loop(0, CHUNKS, drain, 0)


def last_kernel(recv2, loglik_in, out_ref, loglik_ref):
    lanes = recv2.shape[3]
    freqs = CHUNKS * GROUPS * lanes
    loglik_ref[...] = loglik_in[...]
    for c in range(CHUNKS):
        for j in range(lanes // 128):
            total = recv2[c, 0, :, pl.ds(j * 128, 128)].astype(F32)
            for q in range(1, 8):
                total += recv2[c, q, :, pl.ds(j * 128, 128)].astype(F32)
            for s in range(2):
                for r in range(2):
                    for g in range(GROUPS):
                        row = s * 8 + g * 2 + r
                        at = r * freqs + c * GROUPS * lanes + g * lanes + j * 128
                        out_ref[s, :, pl.ds(at, 128)] = total[row:row + 1, :]


def per_device(n_dom, n_ori, particles, refs, inv_sigma2, offsets, owner_map, center):
    pcount, feat = particles.shape
    freqs = feat // 2
    shifts = offsets.shape[0]
    slots = 2 * n_dom
    lanes = freqs // (CHUNKS * GROUPS)
    vmem = pl.BlockSpec(memory_space=pltpu.VMEM)
    far = pl.BlockSpec(memory_space=pltpu.HBM)
    dma = pltpu.SemaphoreType.DMA
    grant = 56 * 1024 * 1024
    partial, loglik = pl.pallas_call(
        functools.partial(em_kernel, n_dom, n_ori, shifts),
        out_shape=(
            jax.ShapeDtypeStruct((CHUNKS, 8, 16, lanes), BF16),
            jax.ShapeDtypeStruct((1, pcount), F32),
        ),
        in_specs=[far] * 6,
        out_specs=(vmem, vmem),
        scratch_shapes=[
            pltpu.VMEM((pcount, feat), BF16),
            pltpu.VMEM((feat, pcount), BF16),
            pltpu.VMEM((lanes // 128, 16 * CHUNKS, 128), F32),
            pltpu.VMEM((2, PAIRS, 16, lanes), BF16),
            pltpu.VMEM((2, 8, PAIRS, 16, lanes), BF16),
            pltpu.VMEM((CHUNKS, RING, 8, 16, lanes), BF16),
            pltpu.VMEM((128, 128), BF16),
            pltpu.VMEM((128, 128), BF16),
            pltpu.VMEM((shifts, freqs), F32),
            pltpu.VMEM((shifts, freqs), F32),
            pltpu.VMEM((shifts * slots, 4 * lanes), BF16),
            pltpu.VMEM((shifts * slots, 4 * lanes), BF16),
            pltpu.VMEM((2, shifts * slots, pcount), F32),
            pltpu.VMEM((shifts * slots, 2 * lanes), F32),
            pltpu.VMEM((shifts * slots, 2 * lanes), F32),
            pltpu.VMEM((2, slots, 128), F32),
            pltpu.VMEM((2, feat), BF16),
            pltpu.SMEM((2, shifts), jnp.int32),
            pltpu.VMEM((1, freqs), F32),
            pltpu.VMEM((1, slots), jnp.int32),
            pltpu.VMEM((1, pcount), jnp.int32),
            pltpu.VMEM((2, pcount), F32),
            pltpu.VMEM((n_ori, 2, pcount), F32),
            pltpu.VMEM((2, shifts * slots, pcount), BF16),
            pltpu.VMEM((CHUNKS, RING, 8, 16, lanes), BF16),
            pltpu.VMEM((CHUNKS, 2, 4, 16, lanes), BF16),
            pltpu.VMEM((CHUNKS, 2, 8, 16, lanes), BF16),
            pltpu.VMEM((CHUNKS, 8, 16, lanes), BF16),
            dma((CHUNKS,)),
            dma((5,)),
            dma((2, 2)),
            dma((2, 2)),
            dma((CHUNKS,)),
            dma((CHUNKS, 2, 2)),
            dma((CHUNKS, 2)),
            dma,
            dma,
            dma((CHUNKS,)),
            dma((CHUNKS,)),
            dma((CHUNKS, 2)),
            dma((CHUNKS, 2)),
            dma((CHUNKS, 2)),
            dma((CHUNKS,)),
        ],
        compiler_params=pltpu.CompilerParams(collective_id=0, has_side_effects=True, vmem_limit_bytes=grant),
        cost_estimate=pl.CostEstimate(
            flops=4 * shifts * slots * pcount * feat, bytes_accessed=2 * pcount * feat, transcendentals=0
        ),
    )(
        refs.reshape(2, feat), particles, inv_sigma2.reshape(1, freqs), offsets.T, owner_map.reshape(1, slots),
        center.reshape(1, pcount),
    )
    sums, loglik = pl.pallas_call(
        last_kernel,
        out_shape=(jax.ShapeDtypeStruct((2, 1, feat), F32), jax.ShapeDtypeStruct((1, pcount), F32)),
        in_specs=[vmem, vmem],
        out_specs=(vmem, vmem),
        compiler_params=pltpu.CompilerParams(vmem_limit_bytes=grant),
    )(partial, loglik)
    return sums, loglik.reshape(pcount)


def solution(mesh):
    return jax.shard_map(
        functools.partial(per_device, mesh.shape["dom"], mesh.shape["orient"]),
        mesh=mesh,
        in_specs=(P("dom", None), P("dom", "orient", None), P(), P(), P(), P("dom")),
        out_specs=(P("dom", "orient", None), P("dom")),
        check_vma=False,
    )
```

```python
import functools
import math

import jax
import jax.numpy as jnp
from jax import lax
from jax.experimental import pallas as pl
from jax.experimental.pallas import tpu as pltpu
from jax.sharding import PartitionSpec as P

BOX = 128
CHUNKS = 4
GROUPS = 4
PAIRS = CHUNKS // 2
RING = 4
NEG_FILL = -1e30
MESH = pl.DeviceIdType.MESH
BF16, F32 = jnp.bfloat16, jnp.float32


def unit_circle(phase):
    folded = ((phase + 64) & 127) - 64
    quarter = (folded + 16) >> 5
    x = (folded - quarter * 32).astype(F32) * (2.0 * math.pi / BOX)
    x2 = x * x
    sine = x * (1.0 + x2 * (-1 / 6 + x2 * (1 / 120 + x2 * (-1 / 5040 + x2 * (1 / 362880)))))
    cosine = 1.0 + x2 * (-0.5 + x2 * (1 / 24 + x2 * (-1 / 720 + x2 * (1 / 40320))))
    odd = (quarter & 1) == 1
    cos_sign = jnp.where(((quarter + 1) & 2) == 2, -1.0, 1.0)
    sin_sign = jnp.where((quarter & 2) == 2, -1.0, 1.0)
    return jnp.where(odd, sine, cosine) * cos_sign, jnp.where(odd, cosine, sine) * sin_sign


class Torus:
    def __init__(self):
        self.me = lax.axis_index("dom")
        self.core = lax.axis_index("orient") % 2
        self.y, self.x, self.z = self.me // 8, (self.me // 2) % 4, self.me % 2

    def turned(self, c):
        return (c + self.core) % 2

    def axes(self, c):
        odd = self.turned(c)
        return odd, self.y * (1 - odd) + self.x * odd, self.x * (1 - odd) + self.y * odd

    def peers(self):
        near = [device(0, self.y, self.x, 1 - self.z)]
        for by in (1, 2, 3):
            for z in (self.z, 1 - self.z):
                near.append(device(0, self.y, step(self.x, by), z))
                near.append(device(0, step(self.y, by), self.x, z))
        return near


def device(odd, v, u, z):
    return {"dom": ((v * (1 - odd) + u * odd) * 4 + u * (1 - odd) + v * odd) * 2 + z}


def step(a, by):
    return (a + by) % RING


def greet(barrier, to):
    pl.semaphore_signal(barrier, inc=1, device_id=to, device_id_type=MESH)


def send(src, dst, send_sem, recv_sem, to):
    pltpu.make_async_remote_copy(
        src_ref=src, dst_ref=dst, send_sem=send_sem, recv_sem=recv_sem, device_id=to, device_id_type=MESH
    ).start()


def wait(ref, sem):
    pltpu.make_async_copy(ref, ref, sem).wait()


def fetch_particles(part_hbm, part, part_sem, freqs, c):
    width = freqs // CHUNKS
    for base in (0, freqs):
        cols = pl.ds(base + c * width, width)
        pltpu.make_async_copy(part_hbm.at[:, cols], part.at[:, cols], part_sem.at[c]).start()


def exchange(perm, perm_t):
    there = lax.broadcasted_iota(jnp.int32, (128, 128), 0)
    here = lax.broadcasted_iota(jnp.int32, (128, 128), 1)
    for ref, out, src in ((perm, there, here), (perm_t, here, there)):
        q, s, r = src >> 4, (src >> 3) & 1, src & 7
        ref[...] = (out == r * 16 + q * 2 + s).astype(F32).astype(BF16)


def em_kernel(
    n_dom, n_ori, shifts,
    refs_hbm, part_hbm, inv_hbm, off_hbm, omap_hbm, center_hbm,
    recv2, loglik_ref,
    part, part_t, stage, mine, pieces, gath, perm, perm_t, cos_tab, sin_tab, lhs_a, lhs_b, acc, prods_a, prods_b, power,
    refs_ref, off_ref, inv_ref, omap_ref, center_ref, stat_out, stat_in, by_class, sends, near_in, send2,
    part_sem, small_sem, ag_send, ag_recv, ring_send, ag_ring, st_send, st_recv,
    rs_send, share_send, near_sem, rs_recv,
):
    freqs = inv_ref.shape[1]
    slots = 2 * n_dom
    lanes = mine.shape[3]
    width = freqs // CHUNKS
    half = 4
    here = Torus()
    axes, turned, my_z = here.axes, here.turned, here.z
    my_ori = lax.axis_index("orient")

    smalls = [
        pltpu.make_async_copy(src, dst, small_sem.at[k])
        for k, (src, dst) in enumerate((
            (refs_hbm, refs_ref), (off_hbm, off_ref), (inv_hbm, inv_ref), (omap_hbm, omap_ref), (center_hbm, center_ref)
        ))
    ]

    for copy in smalls:
        copy.start()

    barrier = pltpu.get_barrier_semaphore()
    peers = here.peers()
    for to in peers:
        greet(barrier, to)

    def greet_ori(i, carry):
        greet(barrier, {"orient": lax.rem(my_ori + i, n_ori)})
        return carry

    lax.fori_loop(1, n_ori, greet_ori, 0)
    smalls[0].wait()

    for c in range(CHUNKS):
        for r in range(2):
            for g in range(GROUPS):
                for j in range(lanes // 128):
                    at = r * freqs + c * width + g * lanes + j * 128
                    stage[j, pl.ds(c * 16 + g * 2 + r, 2, stride=8), :] = refs_ref[:, pl.ds(at, 128)].astype(F32)
        for j in range(lanes // 128):
            mine[c % 2, c // 2, :, pl.ds(j * 128, 128)] = stage[j, pl.ds(c * 16, 16), :].astype(BF16)

    pl.semaphore_wait(barrier, len(peers) + n_ori - 1)

    batches = ((0, 1), (1, 1))

    def gather0(b):
        for kind in range(2):
            odd, v, u = axes(kind)
            home = u * 2 + my_z
            ks = pl.ds(*batches[b])

            def share(i, carry):
                q = (home + i) % 8
                send(
                    mine.at[kind, ks], pieces.at[kind, home, ks], ag_send.at[b, kind], ag_recv.at[b, kind],
                    device(odd, v, q // 2, q % 2),
                )
                return carry

            lax.fori_loop(1, 8, share, 0)
            pieces[kind, home, ks] = mine[kind, ks]

    def gather0_wait(b):
        for kind in range(2):
            wait(pieces.at[kind, pl.ds(0, 7), pl.ds(*batches[b])], ag_recv.at[b, kind])

    def gather1(c):
        odd, v, u = axes(c)
        joined = jnp.dot(
            perm[...], pieces[c % 2, :, c // 2].reshape(128, lanes), preferred_element_type=F32
        ).astype(BF16)
        gath[c, v] = joined.reshape(8, 16, lanes)
        for h in range(2):
            block = gath.at[c, v, pl.ds(h * half, half)]
            for by in (2, 1, 3):
                send(block, block, ring_send.at[c], ag_ring.at[c, h], device(odd, step(v, by), u, my_z))

    def gather2(c, h):
        wait(gath.at[c, pl.ds(0, RING - 1), pl.ds(h * half, half)], ag_ring.at[c, h])

    def pair(k, stage):
        def one(i, carry):
            stage(2 * k + i)
            return carry

        lax.fori_loop(0, 2, one, 0)

    def turn_pair(k):
        for c in (2 * k, 2 * k + 1):
            wait(part.at[:, pl.ds(0, 2 * width)], part_sem.at[c])

        def turn(i, carry):
            at = pl.ds(pl.multiple_of(i // 4 * freqs + k * 2 * width + i % 4 * (width // 2), width // 2), width // 2)
            part_t[at, :] = part[:, at].T
            return carry

        lax.fori_loop(0, 8, turn, 0)

    gather0(0)
    gather0(1)
    for c in range(2):
        fetch_particles(part_hbm, part, part_sem, freqs, c)
    exchange(perm, perm_t)
    smalls[1].wait()

    shift_ids = lax.broadcasted_iota(jnp.int32, (shifts, 128), 0)
    off_x = jnp.zeros((shifts, 128), jnp.int32)
    off_y = jnp.zeros((shifts, 128), jnp.int32)
    for t in range(shifts):
        off_x = jnp.where(shift_ids == t, off_ref[0, t], off_x)
        off_y = jnp.where(shift_ids == t, off_ref[1, t], off_y)

    def tables(j, carry):
        for h in range(4):
            at = pl.multiple_of(j * 512 + h * 128, 128)
            freq = lax.broadcasted_iota(jnp.int32, (shifts, 128), 1) + at
            fx = freq & (BOX // 2 - 1)
            fy = freq >> 6
            fy = jnp.where(fy < BOX // 2, fy, fy - BOX)
            cosine, sine = unit_circle(off_x * fx + off_y * fy)
            cos_tab[:, pl.ds(at, 128)] = cosine
            sin_tab[:, pl.ds(at, 128)] = sine
        return carry

    lax.fori_loop(0, freqs // 1024, tables, 0)
    gather0_wait(0)
    pair(0, gather1)
    lax.fori_loop(freqs // 1024, freqs // 512, tables, 0)
    gather0_wait(1)
    pair(1, gather1)
    for c in range(2, CHUNKS):
        fetch_particles(part_hbm, part, part_sem, freqs, c)
    turn_pair(0)
    turn_pair(1)
    for copy in smalls[2:]:
        copy.wait()
    acc[...] = jnp.zeros_like(acc)
    power[...] = jnp.zeros_like(power)
    lhs_b[...] = jnp.zeros_like(lhs_b)

    def columns(group):
        at = pl.multiple_of(group * lanes, lanes)
        return pl.ds(at, lanes), pl.ds(pl.multiple_of(freqs + at, lanes), lanes)

    def score_product(lhs, c, half_chunk):
        at = pl.multiple_of((2 * c + half_chunk) * 2 * lanes, 2 * lanes)
        block = jnp.concatenate(
            [part_t[pl.ds(at, 2 * lanes), :], part_t[pl.ds(pl.multiple_of(freqs + at, 2 * lanes), 2 * lanes), :]], axis=0
        )
        for m in range(0, shifts * slots, shifts * slots // 2):
            rows = pl.ds(m, shifts * slots // 2)
            acc[turned(c), rows, :] += jnp.dot(lhs[rows, :], block, preferred_element_type=F32)

    def shift(lhs, c, g):
        for j in range(lanes // 128):
            at = pl.ds(j * 128, 128)
            col = g % 2 * lanes + j * 128
            there = pl.ds(pl.multiple_of((c * GROUPS + g) * lanes + j * 128, 128), 128)
            real = jnp.concatenate([gath[c, w, 2 * g, :, at] for w in range(RING)], axis=0).astype(F32)
            imag = jnp.concatenate([gath[c, w, 2 * g + 1, :, at] for w in range(RING)], axis=0).astype(F32)
            inv = inv_ref[:, there]
            re = real * inv
            im = imag * inv
            power[turned(c)] += re * real + im * imag
            for t in range(shifts):
                cosine = cos_tab[pl.ds(t, 1), there]
                sine = sin_tab[pl.ds(t, 1), there]
                into = lhs.at[pl.ds(t * slots, slots)]
                into[:, pl.ds(col, 128)] = (re * cosine + im * sine).astype(BF16)
                into[:, pl.ds(2 * lanes + col, 128)] = (im * cosine - re * sine).astype(BF16)

    def score_chunk(c, carry):
        gather2(c, 0)
        score_product(lhs_b, jnp.maximum(c - 1, 0), 1)
        shift(lhs_a, c, 0)
        shift(lhs_a, c, 1)
        gather2(c, 1)
        score_product(lhs_a, c, 0)
        shift(lhs_b, c, 2)
        shift(lhs_b, c, 3)

        return carry

    lax.fori_loop(0, CHUNKS, score_chunk, 0)
    score_product(lhs_b, CHUNKS - 1, 1)

    for base, ref in [(t * slots, acc) for t in range(shifts)] + [(0, power)]:
        for y in range(4):
            for x in range(4):
                ref[0, pl.ds(base + y * 16 + x * 4, 4), :] += ref[1, pl.ds(base + x * 16 + y * 4, 4), :]

    power_col = 0.5 * jnp.sum(power[0], axis=1, keepdims=True)
    distance = jnp.abs(my_ori - center_ref[...])
    allowed = jnp.minimum(distance, n_ori - distance) <= n_ori // 4
    best = None
    for t in range(shifts):
        at = pl.ds(t * slots, slots)
        value = jnp.where(allowed, acc[0, at, :] - power_col, NEG_FILL)
        acc[0, at, :] = value
        top = jnp.max(value, axis=0, keepdims=True)
        best = top if best is None else jnp.maximum(best, top)
    total = jnp.zeros_like(best)
    for t in range(shifts):
        at = pl.ds(t * slots, slots)
        value = jnp.exp(acc[0, at, :] - best)
        acc[0, at, :] = value
        total += jnp.sum(value, axis=0, keepdims=True)
    mine_best = best
    stat_out[0:1, :] = best
    stat_out[1:2, :] = total

    def stat_send(i, carry):
        send(stat_out, stat_in.at[my_ori], st_send, st_recv, {"orient": lax.rem(my_ori + i, n_ori)})
        return carry

    lax.fori_loop(1, n_ori, stat_send, 0)
    stat_in[my_ori] = stat_out[...]
    if n_ori > 1:
        others = stat_in.at[pl.ds(0, n_ori - 1)]
        wait(others, st_recv)
        wait(others, st_send)
    bests = [stat_in[o, 0:1, :] for o in range(n_ori)]
    best = functools.reduce(jnp.maximum, bests)
    total = sum(stat_in[o, 1:2, :] * jnp.exp(bests[o] - best) for o in range(n_ori))
    loglik_ref[...] = best + jnp.log(total)
    scale = jnp.exp(mine_best - best) / total

    pick = (lax.broadcasted_iota(jnp.int32, (slots, slots), 0) == omap_ref[...]).astype(F32).astype(BF16)
    weights = jnp.concatenate(
        [(acc[0, pl.ds(t * slots, slots), :] * scale).astype(BF16) for t in range(shifts)], axis=1
    )
    row = lax.broadcasted_iota(jnp.int32, (slots, slots), 1)
    swapped = ((row >> 2) & 3) * 16 + (row >> 4) * 4 + (row & 3)
    swap = (lax.broadcasted_iota(jnp.int32, (slots, slots), 0) == swapped).astype(F32).astype(BF16)
    picks = jnp.concatenate([pick, jnp.dot(pick, swap, preferred_element_type=F32).astype(BF16)], axis=1)
    picked = lax.dot_general(picks, weights, (((0,), (0,)), ((), ())), preferred_element_type=F32).astype(BF16)
    pcount = acc.shape[2]
    for odd in range(2):
        for t in range(shifts):
            by_class[odd, pl.ds(t * slots, slots), :] = picked[
                odd * slots:(odd + 1) * slots, t * pcount:(t + 1) * pcount
            ]

    def multiply(prods, group):
        block = jnp.concatenate([part[:, at] for at in columns(group)], axis=1)
        prods[...] = jnp.dot(by_class[turned(group // GROUPS)], block, preferred_element_type=F32)

    def rotate(prods, c, g):
        for j in range(lanes // 128):
            at = pl.ds(j * 128, 128)
            there = pl.ds(pl.multiple_of((c * GROUPS + g) * lanes + j * 128, 128), 128)
            out_real = out_imag = None
            for t in range(shifts):
                cosine = cos_tab[pl.ds(t, 1), there]
                sine = sin_tab[pl.ds(t, 1), there]
                re = prods[pl.ds(t * slots, slots), at]
                im = prods[pl.ds(t * slots, slots), pl.ds(lanes + j * 128, 128)]
                term_real = re * cosine - im * sine
                term_imag = im * cosine + re * sine
                out_real = term_real if t == 0 else out_real + term_real
                out_imag = term_imag if t == 0 else out_imag + term_imag
            for w in range(RING):
                sends[c, w, 2 * g, :, at] = out_real[w * 16:(w + 1) * 16].astype(BF16)
                sends[c, w, 2 * g + 1, :, at] = out_imag[w * 16:(w + 1) * 16].astype(BF16)

    def sum_half(c, h):
        first = c * GROUPS + 2 * h
        multiply(prods_b, first + 1)
        rotate(prods_a, c, 2 * h)
        multiply(prods_a, jnp.minimum(first + 2, CHUNKS * GROUPS - 1))
        rotate(prods_b, c, 2 * h + 1)

    def reduce0(c, h):
        odd, v, u = axes(c)
        part_of = pl.ds(h * half, half)
        for by in (2, 1, 3):
            w = step(v, by)
            send(
                sends.at[c, w, part_of], near_in.at[c, by - 1, part_of], rs_send.at[c], near_sem.at[c],
                device(odd, w, u, my_z),
            )

    def reduce1(c):
        odd, v, u = axes(c)
        wait(near_in.at[c], near_sem.at[c])
        total = sends[c, v].astype(F32)
        for k in range(RING - 1):
            total += near_in[c, k].astype(F32)
        apart = jnp.dot(
            perm_t[...], total.astype(BF16).reshape(128, lanes), preferred_element_type=F32
        ).astype(BF16)
        send2[c] = apart.reshape(8, 16, lanes)
        home = u * 2 + my_z

        def share(i, carry):
            q = (home + i) % 8
            send(send2.at[c, q], recv2.at[c, home], share_send.at[c], rs_recv.at[c], device(odd, v, q // 2, q % 2))
            return carry

        lax.fori_loop(1, 8, share, 0)
        recv2[c, home] = send2[c, home]

    def sum_step(i, carry):
        c, h = i // 2, i % 2
        sum_half(c, h)
        reduce0(c, h)

        @pl.when((h == 1) & (c >= 1))
        def _():
            reduce1(c - 1)

        return carry

    multiply(prods_a, 0)
    lax.fori_loop(0, 2 * CHUNKS, sum_step, 0)
    reduce1(CHUNKS - 1)

    for b in range(2):
        for odd in range(2):
            wait(pieces.at[odd, pl.ds(0, 7), pl.ds(*batches[b])], ag_send.at[b, odd])

    def drain(c, carry):
        wait(recv2.at[c, pl.ds(0, 7)], rs_recv.at[c])
        wait(gath.at[c, pl.ds(0, 3)], ring_send.at[c])
        wait(sends.at[c, pl.ds(0, 3)], rs_send.at[c])
        wait(send2.at[c, pl.ds(0, 7)], share_send.at[c])
        return carry

    lax.fori_loop(0, CHUNKS, drain, 0)


def last_kernel(recv2, loglik_in, out_ref, loglik_ref):
    lanes = recv2.shape[3]
    freqs = CHUNKS * GROUPS * lanes
    loglik_ref[...] = loglik_in[...]
    for c in range(CHUNKS):
        for j in range(lanes // 128):
            total = recv2[c, 0, :, pl.ds(j * 128, 128)].astype(F32)
            for q in range(1, 8):
                total += recv2[c, q, :, pl.ds(j * 128, 128)].astype(F32)
            for s in range(2):
                for r in range(2):
                    for g in range(GROUPS):
                        row = s * 8 + g * 2 + r
                        at = r * freqs + c * GROUPS * lanes + g * lanes + j * 128
                        out_ref[s, :, pl.ds(at, 128)] = total[row:row + 1, :]


def per_device(n_dom, n_ori, particles, refs, inv_sigma2, offsets, owner_map, center):
    pcount, feat = particles.shape
    freqs = feat // 2
    shifts = offsets.shape[0]
    slots = 2 * n_dom
    lanes = freqs // (CHUNKS * GROUPS)
    vmem = pl.BlockSpec(memory_space=pltpu.VMEM)
    far = pl.BlockSpec(memory_space=pltpu.HBM)
    dma = pltpu.SemaphoreType.DMA
    grant = 56 * 1024 * 1024
    partial, loglik = pl.pallas_call(
        functools.partial(em_kernel, n_dom, n_ori, shifts),
        out_shape=(
            jax.ShapeDtypeStruct((CHUNKS, 8, 16, lanes), BF16),
            jax.ShapeDtypeStruct((1, pcount), F32),
        ),
        in_specs=[far] * 6,
        out_specs=(vmem, vmem),
        scratch_shapes=[
            pltpu.VMEM((pcount, feat), BF16),
            pltpu.VMEM((feat, pcount), BF16),
            pltpu.VMEM((lanes // 128, 16 * CHUNKS, 128), F32),
            pltpu.VMEM((2, PAIRS, 16, lanes), BF16),
            pltpu.VMEM((2, 8, PAIRS, 16, lanes), BF16),
            pltpu.VMEM((CHUNKS, RING, 8, 16, lanes), BF16),
            pltpu.VMEM((128, 128), BF16),
            pltpu.VMEM((128, 128), BF16),
            pltpu.VMEM((shifts, freqs), F32),
            pltpu.VMEM((shifts, freqs), F32),
            pltpu.VMEM((shifts * slots, 4 * lanes), BF16),
            pltpu.VMEM((shifts * slots, 4 * lanes), BF16),
            pltpu.VMEM((2, shifts * slots, pcount), F32),
            pltpu.VMEM((shifts * slots, 2 * lanes), F32),
            pltpu.VMEM((shifts * slots, 2 * lanes), F32),
            pltpu.VMEM((2, slots, 128), F32),
            pltpu.VMEM((2, feat), BF16),
            pltpu.SMEM((2, shifts), jnp.int32),
            pltpu.VMEM((1, freqs), F32),
            pltpu.VMEM((1, slots), jnp.int32),
            pltpu.VMEM((1, pcount), jnp.int32),
            pltpu.VMEM((2, pcount), F32),
            pltpu.VMEM((n_ori, 2, pcount), F32),
            pltpu.VMEM((2, shifts * slots, pcount), BF16),
            pltpu.VMEM((CHUNKS, RING, 8, 16, lanes), BF16),
            pltpu.VMEM((CHUNKS, RING - 1, 8, 16, lanes), BF16),
            pltpu.VMEM((CHUNKS, 8, 16, lanes), BF16),
            dma((CHUNKS,)),
            dma((5,)),
            dma((2, 2)),
            dma((2, 2)),
            dma((CHUNKS,)),
            dma((CHUNKS, 2)),
            dma,
            dma,
            dma((CHUNKS,)),
            dma((CHUNKS,)),
            dma((CHUNKS,)),
            dma((CHUNKS,)),
        ],
        compiler_params=pltpu.CompilerParams(collective_id=0, has_side_effects=True, vmem_limit_bytes=grant),
        cost_estimate=pl.CostEstimate(
            flops=4 * shifts * slots * pcount * feat, bytes_accessed=2 * pcount * feat, transcendentals=0
        ),
    )(
        refs.reshape(2, feat), particles, inv_sigma2.reshape(1, freqs), offsets.T, owner_map.reshape(1, slots),
        center.reshape(1, pcount),
    )
    sums, loglik = pl.pallas_call(
        last_kernel,
        out_shape=(jax.ShapeDtypeStruct((2, 1, feat), F32), jax.ShapeDtypeStruct((1, pcount), F32)),
        in_specs=[vmem, vmem],
        out_specs=(vmem, vmem),
        compiler_params=pltpu.CompilerParams(vmem_limit_bytes=grant),
    )(partial, loglik)
    return sums, loglik.reshape(pcount)


def solution(mesh):
    return jax.shard_map(
        functools.partial(per_device, mesh.shape["dom"], mesh.shape["orient"]),
        mesh=mesh,
        in_specs=(P("dom", None), P("dom", "orient", None), P(), P(), P(), P("dom")),
        out_specs=(P("dom", "orient", None), P("dom")),
        check_vma=False,
    )
```

```python
import functools
import math

import jax
import jax.numpy as jnp
from jax import lax
from jax.experimental import pallas as pl
from jax.experimental.pallas import tpu as pltpu
from jax.sharding import PartitionSpec as P

BOX = 128
CHUNKS = 4
GROUPS = 4
PAIRS = CHUNKS // 2
RING = 4
NEG_FILL = -1e30
MESH = pl.DeviceIdType.MESH
BF16, F32 = jnp.bfloat16, jnp.float32


def unit_circle(phase):
    folded = ((phase + 64) & 127) - 64
    quarter = (folded + 16) >> 5
    x = (folded - quarter * 32).astype(F32) * (2.0 * math.pi / BOX)
    x2 = x * x
    sine = x * (1.0 + x2 * (-1 / 6 + x2 * (1 / 120 + x2 * (-1 / 5040 + x2 * (1 / 362880)))))
    cosine = 1.0 + x2 * (-0.5 + x2 * (1 / 24 + x2 * (-1 / 720 + x2 * (1 / 40320))))
    odd = (quarter & 1) == 1
    cos_sign = jnp.where(((quarter + 1) & 2) == 2, -1.0, 1.0)
    sin_sign = jnp.where((quarter & 2) == 2, -1.0, 1.0)
    return jnp.where(odd, sine, cosine) * cos_sign, jnp.where(odd, cosine, sine) * sin_sign


class Torus:
    def __init__(self):
        self.me = lax.axis_index("dom")
        self.core = lax.axis_index("orient") % 2
        self.y, self.x, self.z = self.me // 8, (self.me // 2) % 4, self.me % 2

    def turned(self, c):
        return (c + self.core) % 2

    def axes(self, c):
        odd = self.turned(c)
        return odd, self.y * (1 - odd) + self.x * odd, self.x * (1 - odd) + self.y * odd

    def peers(self):
        near = [device(0, self.y, self.x, 1 - self.z)]
        for by in (1, 2, 3):
            for z in (self.z, 1 - self.z):
                near.append(device(0, self.y, step(self.x, by), z))
                near.append(device(0, step(self.y, by), self.x, z))
        return near


def device(odd, v, u, z):
    return {"dom": ((v * (1 - odd) + u * odd) * 4 + u * (1 - odd) + v * odd) * 2 + z}


def step(a, by):
    return (a + by) % RING


def greet(barrier, to):
    pl.semaphore_signal(barrier, inc=1, device_id=to, device_id_type=MESH)


def send(src, dst, send_sem, recv_sem, to):
    pltpu.make_async_remote_copy(
        src_ref=src, dst_ref=dst, send_sem=send_sem, recv_sem=recv_sem, device_id=to, device_id_type=MESH
    ).start()


def wait(ref, sem):
    pltpu.make_async_copy(ref, ref, sem).wait()


def fetch_particles(part_hbm, part, part_sem, freqs, c):
    width = freqs // CHUNKS
    for base in (0, freqs):
        cols = pl.ds(base + c * width, width)
        pltpu.make_async_copy(part_hbm.at[:, cols], part.at[:, cols], part_sem.at[c]).start()


def exchange(perm, perm_t):
    there = lax.broadcasted_iota(jnp.int32, (128, 128), 0)
    here = lax.broadcasted_iota(jnp.int32, (128, 128), 1)
    for ref, out, src in ((perm, there, here), (perm_t, here, there)):
        q, s, r = src >> 4, (src >> 3) & 1, src & 7
        ref[...] = (out == r * 16 + q * 2 + s).astype(F32).astype(BF16)


def em_kernel(
    n_dom, n_ori, shifts,
    refs_hbm, part_hbm, inv_hbm, off_hbm, omap_hbm, center_hbm,
    recv2, loglik_ref,
    part, part_t, stage, mine, pieces, gath, perm, perm_t, cos_tab, sin_tab, lhs_a, lhs_b, acc, prods_a, prods_b, power,
    refs_ref, off_ref, inv_ref, omap_ref, center_ref, stat_out, stat_in, by_class, sends, near_in, send2,
    part_sem, small_sem, ag_send, ag_recv, ring_send, ag_ring, st_send, st_recv,
    rs_send, share_send, near_sem, rs_recv,
):
    freqs = inv_ref.shape[1]
    slots = 2 * n_dom
    lanes = mine.shape[3]
    width = freqs // CHUNKS
    half = 4
    here = Torus()
    axes, turned, my_z = here.axes, here.turned, here.z
    my_ori = lax.axis_index("orient")

    smalls = [
        pltpu.make_async_copy(src, dst, small_sem.at[k])
        for k, (src, dst) in enumerate((
            (refs_hbm, refs_ref), (off_hbm, off_ref), (inv_hbm, inv_ref), (omap_hbm, omap_ref), (center_hbm, center_ref)
        ))
    ]

    for copy in smalls:
        copy.start()

    barrier = pltpu.get_barrier_semaphore()
    peers = here.peers()
    for to in peers:
        greet(barrier, to)

    def greet_ori(i, carry):
        greet(barrier, {"orient": lax.rem(my_ori + i, n_ori)})
        return carry

    lax.fori_loop(1, n_ori, greet_ori, 0)
    smalls[0].wait()

    for c in range(CHUNKS):
        for r in range(2):
            for g in range(GROUPS):
                for j in range(lanes // 128):
                    at = r * freqs + c * width + g * lanes + j * 128
                    stage[j, pl.ds(c * 16 + g * 2 + r, 2, stride=8), :] = refs_ref[:, pl.ds(at, 128)].astype(F32)
        for j in range(lanes // 128):
            mine[c % 2, c // 2, :, pl.ds(j * 128, 128)] = stage[j, pl.ds(c * 16, 16), :].astype(BF16)

    pl.semaphore_wait(barrier, len(peers) + n_ori - 1)

    batches = ((0, 1), (1, 1))

    def gather0(b):
        for kind in range(2):
            odd, v, u = axes(kind)
            home = u * 2 + my_z
            ks = pl.ds(*batches[b])

            def share(i, carry):
                q = (home + i) % 8
                send(
                    mine.at[kind, ks], pieces.at[kind, home, ks], ag_send.at[b, kind], ag_recv.at[b, kind],
                    device(odd, v, q // 2, q % 2),
                )
                return carry

            lax.fori_loop(1, 8, share, 0)
            pieces[kind, home, ks] = mine[kind, ks]

    def gather0_wait(b):
        for kind in range(2):
            wait(pieces.at[kind, pl.ds(0, 7), pl.ds(*batches[b])], ag_recv.at[b, kind])

    def gather1(c):
        odd, v, u = axes(c)
        joined = jnp.dot(
            perm[...], pieces[c % 2, :, c // 2].reshape(128, lanes), preferred_element_type=F32
        ).astype(BF16)
        gath[c, v] = joined.reshape(8, 16, lanes)
        for h in range(2):
            block = gath.at[c, v, pl.ds(h * half, half)]
            for by in (2, 1, 3):
                send(block, block, ring_send.at[c], ag_ring.at[c, h], device(odd, step(v, by), u, my_z))

    def gather2(c, h):
        wait(gath.at[c, pl.ds(0, RING - 1), pl.ds(h * half, half)], ag_ring.at[c, h])

    def pair(k, stage):
        def one(i, carry):
            stage(2 * k + i)
            return carry

        lax.fori_loop(0, 2, one, 0)

    def turn_pair(k):
        for c in (2 * k, 2 * k + 1):
            wait(part.at[:, pl.ds(0, 2 * width)], part_sem.at[c])

        def turn(i, carry):
            at = pl.ds(pl.multiple_of(i // 4 * freqs + k * 2 * width + i % 4 * (width // 2), width // 2), width // 2)
            part_t[at, :] = part[:, at].T
            return carry

        lax.fori_loop(0, 8, turn, 0)

    gather0(0)
    gather0(1)
    for c in range(2):
        fetch_particles(part_hbm, part, part_sem, freqs, c)
    exchange(perm, perm_t)
    smalls[1].wait()

    shift_ids = lax.broadcasted_iota(jnp.int32, (shifts, 128), 0)
    off_x = jnp.zeros((shifts, 128), jnp.int32)
    off_y = jnp.zeros((shifts, 128), jnp.int32)
    for t in range(shifts):
        off_x = jnp.where(shift_ids == t, off_ref[0, t], off_x)
        off_y = jnp.where(shift_ids == t, off_ref[1, t], off_y)

    def tables(j, carry):
        for h in range(4):
            at = pl.multiple_of(j * 512 + h * 128, 128)
            freq = lax.broadcasted_iota(jnp.int32, (shifts, 128), 1) + at
            fx = freq & (BOX // 2 - 1)
            fy = freq >> 6
            fy = jnp.where(fy < BOX // 2, fy, fy - BOX)
            cosine, sine = unit_circle(off_x * fx + off_y * fy)
            cos_tab[:, pl.ds(at, 128)] = cosine
            sin_tab[:, pl.ds(at, 128)] = sine
        return carry

    lax.fori_loop(0, freqs // 1024, tables, 0)
    gather0_wait(0)
    pair(0, gather1)
    lax.fori_loop(freqs // 1024, freqs // 512, tables, 0)
    gather0_wait(1)
    pair(1, gather1)
    for c in range(2, CHUNKS):
        fetch_particles(part_hbm, part, part_sem, freqs, c)
    turn_pair(0)
    for copy in smalls[2:]:
        copy.wait()
    acc[...] = jnp.zeros_like(acc)
    power[...] = jnp.zeros_like(power)
    lhs_b[...] = jnp.zeros_like(lhs_b)

    def columns(group):
        at = pl.multiple_of(group * lanes, lanes)
        return pl.ds(at, lanes), pl.ds(pl.multiple_of(freqs + at, lanes), lanes)

    def score_product(lhs, c, half_chunk):
        at = pl.multiple_of((2 * c + half_chunk) * 2 * lanes, 2 * lanes)
        block = jnp.concatenate(
            [part_t[pl.ds(at, 2 * lanes), :], part_t[pl.ds(pl.multiple_of(freqs + at, 2 * lanes), 2 * lanes), :]], axis=0
        )
        for m in range(0, shifts * slots, shifts * slots // 2):
            rows = pl.ds(m, shifts * slots // 2)
            acc[turned(c), rows, :] += jnp.dot(lhs[rows, :], block, preferred_element_type=F32)

    def shift(lhs, c, g):
        for j in range(lanes // 128):
            at = pl.ds(j * 128, 128)
            col = g % 2 * lanes + j * 128
            there = pl.ds(pl.multiple_of((c * GROUPS + g) * lanes + j * 128, 128), 128)
            real = jnp.concatenate([gath[c, w, 2 * g, :, at] for w in range(RING)], axis=0).astype(F32)
            imag = jnp.concatenate([gath[c, w, 2 * g + 1, :, at] for w in range(RING)], axis=0).astype(F32)
            inv = inv_ref[:, there]
            re = real * inv
            im = imag * inv
            power[turned(c)] += re * real + im * imag
            for t in range(shifts):
                cosine = cos_tab[pl.ds(t, 1), there]
                sine = sin_tab[pl.ds(t, 1), there]
                into = lhs.at[pl.ds(t * slots, slots)]
                into[:, pl.ds(col, 128)] = (re * cosine + im * sine).astype(BF16)
                into[:, pl.ds(2 * lanes + col, 128)] = (im * cosine - re * sine).astype(BF16)

    def score_chunk(c, carry):
        score_product(lhs_b, jnp.maximum(c - 1, 0), 1)
        gather2(c, 0)
        shift(lhs_a, c, 0)
        shift(lhs_a, c, 1)
        score_product(lhs_a, c, 0)
        gather2(c, 1)
        shift(lhs_b, c, 2)
        shift(lhs_b, c, 3)

        @pl.when(c == 1)
        def _():
            turn_pair(1)

        return carry

    lax.fori_loop(0, CHUNKS, score_chunk, 0)
    score_product(lhs_b, CHUNKS - 1, 1)

    for base, ref in [(t * slots, acc) for t in range(shifts)] + [(0, power)]:
        for y in range(4):
            for x in range(4):
                ref[0, pl.ds(base + y * 16 + x * 4, 4), :] += ref[1, pl.ds(base + x * 16 + y * 4, 4), :]

    power_col = 0.5 * jnp.sum(power[0], axis=1, keepdims=True)
    distance = jnp.abs(my_ori - center_ref[...])
    allowed = jnp.minimum(distance, n_ori - distance) <= n_ori // 4
    best = None
    for t in range(shifts):
        at = pl.ds(t * slots, slots)
        value = jnp.where(allowed, acc[0, at, :] - power_col, NEG_FILL)
        acc[0, at, :] = value
        top = jnp.max(value, axis=0, keepdims=True)
        best = top if best is None else jnp.maximum(best, top)
    total = jnp.zeros_like(best)
    for t in range(shifts):
        at = pl.ds(t * slots, slots)
        value = jnp.exp(acc[0, at, :] - best)
        acc[0, at, :] = value
        total += jnp.sum(value, axis=0, keepdims=True)
    mine_best = best
    stat_out[0:1, :] = best
    stat_out[1:2, :] = total

    def stat_send(i, carry):
        send(stat_out, stat_in.at[my_ori], st_send, st_recv, {"orient": lax.rem(my_ori + i, n_ori)})
        return carry

    lax.fori_loop(1, n_ori, stat_send, 0)
    stat_in[my_ori] = stat_out[...]
    pick = (lax.broadcasted_iota(jnp.int32, (slots, slots), 0) == omap_ref[...]).astype(F32).astype(BF16)
    row = lax.broadcasted_iota(jnp.int32, (slots, slots), 1)
    swapped = ((row >> 2) & 3) * 16 + (row >> 4) * 4 + (row & 3)
    swap = (lax.broadcasted_iota(jnp.int32, (slots, slots), 0) == swapped).astype(F32).astype(BF16)
    picks = jnp.concatenate([pick, jnp.dot(pick, swap, preferred_element_type=F32).astype(BF16)], axis=1)
    if n_ori > 1:
        others = stat_in.at[pl.ds(0, n_ori - 1)]
        wait(others, st_recv)
        wait(others, st_send)
    bests = [stat_in[o, 0:1, :] for o in range(n_ori)]
    best = functools.reduce(jnp.maximum, bests)
    total = sum(stat_in[o, 1:2, :] * jnp.exp(bests[o] - best) for o in range(n_ori))
    loglik_ref[...] = best + jnp.log(total)
    scale = jnp.exp(mine_best - best) / total

    weights = jnp.concatenate(
        [(acc[0, pl.ds(t * slots, slots), :] * scale).astype(BF16) for t in range(shifts)], axis=1
    )
    picked = lax.dot_general(picks, weights, (((0,), (0,)), ((), ())), preferred_element_type=F32).astype(BF16)
    pcount = acc.shape[2]
    for odd in range(2):
        for t in range(shifts):
            by_class[odd, pl.ds(t * slots, slots), :] = picked[
                odd * slots:(odd + 1) * slots, t * pcount:(t + 1) * pcount
            ]

    def multiply(prods, group):
        block = jnp.concatenate([part[:, at] for at in columns(group)], axis=1)
        prods[...] = jnp.dot(by_class[turned(group // GROUPS)], block, preferred_element_type=F32)

    def rotate(prods, c, g):
        for j in range(lanes // 128):
            at = pl.ds(j * 128, 128)
            there = pl.ds(pl.multiple_of((c * GROUPS + g) * lanes + j * 128, 128), 128)
            out_real = out_imag = None
            for t in range(shifts):
                cosine = cos_tab[pl.ds(t, 1), there]
                sine = sin_tab[pl.ds(t, 1), there]
                re = prods[pl.ds(t * slots, slots), at]
                im = prods[pl.ds(t * slots, slots), pl.ds(lanes + j * 128, 128)]
                term_real = re * cosine - im * sine
                term_imag = im * cosine + re * sine
                out_real = term_real if t == 0 else out_real + term_real
                out_imag = term_imag if t == 0 else out_imag + term_imag
            for w in range(RING):
                sends[c, w, 2 * g, :, at] = out_real[w * 16:(w + 1) * 16].astype(BF16)
                sends[c, w, 2 * g + 1, :, at] = out_imag[w * 16:(w + 1) * 16].astype(BF16)

    def sum_half(c, h):
        first = c * GROUPS + 2 * h
        multiply(prods_b, first + 1)
        rotate(prods_a, c, 2 * h)
        multiply(prods_a, jnp.minimum(first + 2, CHUNKS * GROUPS - 1))
        rotate(prods_b, c, 2 * h + 1)

    def reduce0(c, h):
        odd, v, u = axes(c)
        part_of = pl.ds(h * half, half)
        for by in (2, 1, 3):
            w = step(v, by)
            send(
                sends.at[c, w, part_of], near_in.at[c, by - 1, part_of], rs_send.at[c], near_sem.at[c],
                device(odd, w, u, my_z),
            )

    def reduce1(c):
        odd, v, u = axes(c)
        wait(near_in.at[c], near_sem.at[c])
        total = sends[c, v].astype(F32)
        for k in range(RING - 1):
            total += near_in[c, k].astype(F32)
        apart = jnp.dot(
            perm_t[...], total.astype(BF16).reshape(128, lanes), preferred_element_type=F32
        ).astype(BF16)
        send2[c] = apart.reshape(8, 16, lanes)
        home = u * 2 + my_z

        def share(i, carry):
            q = (home + i) % 8
            send(send2.at[c, q], recv2.at[c, home], share_send.at[c], rs_recv.at[c], device(odd, v, q // 2, q % 2))
            return carry

        lax.fori_loop(1, 8, share, 0)
        recv2[c, home] = send2[c, home]

    def sum_step(i, carry):
        c, h = i // 2, i % 2
        sum_half(c, h)
        reduce0(c, h)

        @pl.when((h == 1) & (c >= 1))
        def _():
            reduce1(c - 1)

        return carry

    multiply(prods_a, 0)
    lax.fori_loop(0, 2 * CHUNKS, sum_step, 0)
    reduce1(CHUNKS - 1)

    for b in range(2):
        for odd in range(2):
            wait(pieces.at[odd, pl.ds(0, 7), pl.ds(*batches[b])], ag_send.at[b, odd])

    def drain(c, carry):
        wait(recv2.at[c, pl.ds(0, 7)], rs_recv.at[c])
        wait(gath.at[c, pl.ds(0, 3)], ring_send.at[c])
        wait(sends.at[c, pl.ds(0, 3)], rs_send.at[c])
        wait(send2.at[c, pl.ds(0, 7)], share_send.at[c])
        return carry

    lax.fori_loop(0, CHUNKS, drain, 0)


def last_kernel(recv2, loglik_in, out_ref, loglik_ref):
    lanes = recv2.shape[3]
    freqs = CHUNKS * GROUPS * lanes
    loglik_ref[...] = loglik_in[...]
    for c in range(CHUNKS):
        for j in range(lanes // 128):
            total = recv2[c, 0, :, pl.ds(j * 128, 128)].astype(F32)
            for q in range(1, 8):
                total += recv2[c, q, :, pl.ds(j * 128, 128)].astype(F32)
            for s in range(2):
                for r in range(2):
                    for g in range(GROUPS):
                        row = s * 8 + g * 2 + r
                        at = r * freqs + c * GROUPS * lanes + g * lanes + j * 128
                        out_ref[s, :, pl.ds(at, 128)] = total[row:row + 1, :]


def per_device(n_dom, n_ori, particles, refs, inv_sigma2, offsets, owner_map, center):
    pcount, feat = particles.shape
    freqs = feat // 2
    shifts = offsets.shape[0]
    slots = 2 * n_dom
    lanes = freqs // (CHUNKS * GROUPS)
    vmem = pl.BlockSpec(memory_space=pltpu.VMEM)
    far = pl.BlockSpec(memory_space=pltpu.HBM)
    dma = pltpu.SemaphoreType.DMA
    grant = 56 * 1024 * 1024
    partial, loglik = pl.pallas_call(
        functools.partial(em_kernel, n_dom, n_ori, shifts),
        out_shape=(
            jax.ShapeDtypeStruct((CHUNKS, 8, 16, lanes), BF16),
            jax.ShapeDtypeStruct((1, pcount), F32),
        ),
        in_specs=[far] * 6,
        out_specs=(vmem, vmem),
        scratch_shapes=[
            pltpu.VMEM((pcount, feat), BF16),
            pltpu.VMEM((feat, pcount), BF16),
            pltpu.VMEM((lanes // 128, 16 * CHUNKS, 128), F32),
            pltpu.VMEM((2, PAIRS, 16, lanes), BF16),
            pltpu.VMEM((2, 8, PAIRS, 16, lanes), BF16),
            pltpu.VMEM((CHUNKS, RING, 8, 16, lanes), BF16),
            pltpu.VMEM((128, 128), BF16),
            pltpu.VMEM((128, 128), BF16),
            pltpu.VMEM((shifts, freqs), F32),
            pltpu.VMEM((shifts, freqs), F32),
            pltpu.VMEM((shifts * slots, 4 * lanes), BF16),
            pltpu.VMEM((shifts * slots, 4 * lanes), BF16),
            pltpu.VMEM((2, shifts * slots, pcount), F32),
            pltpu.VMEM((shifts * slots, 2 * lanes), F32),
            pltpu.VMEM((shifts * slots, 2 * lanes), F32),
            pltpu.VMEM((2, slots, 128), F32),
            pltpu.VMEM((2, feat), BF16),
            pltpu.SMEM((2, shifts), jnp.int32),
            pltpu.VMEM((1, freqs), F32),
            pltpu.VMEM((1, slots), jnp.int32),
            pltpu.VMEM((1, pcount), jnp.int32),
            pltpu.VMEM((2, pcount), F32),
            pltpu.VMEM((n_ori, 2, pcount), F32),
            pltpu.VMEM((2, shifts * slots, pcount), BF16),
            pltpu.VMEM((CHUNKS, RING, 8, 16, lanes), BF16),
            pltpu.VMEM((CHUNKS, RING - 1, 8, 16, lanes), BF16),
            pltpu.VMEM((CHUNKS, 8, 16, lanes), BF16),
            dma((CHUNKS,)),
            dma((5,)),
            dma((2, 2)),
            dma((2, 2)),
            dma((CHUNKS,)),
            dma((CHUNKS, 2)),
            dma,
            dma,
            dma((CHUNKS,)),
            dma((CHUNKS,)),
            dma((CHUNKS,)),
            dma((CHUNKS,)),
        ],
        compiler_params=pltpu.CompilerParams(collective_id=0, has_side_effects=True, vmem_limit_bytes=grant),
        cost_estimate=pl.CostEstimate(
            flops=4 * shifts * slots * pcount * feat, bytes_accessed=2 * pcount * feat, transcendentals=0
        ),
    )(
        refs.reshape(2, feat), particles, inv_sigma2.reshape(1, freqs), offsets.T, owner_map.reshape(1, slots),
        center.reshape(1, pcount),
    )
    sums, loglik = pl.pallas_call(
        last_kernel,
        out_shape=(jax.ShapeDtypeStruct((2, 1, feat), F32), jax.ShapeDtypeStruct((1, pcount), F32)),
        in_specs=[vmem, vmem],
        out_specs=(vmem, vmem),
        compiler_params=pltpu.CompilerParams(vmem_limit_bytes=grant),
    )(partial, loglik)
    return sums, loglik.reshape(pcount)


def solution(mesh):
    return jax.shard_map(
        functools.partial(per_device, mesh.shape["dom"], mesh.shape["orient"]),
        mesh=mesh,
        in_specs=(P("dom", None), P("dom", "orient", None), P(), P(), P(), P("dom")),
        out_specs=(P("dom", "orient", None), P("dom")),
        check_vma=False,
    )
```

```python
import functools
import math

import jax
import jax.numpy as jnp
from jax import lax
from jax.experimental import pallas as pl
from jax.experimental.pallas import tpu as pltpu
from jax.sharding import PartitionSpec as P

BOX = 128
CHUNKS = 4
GROUPS = 4
PAIRS = CHUNKS // 2
RING = 4
NEG_FILL = -1e30
MESH = pl.DeviceIdType.MESH
BF16, F32 = jnp.bfloat16, jnp.float32


def unit_circle(phase):
    folded = ((phase + 64) & 127) - 64
    quarter = (folded + 16) >> 5
    x = (folded - quarter * 32).astype(F32) * (2.0 * math.pi / BOX)
    x2 = x * x
    sine = x * (1.0 + x2 * (-1 / 6 + x2 * (1 / 120 + x2 * (-1 / 5040 + x2 * (1 / 362880)))))
    cosine = 1.0 + x2 * (-0.5 + x2 * (1 / 24 + x2 * (-1 / 720 + x2 * (1 / 40320))))
    odd = (quarter & 1) == 1
    cos_sign = jnp.where(((quarter + 1) & 2) == 2, -1.0, 1.0)
    sin_sign = jnp.where((quarter & 2) == 2, -1.0, 1.0)
    return jnp.where(odd, sine, cosine) * cos_sign, jnp.where(odd, cosine, sine) * sin_sign


class Torus:
    def __init__(self):
        self.me = lax.axis_index("dom")
        self.core = lax.axis_index("orient") % 2
        self.y, self.x, self.z = self.me // 8, (self.me // 2) % 4, self.me % 2

    def turned(self, c):
        return (c + self.core) % 2

    def axes(self, c):
        odd = self.turned(c)
        return odd, self.y * (1 - odd) + self.x * odd, self.x * (1 - odd) + self.y * odd

    def peers(self):
        near = [device(0, self.y, self.x, 1 - self.z)]
        for by in (1, 2, 3):
            for z in (self.z, 1 - self.z):
                near.append(device(0, self.y, step(self.x, by), z))
                near.append(device(0, step(self.y, by), self.x, z))
        return near


def device(odd, v, u, z):
    return {"dom": ((v * (1 - odd) + u * odd) * 4 + u * (1 - odd) + v * odd) * 2 + z}


def step(a, by):
    return (a + by) % RING


def greet(barrier, to):
    pl.semaphore_signal(barrier, inc=1, device_id=to, device_id_type=MESH)


def send(src, dst, send_sem, recv_sem, to):
    pltpu.make_async_remote_copy(
        src_ref=src, dst_ref=dst, send_sem=send_sem, recv_sem=recv_sem, device_id=to, device_id_type=MESH
    ).start()


def wait(ref, sem):
    pltpu.make_async_copy(ref, ref, sem).wait()


def fetch_particles(part_hbm, part, part_sem, freqs, c):
    width = freqs // CHUNKS
    for base in (0, freqs):
        cols = pl.ds(base + c * width, width)
        pltpu.make_async_copy(part_hbm.at[:, cols], part.at[:, cols], part_sem.at[c]).start()


def exchange(perm, perm_t):
    there = lax.broadcasted_iota(jnp.int32, (128, 128), 0)
    here = lax.broadcasted_iota(jnp.int32, (128, 128), 1)
    for ref, out, src in ((perm, there, here), (perm_t, here, there)):
        q, s, r = src >> 4, (src >> 3) & 1, src & 7
        ref[...] = (out == r * 16 + q * 2 + s).astype(F32).astype(BF16)


def em_kernel(
    n_dom, n_ori, shifts,
    refs_hbm, part_hbm, inv_hbm, off_hbm, omap_hbm, center_hbm,
    recv2, loglik_ref,
    part, stage, mine, pieces, gath, perm, perm_t, cos_tab, sin_tab, lhs_a, lhs_b, acc, prods_a, prods_b, power,
    refs_ref, off_ref, inv_ref, omap_ref, center_ref, stat_out, stat_in, by_class, sends, near_in, send2,
    part_sem, small_sem, ag_send, ag_recv, ring_send, ag_ring, st_send, st_recv,
    rs_send, share_send, near_sem, rs_recv,
):
    freqs = inv_ref.shape[1]
    slots = 2 * n_dom
    lanes = mine.shape[3]
    width = freqs // CHUNKS
    half = 4
    here = Torus()
    axes, turned, my_z = here.axes, here.turned, here.z
    my_ori = lax.axis_index("orient")

    smalls = [
        pltpu.make_async_copy(src, dst, small_sem.at[k])
        for k, (src, dst) in enumerate((
            (refs_hbm, refs_ref), (off_hbm, off_ref), (inv_hbm, inv_ref), (omap_hbm, omap_ref), (center_hbm, center_ref)
        ))
    ]

    for copy in smalls:
        copy.start()

    barrier = pltpu.get_barrier_semaphore()
    peers = here.peers()
    for to in peers:
        greet(barrier, to)

    def greet_ori(i, carry):
        greet(barrier, {"orient": lax.rem(my_ori + i, n_ori)})
        return carry

    lax.fori_loop(1, n_ori, greet_ori, 0)
    smalls[0].wait()

    for c in range(CHUNKS):
        for r in range(2):
            for g in range(GROUPS):
                for j in range(lanes // 128):
                    at = r * freqs + c * width + g * lanes + j * 128
                    stage[j, pl.ds(c * 16 + g * 2 + r, 2, stride=8), :] = refs_ref[:, pl.ds(at, 128)].astype(F32)
        for j in range(lanes // 128):
            mine[c % 2, c // 2, :, pl.ds(j * 128, 128)] = stage[j, pl.ds(c * 16, 16), :].astype(BF16)

    pl.semaphore_wait(barrier, len(peers) + n_ori - 1)

    batches = ((0, 1), (1, 1))

    def gather0(b):
        for kind in range(2):
            odd, v, u = axes(kind)
            home = u * 2 + my_z
            ks = pl.ds(*batches[b])

            def share(i, carry):
                q = (home + i) % 8
                send(
                    mine.at[kind, ks], pieces.at[kind, home, ks], ag_send.at[b, kind], ag_recv.at[b, kind],
                    device(odd, v, q // 2, q % 2),
                )
                return carry

            lax.fori_loop(1, 8, share, 0)
            pieces[kind, home, ks] = mine[kind, ks]

    def gather0_wait(b):
        for kind in range(2):
            wait(pieces.at[kind, pl.ds(0, 7), pl.ds(*batches[b])], ag_recv.at[b, kind])

    def gather1(c):
        odd, v, u = axes(c)
        joined = jnp.dot(
            perm[...], pieces[c % 2, :, c // 2].reshape(128, lanes), preferred_element_type=F32
        ).astype(BF16)
        gath[c, v] = joined.reshape(8, 16, lanes)
        for h in range(2):
            block = gath.at[c, v, pl.ds(h * half, half)]
            for by in (2, 1, 3):
                send(block, block, ring_send.at[c], ag_ring.at[c, h], device(odd, step(v, by), u, my_z))

    def gather2(c, h):
        wait(gath.at[c, pl.ds(0, RING - 1), pl.ds(h * half, half)], ag_ring.at[c, h])

    def pair(k, stage):
        def one(i, carry):
            stage(2 * k + i)
            return carry

        lax.fori_loop(0, 2, one, 0)

    gather0(0)
    gather0(1)
    for c in range(2):
        fetch_particles(part_hbm, part, part_sem, freqs, c)
    exchange(perm, perm_t)
    smalls[1].wait()

    shift_ids = lax.broadcasted_iota(jnp.int32, (shifts, 128), 0)
    off_x = jnp.zeros((shifts, 128), jnp.int32)
    off_y = jnp.zeros((shifts, 128), jnp.int32)
    for t in range(shifts):
        off_x = jnp.where(shift_ids == t, off_ref[0, t], off_x)
        off_y = jnp.where(shift_ids == t, off_ref[1, t], off_y)

    def tables(j, carry):
        for h in range(4):
            at = pl.multiple_of(j * 512 + h * 128, 128)
            freq = lax.broadcasted_iota(jnp.int32, (shifts, 128), 1) + at
            fx = freq & (BOX // 2 - 1)
            fy = freq >> 6
            fy = jnp.where(fy < BOX // 2, fy, fy - BOX)
            cosine, sine = unit_circle(off_x * fx + off_y * fy)
            cos_tab[:, pl.ds(at, 128)] = cosine
            sin_tab[:, pl.ds(at, 128)] = sine
        return carry

    lax.fori_loop(0, freqs // 1024, tables, 0)
    gather0_wait(0)
    pair(0, gather1)
    lax.fori_loop(freqs // 1024, freqs // 512, tables, 0)
    gather0_wait(1)
    pair(1, gather1)
    for c in range(2, CHUNKS):
        fetch_particles(part_hbm, part, part_sem, freqs, c)
    for copy in smalls[2:]:
        copy.wait()
    acc[...] = jnp.zeros_like(acc)
    power[...] = jnp.zeros_like(power)
    lhs_b[...] = jnp.zeros_like(lhs_b)

    def columns(group):
        at = pl.multiple_of(group * lanes, lanes)
        return pl.ds(at, lanes), pl.ds(pl.multiple_of(freqs + at, lanes), lanes)

    def score_product(lhs, c, half_chunk):
        at = pl.multiple_of((2 * c + half_chunk) * 2 * lanes, 2 * lanes)
        block = jnp.concatenate(
            [part[:, pl.ds(at, 2 * lanes)], part[:, pl.ds(pl.multiple_of(freqs + at, 2 * lanes), 2 * lanes)]], axis=1
        )
        for m in range(0, shifts * slots, shifts * slots // 2):
            rows = pl.ds(m, shifts * slots // 2)
            acc[turned(c), rows, :] += lax.dot_general(
                lhs[rows, :], block, (((1,), (1,)), ((), ())), preferred_element_type=F32
            )

    def shift(lhs, c, g):
        for j in range(lanes // 128):
            at = pl.ds(j * 128, 128)
            col = g % 2 * lanes + j * 128
            there = pl.ds(pl.multiple_of((c * GROUPS + g) * lanes + j * 128, 128), 128)
            real = jnp.concatenate([gath[c, w, 2 * g, :, at] for w in range(RING)], axis=0).astype(F32)
            imag = jnp.concatenate([gath[c, w, 2 * g + 1, :, at] for w in range(RING)], axis=0).astype(F32)
            inv = inv_ref[:, there]
            re = real * inv
            im = imag * inv
            power[turned(c)] += re * real + im * imag
            for t in range(shifts):
                cosine = cos_tab[pl.ds(t, 1), there]
                sine = sin_tab[pl.ds(t, 1), there]
                into = lhs.at[pl.ds(t * slots, slots)]
                into[:, pl.ds(col, 128)] = (re * cosine + im * sine).astype(BF16)
                into[:, pl.ds(2 * lanes + col, 128)] = (im * cosine - re * sine).astype(BF16)

    def score_chunk(c, carry):
        wait(part.at[:, pl.ds(0, 2 * width)], part_sem.at[c])
        score_product(lhs_b, jnp.maximum(c - 1, 0), 1)
        gather2(c, 0)
        shift(lhs_a, c, 0)
        shift(lhs_a, c, 1)
        score_product(lhs_a, c, 0)
        gather2(c, 1)
        shift(lhs_b, c, 2)
        shift(lhs_b, c, 3)

        return carry

    lax.fori_loop(0, CHUNKS, score_chunk, 0)
    score_product(lhs_b, CHUNKS - 1, 1)

    for base, ref in [(t * slots, acc) for t in range(shifts)] + [(0, power)]:
        for y in range(4):
            for x in range(4):
                ref[0, pl.ds(base + y * 16 + x * 4, 4), :] += ref[1, pl.ds(base + x * 16 + y * 4, 4), :]

    power_col = 0.5 * jnp.sum(power[0], axis=1, keepdims=True)
    distance = jnp.abs(my_ori - center_ref[...])
    allowed = jnp.minimum(distance, n_ori - distance) <= n_ori // 4
    best = None
    for t in range(shifts):
        at = pl.ds(t * slots, slots)
        value = jnp.where(allowed, acc[0, at, :] - power_col, NEG_FILL)
        acc[0, at, :] = value
        top = jnp.max(value, axis=0, keepdims=True)
        best = top if best is None else jnp.maximum(best, top)
    total = jnp.zeros_like(best)
    for t in range(shifts):
        at = pl.ds(t * slots, slots)
        value = jnp.exp(acc[0, at, :] - best)
        acc[0, at, :] = value
        total += jnp.sum(value, axis=0, keepdims=True)
    mine_best = best
    stat_out[0:1, :] = best
    stat_out[1:2, :] = total

    def stat_send(i, carry):
        send(stat_out, stat_in.at[my_ori], st_send, st_recv, {"orient": lax.rem(my_ori + i, n_ori)})
        return carry

    lax.fori_loop(1, n_ori, stat_send, 0)
    stat_in[my_ori] = stat_out[...]
    pick = (lax.broadcasted_iota(jnp.int32, (slots, slots), 0) == omap_ref[...]).astype(F32).astype(BF16)
    row = lax.broadcasted_iota(jnp.int32, (slots, slots), 1)
    swapped = ((row >> 2) & 3) * 16 + (row >> 4) * 4 + (row & 3)
    swap = (lax.broadcasted_iota(jnp.int32, (slots, slots), 0) == swapped).astype(F32).astype(BF16)
    picks = jnp.concatenate([pick, jnp.dot(pick, swap, preferred_element_type=F32).astype(BF16)], axis=1)
    for b in range(2):
        for kind in range(2):
            wait(pieces.at[kind, pl.ds(0, 7), pl.ds(*batches[b])], ag_send.at[b, kind])
    for c in range(CHUNKS):
        wait(gath.at[c, pl.ds(0, RING - 1)], ring_send.at[c])
    if n_ori > 1:
        others = stat_in.at[pl.ds(0, n_ori - 1)]
        wait(others, st_recv)
        wait(others, st_send)
    bests = [stat_in[o, 0:1, :] for o in range(n_ori)]
    best = functools.reduce(jnp.maximum, bests)
    total = sum(stat_in[o, 1:2, :] * jnp.exp(bests[o] - best) for o in range(n_ori))
    loglik_ref[...] = best + jnp.log(total)
    scale = jnp.exp(mine_best - best) / total

    weights = jnp.concatenate(
        [(acc[0, pl.ds(t * slots, slots), :] * scale).astype(BF16) for t in range(shifts)], axis=1
    )
    picked = lax.dot_general(picks, weights, (((0,), (0,)), ((), ())), preferred_element_type=F32).astype(BF16)
    pcount = acc.shape[2]
    for odd in range(2):
        for t in range(shifts):
            by_class[odd, pl.ds(t * slots, slots), :] = picked[
                odd * slots:(odd + 1) * slots, t * pcount:(t + 1) * pcount
            ]

    def multiply(prods, group):
        block = jnp.concatenate([part[:, at] for at in columns(group)], axis=1)
        prods[...] = jnp.dot(by_class[turned(group // GROUPS)], block, preferred_element_type=F32)

    def rotate(prods, c, g):
        for j in range(lanes // 128):
            at = pl.ds(j * 128, 128)
            there = pl.ds(pl.multiple_of((c * GROUPS + g) * lanes + j * 128, 128), 128)
            out_real = out_imag = None
            for t in range(shifts):
                cosine = cos_tab[pl.ds(t, 1), there]
                sine = sin_tab[pl.ds(t, 1), there]
                re = prods[pl.ds(t * slots, slots), at]
                im = prods[pl.ds(t * slots, slots), pl.ds(lanes + j * 128, 128)]
                term_real = re * cosine - im * sine
                term_imag = im * cosine + re * sine
                out_real = term_real if t == 0 else out_real + term_real
                out_imag = term_imag if t == 0 else out_imag + term_imag
            for w in range(RING):
                sends[c, w, 2 * g, :, at] = out_real[w * 16:(w + 1) * 16].astype(BF16)
                sends[c, w, 2 * g + 1, :, at] = out_imag[w * 16:(w + 1) * 16].astype(BF16)

    def sum_half(c, h):
        first = c * GROUPS + 2 * h
        multiply(prods_b, first + 1)
        rotate(prods_a, c, 2 * h)
        multiply(prods_a, jnp.minimum(first + 2, CHUNKS * GROUPS - 1))
        rotate(prods_b, c, 2 * h + 1)

    def reduce0(c, h):
        odd, v, u = axes(c)
        part_of = pl.ds(h * half, half)
        for by in (2, 1, 3):
            w = step(v, by)
            send(
                sends.at[c, w, part_of], near_in.at[c, by - 1, part_of], rs_send.at[c], near_sem.at[c],
                device(odd, w, u, my_z),
            )

    def reduce1(c):
        odd, v, u = axes(c)
        wait(near_in.at[c], near_sem.at[c])
        total = sends[c, v].astype(F32)
        for k in range(RING - 1):
            total += near_in[c, k].astype(F32)
        apart = jnp.dot(
            perm_t[...], total.astype(BF16).reshape(128, lanes), preferred_element_type=F32
        ).astype(BF16)
        send2[c] = apart.reshape(8, 16, lanes)
        home = u * 2 + my_z

        def share(i, carry):
            q = (home + i) % 8
            send(send2.at[c, q], recv2.at[c, home], share_send.at[c], rs_recv.at[c], device(odd, v, q // 2, q % 2))
            return carry

        lax.fori_loop(1, 8, share, 0)
        recv2[c, home] = send2[c, home]

    def sum_step(i, carry):
        c, h = i // 2, i % 2
        sum_half(c, h)
        reduce0(c, h)

        @pl.when((h == 1) & (c >= 1))
        def _():
            reduce1(c - 1)

        return carry

    multiply(prods_a, 0)
    lax.fori_loop(0, 2 * CHUNKS, sum_step, 0)
    for c in range(CHUNKS - 1):
        wait(sends.at[c, pl.ds(0, RING - 1)], rs_send.at[c])
    reduce1(CHUNKS - 1)

    wait(sends.at[CHUNKS - 1, pl.ds(0, RING - 1)], rs_send.at[CHUNKS - 1])
    for c in range(CHUNKS):
        wait(send2.at[c, pl.ds(0, 7)], share_send.at[c])
        wait(recv2.at[c, pl.ds(0, 7)], rs_recv.at[c])


def last_kernel(recv2, loglik_in, out_ref, loglik_ref):
    lanes = recv2.shape[3]
    freqs = CHUNKS * GROUPS * lanes
    loglik_ref[...] = loglik_in[...]
    for c in range(CHUNKS):
        for j in range(lanes // 128):
            total = recv2[c, 0, :, pl.ds(j * 128, 128)].astype(F32)
            for q in range(1, 8):
                total += recv2[c, q, :, pl.ds(j * 128, 128)].astype(F32)
            for s in range(2):
                for r in range(2):
                    for g in range(GROUPS):
                        row = s * 8 + g * 2 + r
                        at = r * freqs + c * GROUPS * lanes + g * lanes + j * 128
                        out_ref[s, :, pl.ds(at, 128)] = total[row:row + 1, :]


def per_device(n_dom, n_ori, particles, refs, inv_sigma2, offsets, owner_map, center):
    pcount, feat = particles.shape
    freqs = feat // 2
    shifts = offsets.shape[0]
    slots = 2 * n_dom
    lanes = freqs // (CHUNKS * GROUPS)
    vmem = pl.BlockSpec(memory_space=pltpu.VMEM)
    far = pl.BlockSpec(memory_space=pltpu.HBM)
    dma = pltpu.SemaphoreType.DMA
    grant = 56 * 1024 * 1024
    partial, loglik = pl.pallas_call(
        functools.partial(em_kernel, n_dom, n_ori, shifts),
        out_shape=(
            jax.ShapeDtypeStruct((CHUNKS, 8, 16, lanes), BF16),
            jax.ShapeDtypeStruct((1, pcount), F32),
        ),
        in_specs=[far] * 6,
        out_specs=(vmem, vmem),
        scratch_shapes=[
            pltpu.VMEM((pcount, feat), BF16),
            pltpu.VMEM((lanes // 128, 16 * CHUNKS, 128), F32),
            pltpu.VMEM((2, PAIRS, 16, lanes), BF16),
            pltpu.VMEM((2, 8, PAIRS, 16, lanes), BF16),
            pltpu.VMEM((CHUNKS, RING, 8, 16, lanes), BF16),
            pltpu.VMEM((128, 128), BF16),
            pltpu.VMEM((128, 128), BF16),
            pltpu.VMEM((shifts, freqs), F32),
            pltpu.VMEM((shifts, freqs), F32),
            pltpu.VMEM((shifts * slots, 4 * lanes), BF16),
            pltpu.VMEM((shifts * slots, 4 * lanes), BF16),
            pltpu.VMEM((2, shifts * slots, pcount), F32),
            pltpu.VMEM((shifts * slots, 2 * lanes), F32),
            pltpu.VMEM((shifts * slots, 2 * lanes), F32),
            pltpu.VMEM((2, slots, 128), F32),
            pltpu.VMEM((2, feat), BF16),
            pltpu.SMEM((2, shifts), jnp.int32),
            pltpu.VMEM((1, freqs), F32),
            pltpu.VMEM((1, slots), jnp.int32),
            pltpu.VMEM((1, pcount), jnp.int32),
            pltpu.VMEM((2, pcount), F32),
            pltpu.VMEM((n_ori, 2, pcount), F32),
            pltpu.VMEM((2, shifts * slots, pcount), BF16),
            pltpu.VMEM((CHUNKS, RING, 8, 16, lanes), BF16),
            pltpu.VMEM((CHUNKS, RING - 1, 8, 16, lanes), BF16),
            pltpu.VMEM((CHUNKS, 8, 16, lanes), BF16),
            dma((CHUNKS,)),
            dma((5,)),
            dma((2, 2)),
            dma((2, 2)),
            dma((CHUNKS,)),
            dma((CHUNKS, 2)),
            dma,
            dma,
            dma((CHUNKS,)),
            dma((CHUNKS,)),
            dma((CHUNKS,)),
            dma((CHUNKS,)),
        ],
        compiler_params=pltpu.CompilerParams(collective_id=0, has_side_effects=True, vmem_limit_bytes=grant),
        cost_estimate=pl.CostEstimate(
            flops=4 * shifts * slots * pcount * feat, bytes_accessed=2 * pcount * feat, transcendentals=0
        ),
    )(
        refs.reshape(2, feat), particles, inv_sigma2.reshape(1, freqs), offsets.T, owner_map.reshape(1, slots),
        center.reshape(1, pcount),
    )
    sums, loglik = pl.pallas_call(
        last_kernel,
        out_shape=(jax.ShapeDtypeStruct((2, 1, feat), F32), jax.ShapeDtypeStruct((1, pcount), F32)),
        in_specs=[vmem, vmem],
        out_specs=(vmem, vmem),
        compiler_params=pltpu.CompilerParams(vmem_limit_bytes=grant),
    )(partial, loglik)
    return sums, loglik.reshape(pcount)


def solution(mesh):
    return jax.shard_map(
        functools.partial(per_device, mesh.shape["dom"], mesh.shape["orient"]),
        mesh=mesh,
        in_specs=(P("dom", None), P("dom", "orient", None), P(), P(), P(), P("dom")),
        out_specs=(P("dom", "orient", None), P("dom")),
        check_vma=False,
    )
```
